128 devices in a mesh: px: 8 (over z, core), py: 16 (over y, x).
Axes of the slice: x: 4, y: 4, z: 4, core: 2. Of those that a mesh axis runs over, the one named last changes fastest.
Arguments:
- background_field: float32 [64, 512, 1024], P('px', 'py'), may hold values from -6 to 6
- perturbation: float32 [64, 512, 1024], P('px', 'py'), may hold values from -6 to 6
- permittivity: float32 [64, 512, 1024], P('px', 'py'), may hold values from 0.5 to 2
- probe_nodes: int32 [4, 131072], P(None, ('px', 'py')), may hold values from 0 to 262143
- probe_weights: float32 [4, 131072], P(None, ('px', 'py')), may hold values from 0.1 to 1
- probe_owner: int32 [131072, 1], P(('px', 'py')), may hold values from 0 to 127; in each aligned block of 1024 rows (0 to 1023, 1024 to 2047, ...) at most 16 rows name the same one
- probe_sensor: int32 [131072], P(('px', 'py')), may hold values from 0 to 7
- sensor_weight: float32 [1024], P(('px', 'py')), may hold values from 0.2 to 5
Outputs:
- hess_vec: float32 [64, 512, 1024], P('px', 'py')
The draws below stay inside these ranges and needn't reach their ends.
Inputs may be any that keep to these rules, and one draw needn't show every extreme that they name: `probe_nodes`: each probe's nodes lie in the block of the device that holds the probe. `probe_owner`: of the probes of one device at most 16 name the same owner, and in every draw some owner is named by exactly 16 of them.
All inputs are finite; a program needn't handle non-finite values.
Results may differ from the reference program's by a relative error of at most 0.00025.
Values sent between devices are 32-bit elements; how exact they have to be, the bound alone decides.
No kernel may reach another device: no remote copies, remote signals or barrier semaphores. Data moves between devices by JAX's collectives and lax.ppermute only.
A program may use at most 64 MiB of HBM per device.

```python
import math
import jax
import jax.numpy as jnp
import numpy as np
from jax import lax

CX = 8
CY = 32
CZ = 1024
PROBE_DEV = 1024
SENS_DEV = 8
SWEEPS = 4
CAP = 16
NX = 64
NY = 512
NZ = 1024
PROBES = 131072
SENSORS = 1024
N_PX = 8
N_PY = 16


def with_ends(values, rng, low, largest):
    longest = values.shape.index(max(values.shape))
    spots = []
    for shift in (0, 1):
        where = [jax.random.randint(jax.random.fold_in(rng, axis), (), 0, length) for axis, length in enumerate(values.shape)]
        where[longest] = (where[longest] + shift) % values.shape[longest]
        spots.append(tuple(where))
    return values.at[spots[0]].set(low).at[spots[1]].set(largest)


def block_levels(key, dims, split, low, top_value):
    level = 1.0
    for dim, shards_of in split:
        steps = jax.random.uniform(jax.random.fold_in(jax.random.fold_in(key, 6), dim), (shards_of,), jnp.float32, low / len(split), top_value / len(split))
        level = level * jnp.repeat(jnp.exp(steps), dims[dim] // shards_of).reshape((-1,) + (1,) * (len(dims) - 1 - dim))
    return level


def assign_block(rng, own, number, rows, count, top, reach, lean):
    sequence = jax.random.permutation(rng, count)
    packed, ordinary = load_shares(count, rows * top, reach, lean, True), load_shares(count, rows * top, reach, lean, False)
    places = jnp.arange(count)

    def named(lengths, turn):
        used = int((lengths > 0).sum())
        fixed = max(1, used // 4)
        shifted = fixed + (places - fixed + turn * (used - fixed)) % max(1, count - fixed)
        return jnp.zeros((count,), jnp.int32).at[sequence[jnp.where(places < fixed, places, shifted)]].set(jnp.asarray(lengths, jnp.int32))

    lengths = jnp.where(number % 4 == 0, named(packed, number // 4), named(ordinary, number - number // 4 - 1))
    mixed = jax.random.permutation(jax.random.fold_in(own, 3), count)
    source_of, taker = mixed[0:count // 2 * 2:2], mixed[1:count // 2 * 2:2]
    slack = jnp.minimum(lengths[source_of] - 1, reach - lengths[taker]) // 2
    slack = jnp.where((source_of == sequence[0]) | (taker == sequence[0]) | (lengths[taker] == 0), 0, jnp.maximum(slack, 0))
    shifted = jax.random.randint(jax.random.fold_in(own, 4), (count // 2,), 0, 1 << 20) % (slack + 1)
    lengths = lengths.at[source_of].add(-shifted).at[taker].add(shifted)
    items = jnp.searchsorted(jnp.cumsum(lengths), jnp.arange(rows * top), side="right").astype(jnp.int32)
    grid = items.reshape(top, rows).T
    grid = grid[jax.random.permutation(jax.random.fold_in(own, 1), rows)]
    turn = jax.random.randint(jax.random.fold_in(own, 2), (rows, 1), 0, top)
    return jnp.take_along_axis(grid, (jnp.arange(top)[None, :] + turn) % top, axis=1)


def load_shares(amount, total, most, skew, full):
    weights = [(1 << 20) // math.isqrt(rank ** skew) + 1 for rank in range(1, amount + 1)]
    largest = most if full else min(most, max(-(-total // amount), total * weights[0] // sum(weights)))
    least = 1 if total - largest >= amount - 1 else 0
    given, surplus = [largest] + [least] * (amount - 1), total - largest - least * (amount - 1)
    while surplus > 0:
        free = [i for i in range(1, amount) if given[i] < largest] or [i for i in range(1, amount) if given[i] < most]
        pool, remaining = sum([weights[i] for i in free]), surplus
        for i in free:
            extra = min(most - given[i], max(1, remaining * weights[i] // pool), surplus)
            given[i] = given[i] + extra
            surplus = surplus - extra
    return np.array(given)


def gaussian(stream_key, shape, width, bound, shards=(), kind=jnp.bfloat16):
    entries = jax.random.normal(stream_key, shape, jnp.float32) * width
    if len(shards) > 0:
        entries = block_levels(stream_key, shape, shards, -0.22, 0.18) * entries
    return jnp.clip(entries, min=-bound, max=bound).astype(kind)


def setup_inputs(seed: int = 0) -> dict:
    streams_of = jax.random.split(jax.random.key(seed), 9)
    background_field = gaussian(streams_of[0], (NX, NY, NZ), 1.0, 6.0, ((0, 8), (1, 16)), jnp.float32)
    perturbation = gaussian(streams_of[1], (NX, NY, NZ), 1.0, 6.0, ((0, 8), (1, 16)), jnp.float32)
    permittivity = jnp.clip(jnp.exp(math.log(2.0) - 1.3862944 * jax.random.uniform(streams_of[2], (NX, NY, NZ), jnp.float32) ** block_levels(streams_of[2], (NX, NY, NZ), ((0, 8), (1, 16)), -0.2, 0.2)), 0.5, 2.0)
    probe_nodes = with_ends(jax.random.randint(streams_of[3], (4, PROBES), 0, CX * CY * CZ), jax.random.fold_in(streams_of[3], 1), 0, (CX * CY * CZ) - 1).astype(jnp.int32)
    probe_weights = jnp.clip(0.1 + 0.9 * jax.random.uniform(streams_of[4], (4, PROBES), jnp.float32) ** block_levels(streams_of[4], (4, PROBES), ((1, 128),), -0.2, 0.2), 0.1, 1.0)
    probe_owner_keys = jax.random.split(jax.random.fold_in(streams_of[5], 1), PROBES // PROBE_DEV)
    probe_owner_turns = jax.random.permutation(jax.random.fold_in(streams_of[5], 3), PROBES // PROBE_DEV)
    probe_owner = jax.vmap(lambda own, number: assign_block(jax.random.fold_in(streams_of[5], 2), own, number, PROBE_DEV, N_PX * N_PY, 1, CAP, 2))(probe_owner_keys, probe_owner_turns).reshape((PROBES, 1))
    probe_sensor = with_ends(jax.random.randint(streams_of[6], (PROBES,), 0, SENS_DEV), jax.random.fold_in(streams_of[6], 1), 0, SENS_DEV - 1).astype(jnp.int32)
    sensor_weight = jnp.clip(jnp.exp(math.log(5.0) - 3.218876 * jax.random.uniform(streams_of[7], (SENSORS,), jnp.float32) ** block_levels(streams_of[7], (SENSORS,), ((0, 128),), -0.2, 0.2)), 0.2, 5.0)
    return dict(background_field=background_field, perturbation=perturbation, permittivity=permittivity, probe_nodes=probe_nodes, probe_weights=probe_weights, probe_owner=probe_owner, probe_sensor=probe_sensor, sensor_weight=sensor_weight)


mass_term = 1.0
bound_low = 1.0
bound_high = 25.0


def widen(array, direction, before, after):
    widths = [(0, 0), (0, 0), (0, 0)]
    widths[direction] = (before, after)
    return jnp.pad(array, widths)


def stiffness(field, permit, mass_value):
    result = mass_value * field
    for direction in range(3):
        extent = field.shape[direction]
        upper_cells = lax.slice_in_dim(field, 1, extent, axis=direction)
        lower_cells = lax.slice_in_dim(field, 0, extent - 1, axis=direction)
        face_coef = 0.5 * (lax.slice_in_dim(permit, 1, extent, axis=direction) + lax.slice_in_dim(permit, 0, extent - 1, axis=direction))
        face_flux = face_coef * (upper_cells - lower_cells)
        result = result - widen(face_flux, direction, 0, 1) + widen(face_flux, direction, 1, 0)
    return result


def chebyshev(source, permit):
    centre = 0.5 * (bound_high + bound_low)
    half_width = 0.5 * (bound_high - bound_low)
    spread = centre / half_width
    iterate = jnp.zeros_like(source)
    remain = source
    search = source / centre
    ratio_now = 1.0 / spread
    for sweep in range(SWEEPS):
        iterate = iterate + search
        if sweep < SWEEPS - 1:
            remain = remain - stiffness(search, permit, mass_term)
            ratio_next = 1.0 / (2.0 * spread - ratio_now)
            search = (ratio_next * ratio_now) * search + (2.0 * ratio_next / half_width) * remain
            ratio_now = ratio_next
    return iterate


def sensitivity(background, adjoint):
    total = jnp.zeros_like(background)
    for direction in range(3):
        extent = background.shape[direction]
        back_step = lax.slice_in_dim(background, 1, extent, axis=direction) - lax.slice_in_dim(background, 0, extent - 1, axis=direction)
        adj_step = lax.slice_in_dim(adjoint, 1, extent, axis=direction) - lax.slice_in_dim(adjoint, 0, extent - 1, axis=direction)
        product = back_step * adj_step
        total = total + widen(product, direction, 0, 1) + widen(product, direction, 1, 0)
    return -0.5 * total


def reference(background_field, perturbation, permittivity, probe_nodes, probe_weights, probe_owner, probe_sensor, sensor_weight):
    tangent = chebyshev(-stiffness(background_field, perturbation, 0.0), permittivity)
    total_x, total_y, total_z = tangent.shape
    probe_ids = jnp.arange(probe_sensor.shape[0], dtype=jnp.int32)
    device = probe_ids // PROBE_DEV
    block_x = device // N_PY
    block_y = device % N_PY
    local_x = probe_nodes // (CY * CZ)
    local_y = (probe_nodes // CZ) % CY
    local_z = probe_nodes % CZ
    global_x = block_x[None, :] * CX + local_x
    global_y = block_y[None, :] * CY + local_y
    global_nodes = ((global_x * total_y + global_y) * total_z + local_z).astype(jnp.int32)
    flat = tangent.reshape(-1)
    values = jnp.sum(probe_weights * flat[global_nodes], axis=0)
    keys = (probe_owner[:, 0] * SENS_DEV + probe_sensor).astype(jnp.int32)
    readings = jax.ops.segment_sum(values, keys, num_segments=N_PX * N_PY * SENS_DEV)
    weighted = readings * sensor_weight
    returned = weighted[keys]
    source = jnp.zeros(flat.shape, jnp.float32).at[global_nodes.reshape(-1)].add((probe_weights * returned[None, :]).reshape(-1))
    adjoint = chebyshev(source.reshape(tangent.shape), permittivity)
    return sensitivity(background_field, adjoint)
```

```python
import jax
import jax.numpy as jnp
import numpy as np
from jax import lax
from jax.experimental import pallas as pl
from jax.experimental.pallas import tpu as pltpu
from jax.sharding import PartitionSpec as P

SWEEPS = 4
MASS = 1.0
LOW = 1.0
HIGH = 25.0
CENTRE = 0.5 * (HIGH + LOW)
HALF = 0.5 * (HIGH - LOW)

CX, CY, CZ = 8, 32, 1024
D = 4
EX, EY = CX + 2 * D, CY + 2 * D
ROWS = CX * CY * 8
HALO_X = D * CY * 8
HALO_Y = CX * D * 8
DC = 3
HALO_C = DC * D * 8
META = 128
F32 = jnp.float32
BF16 = jnp.bfloat16


def horner_terms():
    spread = CENTRE / HALF
    size = SWEEPS
    iterate = np.zeros(size)
    remain = np.eye(size)[0]
    search = remain / CENTRE
    ratio = 1.0 / spread
    for sweep in range(SWEEPS):
        iterate = iterate + search
        if sweep < SWEEPS - 1:
            shifted = np.concatenate([[0.0], search[:-1]])
            remain = remain - (CENTRE * search + HALF * shifted)
            following = 1.0 / (2.0 * spread - ratio)
            search = following * ratio * search + 2.0 * following / HALF * remain
            ratio = following
    return [float(v) for v in iterate]


A0, A1, A2, A3 = horner_terms()


def lane_of(n):
    return lax.broadcasted_iota(jnp.int32, (n, 8, 128), 2)


def z_up(f):
    r = pltpu.roll(f, 127, 2)
    return jnp.where(lane_of(f.shape[0]) == 127, pltpu.roll(r, 7, 1), r)


def z_down(f):
    r = pltpu.roll(f, 1, 2)
    return jnp.where(lane_of(f.shape[0]) == 0, pltpu.roll(r, 1, 1), r)


def z_face(q):
    n = q.shape[0]
    sub = lax.broadcasted_iota(jnp.int32, (n, 8, 128), 1)
    last = (sub == 7) & (lane_of(n) == 127)
    return jnp.where(last, 0.0, q + z_up(q))


def fluxes(src, q, cz, x, y, n):
    fe, qe = src[x, pl.ds(y - 1, n + 2)], q[x, pl.ds(y - 1, n + 2)]
    f, qc = fe[1:-1], qe[1:-1]
    fy = (fe[1:] - fe[:-1]) * (qe[1:] + qe[:-1])
    acc = fy[1:] - fy[:-1]
    acc += (src[x + 1, pl.ds(y, n)] - f) * (q[x + 1, pl.ds(y, n)] + qc)
    acc += (src[x - 1, pl.ds(y, n)] - f) * (q[x - 1, pl.ds(y, n)] + qc)
    fz = (z_up(f) - f) * (z_face(qc) if cz is None else cz[x, pl.ds(y, n)])
    return f, acc + (fz - z_down(fz))


def cover(low, high, n):
    starts = list(range(low, high - n + 1, n))
    if starts[-1] + n < high:
        starts.append(high - n)
    return starts


def sweep(margin, n, step):
    def plane(x, carry):
        for y in cover(margin, EY - margin, n):
            step(x, y, n)
        return carry

    lax.fori_loop(margin, EX - margin, plane, 0)


def own_rows(ref, out, scale):
    def plane(x, carry):
        for yt in range(CY // 8):
            for ys in range(8):
                v = ref[pl.ds((x * (CY // 8) + yt) * 64 + ys, 8, stride=8), :]
                out[x + D, D + yt * 8 + ys] = v * scale if scale != 1.0 else v
        return carry

    lax.fori_loop(0, CX, plane, 0)


def extend(field, own, px_low, px_high, py_low, py_high, c_low, c_high, out, scale):
    own_rows(own, out, scale)
    for ref, at in ((px_low, 0), (px_high, D + CX)):

        def plane(x, carry, ref=ref, at=at):
            for yt in range(CY // 8):
                for ys in range(8):
                    v = ref[
                        pl.ds(field * HALO_X + (x * (CY // 8) + yt) * 64 + ys, 8, stride=8), :
                    ]
                    out[x + at, D + yt * 8 + ys] = v * scale
            return carry

        lax.fori_loop(0, D, plane, 0)
    for ref, at in ((py_low, 0), (py_high, D + CY)):
        for x in range(CX):
            v = ref[pl.ds(field * HALO_Y + x * D * 8, D * 8), :]
            out[x + D, pl.ds(at, D)] = v.reshape(D, 8, 128) * scale
    part = 3 * HALO_C + META
    for ref, at, gap in ((c_low, 1, 0), (c_high, D + CX, D + CX + DC)):
        for side, to in ((0, 0), (1, D + CY)):
            out[gap, pl.ds(to, D)] = jnp.zeros((D, 8, 128), F32)
            for x in range(DC):
                v = ref[pl.ds(side * part + field * HALO_C + x * D * 8, D * 8), :]
                out[at + x, pl.ds(to, D)] = v.reshape(D, 8, 128) * scale


def close_edges(pos, out, sign):
    @pl.when(pos[0] == 0)
    def _():
        out[D - 1] = out[D] * sign

    @pl.when(pos[0] == pos[2])
    def _():
        out[D + CX] = out[D + CX - 1] * sign

    @pl.when(pos[1] == 0)
    def _():
        out[:, D - 1] = out[:, D] * sign

    @pl.when(pos[1] == pos[3])
    def _():
        out[:, D + CY] = out[:, D + CY - 1] * sign


def take_meta(ref, base, out):
    for half in range(2):
        for c in range(8):
            out[half * 8 : half * 8 + 8, c * 128 : (c + 1) * 128] = ref[
                pl.ds(base + half * 64 + c * 8, 8), :
            ]


def two_parts(v):
    high = v.astype(BF16)
    return high, (v - high.astype(F32)).astype(BF16)


def three_parts(v):
    high = v.astype(BF16)
    rest = v - high.astype(F32)
    mid = rest.astype(BF16)
    return high, mid, (rest - mid.astype(F32)).astype(BF16)


def one_hot(index, count):
    at = lax.broadcasted_iota(jnp.int32, (count, index.shape[1]), 0)
    return jnp.where(at == index, 1.0, 0.0).astype(BF16)


def dot(a, b, over):
    return lax.dot_general(a, b, (over, ((), ())), preferred_element_type=F32)


def tangent_kernel(
    pos,
    permit,
    back,
    perturb,
    px_low,
    px_high,
    py_low,
    py_high,
    c_low,
    c_high,
    meta,
    weights,
    out,
    q,
    qp,
    bg,
    cz,
    b,
    y1,
    y2,
    table,
    vals,
):
    sides = (px_low, px_high, py_low, py_high, c_low, c_high)
    extend(0, permit, *sides, q, 0.5 / HALF)
    extend(1, back, *sides, bg, 1.0)
    extend(2, perturb, *sides, qp, 0.5)
    close_edges(pos, q, -1.0)
    close_edges(pos, qp, -1.0)

    def first(x, y, n):
        _, acc = fluxes(bg, qp, None, x, y, n)
        b[x, pl.ds(y, n)] = acc
        cz[x, pl.ds(y, n)] = z_face(q[x, pl.ds(y, n)])

    def second(x, y, n):
        f, acc = fluxes(b, q, cz, x, y, n)
        y1[x, pl.ds(y, n)] = (A2 - A3) * f - A3 * acc

    def third(x, y, n):
        f, acc = fluxes(y1, q, cz, x, y, n)
        y2[x, pl.ds(y, n)] = A1 * b[x, pl.ds(y, n)] - f - acc

    def fourth(x, y, n):
        f, acc = fluxes(y2, q, cz, x, y, n)
        y1[x, pl.ds(y, n)] = A0 * b[x, pl.ds(y, n)] - f - acc

    sweep(1, 4, first)
    sweep(2, 4, second)
    sweep(3, 4, third)
    sweep(4, 4, fourth)

    flat = y1.reshape(EX * EY * 8, 128)
    for x in range(CX):
        for c in range(8):
            v = flat[pl.ds(((x + D) * EY + D) * 8 + c, CY, stride=8), :]
            high, low = two_parts(v)
            table[x * CY : (x + 1) * CY, c * 128 : (c + 1) * 128] = high
            table[CX * CY + x * CY : CX * CY + (x + 1) * CY, c * 128 : (c + 1) * 128] = low

    vals[...] = jnp.zeros_like(vals)
    wide = 512

    def gather(i, carry):
        k, lanes = i // 2, pl.ds(pl.multiple_of((i % 2) * wide, wide), wide)
        node = meta[pl.ds(k, 1), lanes].astype(jnp.int32)
        found = dot(table[...], one_hot(node & (CZ - 1), CZ), ((1,), (0,)))
        found = found[: CX * CY] + found[CX * CY :]
        at = lax.broadcasted_iota(jnp.int32, found.shape, 0)
        found = jnp.sum(jnp.where(at == node >> 10, found, 0.0), axis=0, keepdims=True)
        vals[0:1, lanes] += meta[pl.ds(k + 4, 1), lanes] * found
        return carry

    lax.fori_loop(0, 8, gather, 0)

    key = meta[8:9, :].astype(jnp.int32)
    at = lax.broadcasted_iota(jnp.int32, (8, 1024), 0)
    owned = jnp.where(at == key >> 7, vals[0:1, :], 0.0)
    parts = jnp.concatenate(three_parts(owned), axis=0)
    sums = dot(parts, one_hot(key & 127, 128), ((1,), (1,)))
    readings = sums[0:8] + sums[8:16] + sums[16:24]
    both = jnp.concatenate([readings, weights[...]], axis=0)
    out[...] = jnp.broadcast_to(both[None], out.shape)


def scatter(meta, values, rows, cols, per, tiles, lhs, keep):
    for k in range(4):
        node = meta[k : k + 1, :].astype(jnp.int32)
        high, low = two_parts(values[k : k + 1, :])
        hit = lax.broadcasted_iota(jnp.int32, (per, 1024), 0) == rows(node)
        lanes = slice(k * 1024, (k + 1) * 1024)
        lhs[0:per, lanes] = jnp.where(hit, high.astype(F32), 0.0).astype(BF16)
        lhs[per : 2 * per, lanes] = jnp.where(hit, low.astype(F32), 0.0).astype(BF16)

    def tile(t, carry):
        total = None
        for k in range(4):
            node = meta[k : k + 1, :].astype(jnp.int32)
            lanes = slice(k * 1024, (k + 1) * 1024)
            part = dot(lhs[0 : 2 * per, lanes], one_hot(cols(node) - t * 256, 256), ((1,), (1,)))
            total = part if total is None else total + part
        keep(t, total[0:per] + total[per : 2 * per])
        return carry

    if tiles == 1:
        tile(0, 0)
    else:
        lax.fori_loop(0, tiles, tile, 0)


def adjoint_kernel(
    pos,
    got,
    permit,
    back,
    px_low,
    px_high,
    py_low,
    py_high,
    c_low,
    c_high,
    meta,
    out,
    q,
    bg,
    cz,
    src,
    y1,
    y2,
    lhs,
    near,
    values,
):
    sides = (px_low, px_high, py_low, py_high, c_low, c_high)
    extend(0, permit, *sides, q, 0.5 / HALF)
    extend(1, back, *sides, bg, 1.0)
    close_edges(pos, q, -1.0)
    close_edges(pos, bg, 1.0)

    both = jnp.sum(got[...], axis=0)
    weighted = jnp.concatenate(three_parts(both[0:8] * both[8:16]), axis=0)

    def returned(table):
        key = table[8:9, :].astype(jnp.int32)
        found = dot(weighted, one_hot(key & 127, 128), ((1,), (0,)))
        found = found[0:8] + found[8:16] + found[16:24]
        at = lax.broadcasted_iota(jnp.int32, found.shape, 0)
        found = jnp.sum(jnp.where(at == key >> 7, found, 0.0), axis=0, keepdims=True)
        values[0:4, :] = table[4:8, :] * found

    flat = src.reshape(EX * EY * 8, 128)

    def xy(node):
        return node >> 15, (node >> 10) & (CY - 1)

    def put_planes(x0, planes):
        def keep(t, sums):
            for x in range(planes):
                for half in range(2):
                    flat[pl.ds(((x + x0) * EY + D) * 8 + t * 2 + half, CY, stride=8), :] = sums[
                        x * CY : (x + 1) * CY, half * 128 : (half + 1) * 128
                    ]

        return keep

    def put_strip(x0, planes, y0):
        def keep(t, sums):
            for zq in range(4):
                for x in range(0, planes):
                    block = sums[zq * planes * D + x * D : zq * planes * D + (x + 1) * D]
                    for half in range(2):
                        flat[
                            pl.ds(((x + x0) * EY + y0) * 8 + zq * 2 + half, D, stride=8), :
                        ] = block[:, half * 128 : (half + 1) * 128]

        return keep

    def column(node):
        return node & (CZ - 1)

    def low_column(node):
        return node & 255

    returned(meta)
    scatter(meta, values, lambda n: n >> 10, column, CX * CY, 4, lhs, put_planes(D, CX))

    for ref, x0, first in ((px_low, 0, CX - D), (px_high, D + CX, 0)):
        take_meta(ref, 3 * HALO_X, near)
        returned(near)
        scatter(
            near,
            values,
            lambda n, first=first: (n >> 10) - first * CY,
            column,
            D * CY,
            4,
            lhs,
            put_planes(x0, D),
        )

    def strip(first_x, planes, first_y):
        def rows(node):
            x, y = xy(node)
            x, y = x - first_x, y - first_y
            good = (x >= 0) & (x < planes) & (y >= 0) & (y < D)
            return jnp.where(good, ((node >> 8) & 3) * (planes * D) + x * D + y, -1)

        return rows

    for ref, y0, first in ((py_low, 0, CY - D), (py_high, D + CY, 0)):
        take_meta(ref, 3 * HALO_Y, near)
        returned(near)
        scatter(
            near, values, strip(0, CX, first), low_column, 4 * CX * D, 1, lhs, put_strip(D, CX, y0)
        )

    part = 3 * HALO_C + META
    for ref, x0, first_x in ((c_low, 0, CX - D), (c_high, D + CX, 0)):
        for side, y0, first_y in ((0, 0, CY - D), (1, D + CY, 0)):
            take_meta(ref, side * part + 3 * HALO_C, near)
            returned(near)
            scatter(
                near,
                values,
                strip(first_x, D, first_y),
                low_column,
                4 * D * D,
                1,
                lhs,
                put_strip(x0, D, y0),
            )

    def first(x, y, n):
        cz[x, pl.ds(y, n)] = z_face(q[x, pl.ds(y, n)])
        f, acc = fluxes(src, q, cz, x, y, n)
        y1[x, pl.ds(y, n)] = (A2 - A3) * f - A3 * acc

    def second(x, y, n):
        f, acc = fluxes(y1, q, cz, x, y, n)
        y2[x, pl.ds(y, n)] = A1 * src[x, pl.ds(y, n)] - f - acc

    def third(x, y, n):
        f, acc = fluxes(y2, q, cz, x, y, n)
        y1[x, pl.ds(y, n)] = A0 * src[x, pl.ds(y, n)] - f - acc

    sweep(1, 4, first)
    sweep(2, 4, second)
    sweep(3, 4, third)

    def last(x, y, n):
        ae, be = y1[x, pl.ds(y - 1, n + 2)], bg[x, pl.ds(y - 1, n + 2)]
        a, k = ae[1:-1], be[1:-1]
        sy = (ae[1:] - ae[:-1]) * (be[1:] - be[:-1])
        total = sy[1:] + sy[:-1]
        total += (y1[x + 1, pl.ds(y, n)] - a) * (bg[x + 1, pl.ds(y, n)] - k)
        total += (y1[x - 1, pl.ds(y, n)] - a) * (bg[x - 1, pl.ds(y, n)] - k)
        sub = lax.broadcasted_iota(jnp.int32, (n, 8, 128), 1)
        end = (sub == 7) & (lane_of(n) == 127)
        sz = jnp.where(end, 0.0, (z_up(a) - a) * (z_up(k) - k))
        total = -0.5 * (total + (sz + z_down(sz)))
        yy = y - D
        for i in range(n):
            row = (x - D) * (CY // 8) + (yy + i) // 8
            out[pl.ds(row * 64 + (yy + i) % 8, 8, stride=8), :] = total[i]

    sweep(4, 4, last)


def by_tiles(block):
    lead = block.shape[:-2]
    rows, cols = block.shape[-2:]
    split = block.reshape(*lead, rows // 8, 8, cols // 128, 128)
    return jnp.swapaxes(split, -3, -2).reshape(-1, 128)


def from_tiles(rows):
    split = rows.reshape(CX, CY // 8, CZ // 128, 8, 128)
    return jnp.swapaxes(split, -3, -2).reshape(CX, CY, CZ)


def pack_kernel(permit, back, perturb, meta, low, high):
    for field, ref in enumerate((permit, back, perturb)):
        for x in range(CX):
            for y in range(D):
                at = pl.ds(field * HALO_Y + (x * D + y) * 8, 8)
                low[at, :] = ref[pl.ds(x * (CY // 8) * 64 + y, 8, stride=8), :]
                last = x * (CY // 8) + CY // 8 - 1
                high[at, :] = ref[pl.ds(last * 64 + 8 - D + y, 8, stride=8), :]
    low[3 * HALO_Y :, :] = meta[...]
    high[3 * HALO_Y :, :] = meta[...]


def vmem(count):
    return [pl.BlockSpec(memory_space=pltpu.VMEM)] * count


def shift(x, axis, by):
    count = lax.axis_size(axis)
    return lax.ppermute(x, axis, [(i, (i + by) % count) for i in range(count)])


def body(
    background_field,
    perturbation,
    permittivity,
    probe_nodes,
    probe_weights,
    probe_owner,
    probe_sensor,
    sensor_weight,
):
    count_x, count_y = lax.axis_size("px"), lax.axis_size("py")
    px, py = lax.axis_index("px"), lax.axis_index("py")
    owned = sensor_weight.shape[0]
    devices = count_x * count_y
    pos = jnp.stack([px, py, jnp.int32(count_x - 1), jnp.int32(count_y - 1)]).astype(jnp.int32)
    key = probe_owner.reshape(1, -1) * owned + probe_sensor[None, :]
    meta = jnp.concatenate(
        [
            probe_nodes.astype(F32),
            probe_weights,
            key.astype(F32),
            jnp.zeros((7, key.shape[1]), F32),
        ],
        axis=0,
    )
    weights = lax.dynamic_update_slice(
        jnp.zeros((8, 128), F32), sensor_weight[None, :], (px, py * owned)
    )
    fields = [by_tiles(f) for f in (permittivity, background_field, perturbation)]
    meta_rows = by_tiles(meta)

    low_x = jnp.concatenate([f[:HALO_X] for f in fields] + [meta_rows], axis=0)
    high_x = jnp.concatenate([f[ROWS - HALO_X :] for f in fields] + [meta_rows], axis=0)
    px_low, px_high = shift(high_x, "px", 1), shift(low_x, "px", -1)
    strip = jax.ShapeDtypeStruct((3 * HALO_Y + META, 128), F32)
    low_y, high_y = pl.pallas_call(
        pack_kernel,
        out_shape=(strip, strip),
        in_specs=vmem(4),
        out_specs=tuple(vmem(2)),
    )(*fields, meta_rows)
    py_low, py_high = shift(high_y, "py", 1), shift(low_y, "py", -1)
    low_c, high_c = [], []
    for arrived in (py_low, py_high):
        for field in range(3):
            strip = arrived[field * HALO_Y : (field + 1) * HALO_Y]
            low_c.append(strip[:HALO_C])
            high_c.append(strip[HALO_Y - HALO_C :])
        low_c.append(arrived[3 * HALO_Y :])
        high_c.append(arrived[3 * HALO_Y :])
    c_low = shift(jnp.concatenate(high_c, axis=0), "px", 1)
    c_high = shift(jnp.concatenate(low_c, axis=0), "px", -1)
    sides = (px_low, px_high, py_low, py_high, c_low, c_high)

    block = pltpu.VMEM((EX, EY, 8, 128), F32)
    smem = pl.BlockSpec(memory_space=pltpu.SMEM)
    readings = pl.pallas_call(
        tangent_kernel,
        out_shape=jax.ShapeDtypeStruct((devices, 16, 128), F32),
        in_specs=[smem] + vmem(11),
        out_specs=vmem(1)[0],
        scratch_shapes=[block] * 7
        + [pltpu.VMEM((2 * CX * CY, CZ), BF16), pltpu.VMEM((8, 1024), F32)],
        compiler_params=pltpu.CompilerParams(vmem_limit_bytes=56 * 2**20),
    )(pos, *fields, *sides, meta, weights)
    got = lax.all_to_all(readings, ("px", "py"), split_axis=0, concat_axis=0, tiled=True)
    result = pl.pallas_call(
        adjoint_kernel,
        out_shape=jax.ShapeDtypeStruct((ROWS, 128), F32),
        in_specs=[smem] + vmem(10),
        out_specs=vmem(1)[0],
        scratch_shapes=[block] * 6
        + [
            pltpu.VMEM((2 * CX * CY, 4096), BF16),
            pltpu.VMEM((16, 1024), F32),
            pltpu.VMEM((8, 1024), F32),
        ],
        compiler_params=pltpu.CompilerParams(vmem_limit_bytes=56 * 2**20),
    )(pos, got, *fields[:2], *sides, meta)
    return from_tiles(result)


def solution(mesh):
    placed = (
        P("px", "py", None),
        P("px", "py", None),
        P("px", "py", None),
        P(None, ("px", "py")),
        P(None, ("px", "py")),
        P(("px", "py"), None),
        P(("px", "py")),
        P(("px", "py")),
    )
    return jax.shard_map(
        body, mesh=mesh, in_specs=placed, out_specs=P("px", "py", None), check_vma=False
    )
```

```python
import jax
import jax.numpy as jnp
import numpy as np
from jax import lax
from jax.experimental import pallas as pl
from jax.experimental.pallas import tpu as pltpu
from jax.sharding import PartitionSpec as P

SWEEPS = 4
MASS = 1.0
LOW = 1.0
HIGH = 25.0
CENTRE = 0.5 * (HIGH + LOW)
HALF = 0.5 * (HIGH - LOW)

CX, CY, CZ = 8, 32, 1024
D = 4
EX, EY = CX + 2 * D, CY + 2 * D
ROWS = CX * CY * 8
HALO_X = D * CY * 8
HALO_Y = CX * D * 8
DC = 3
HALO_C = DC * D * 8
META = 128
F32 = jnp.float32
BF16 = jnp.bfloat16


def horner_terms():
    spread = CENTRE / HALF
    size = SWEEPS
    iterate = np.zeros(size)
    remain = np.eye(size)[0]
    search = remain / CENTRE
    ratio = 1.0 / spread
    for sweep in range(SWEEPS):
        iterate = iterate + search
        if sweep < SWEEPS - 1:
            shifted = np.concatenate([[0.0], search[:-1]])
            remain = remain - (CENTRE * search + HALF * shifted)
            following = 1.0 / (2.0 * spread - ratio)
            search = following * ratio * search + 2.0 * following / HALF * remain
            ratio = following
    return [float(v) for v in iterate]


A0, A1, A2, A3 = horner_terms()


def lane_of(n):
    return lax.broadcasted_iota(jnp.int32, (n, 8, 128), 2)


def z_up(f):
    r = pltpu.roll(f, 127, 2)
    return jnp.where(lane_of(f.shape[0]) == 127, pltpu.roll(r, 7, 1), r)


def z_down(f):
    r = pltpu.roll(f, 1, 2)
    return jnp.where(lane_of(f.shape[0]) == 0, pltpu.roll(r, 1, 1), r)


def z_face(q):
    n = q.shape[0]
    sub = lax.broadcasted_iota(jnp.int32, (n, 8, 128), 1)
    last = (sub == 7) & (lane_of(n) == 127)
    return jnp.where(last, 0.0, q + z_up(q))


def fluxes(src, q, cz, x, y, n):
    fe, qe = src[x, pl.ds(y - 1, n + 2)], q[x, pl.ds(y - 1, n + 2)]
    f, qc = fe[1:-1], qe[1:-1]
    fy = (fe[1:] - fe[:-1]) * (qe[1:] + qe[:-1])
    acc = fy[1:] - fy[:-1]
    acc += (src[x + 1, pl.ds(y, n)] - f) * (q[x + 1, pl.ds(y, n)] + qc)
    acc += (src[x - 1, pl.ds(y, n)] - f) * (q[x - 1, pl.ds(y, n)] + qc)
    fz = (z_up(f) - f) * (z_face(qc) if cz is None else cz[x, pl.ds(y, n)])
    return f, acc + (fz - z_down(fz))


def cover(low, high, n):
    starts = list(range(low, high - n + 1, n))
    if starts[-1] + n < high:
        starts.append(high - n)
    return starts


def sweep(margin, n, step):
    def plane(x, carry):
        for y in cover(margin, EY - margin, n):
            step(x, y, n)
        return carry

    lax.fori_loop(margin, EX - margin, plane, 0)


def extend(field, own, sides, out, scale):
    px_low, px_high, py_low, py_high, c_low, c_high = sides
    middle_x, middle_y = slice(D, D + CX), slice(D, D + CY)
    out[middle_x, middle_y] = own[...]
    for ref, at in ((px_low, 0), (px_high, D + CX)):
        v = ref[field * HALO_X : (field + 1) * HALO_X, :]
        out[at : at + D, middle_y] = v.reshape(D, CY, 8, 128) * scale
    for ref, at in ((py_low, 0), (py_high, D + CY)):
        v = ref[field * HALO_Y : (field + 1) * HALO_Y, :]
        out[middle_x, at : at + D] = v.reshape(CX, D, 8, 128) * scale
    part = 3 * HALO_C + META
    for ref, at, gap in ((c_low, 1, 0), (c_high, D + CX, D + CX + DC)):
        for side, to in ((0, 0), (1, D + CY)):
            out[gap, to : to + D] = jnp.zeros((D, 8, 128), F32)
            v = ref[side * part + field * HALO_C : side * part + (field + 1) * HALO_C, :]
            out[at : at + DC, to : to + D] = v.reshape(DC, D, 8, 128) * scale


def close_edges(out, sign):
    px, py = lax.axis_index("px"), lax.axis_index("py")
    last_x, last_y = lax.axis_size("px") - 1, lax.axis_size("py") - 1

    @pl.when(px == 0)
    def _():
        out[D - 1] = out[D] * sign

    @pl.when(px == last_x)
    def _():
        out[D + CX] = out[D + CX - 1] * sign

    @pl.when(py == 0)
    def _():
        out[:, D - 1] = out[:, D] * sign

    @pl.when(py == last_y)
    def _():
        out[:, D + CY] = out[:, D + CY - 1] * sign


def take_meta(ref, base, out):
    for half in range(2):
        for c in range(8):
            out[half * 8 : half * 8 + 8, c * 128 : (c + 1) * 128] = ref[
                pl.ds(base + half * 64 + c * 8, 8), :
            ]


def two_parts(v):
    high = v.astype(BF16)
    return high, (v - high.astype(F32)).astype(BF16)


def three_parts(v):
    high = v.astype(BF16)
    rest = v - high.astype(F32)
    mid = rest.astype(BF16)
    return high, mid, (rest - mid.astype(F32)).astype(BF16)


def one_hot(index, count):
    at = lax.broadcasted_iota(jnp.int32, (count, index.shape[1]), 0)
    return jnp.where(at == index, 1.0, 0.0).astype(BF16)


def dot(a, b, over):
    return lax.dot_general(a, b, (over, ((), ())), preferred_element_type=F32)


def tangent_kernel(
    permit,
    back,
    perturb,
    px_low,
    px_high,
    py_low,
    py_high,
    c_low,
    c_high,
    meta,
    hot,
    weights,
    out,
    q,
    bg,
    cz,
    qp,
    b,
    y1,
    y2,
    table,
    vals,
):
    sides = (px_low, px_high, py_low, py_high, c_low, c_high)
    extend(0, permit, sides, q, 0.5 / HALF)
    extend(1, back, sides, bg, 1.0)
    extend(2, perturb, sides, qp, 0.5)
    close_edges(q, -1.0)
    close_edges(qp, -1.0)
    close_edges(bg, 1.0)

    def first(x, y, n):
        _, acc = fluxes(bg, qp, None, x, y, n)
        b[x, pl.ds(y, n)] = acc
        cz[x, pl.ds(y, n)] = z_face(q[x, pl.ds(y, n)])

    def second(x, y, n):
        f, acc = fluxes(b, q, cz, x, y, n)
        y1[x, pl.ds(y, n)] = (A2 - A3) * f - A3 * acc

    def third(x, y, n):
        f, acc = fluxes(y1, q, cz, x, y, n)
        y2[x, pl.ds(y, n)] = A1 * b[x, pl.ds(y, n)] - f - acc

    def fourth(x, y, n):
        f, acc = fluxes(y2, q, cz, x, y, n)
        y1[x, pl.ds(y, n)] = A0 * b[x, pl.ds(y, n)] - f - acc

    sweep(1, 4, first)
    sweep(2, 4, second)
    sweep(3, 4, third)
    sweep(4, 4, fourth)

    flat = y1.reshape(EX * EY * 8, 128)
    for x in range(CX):
        for c in range(8):
            v = flat[pl.ds(((x + D) * EY + D) * 8 + c, CY, stride=8), :]
            high, low = two_parts(v)
            table[x * CY : (x + 1) * CY, c * 128 : (c + 1) * 128] = high
            table[CX * CY + x * CY : CX * CY + (x + 1) * CY, c * 128 : (c + 1) * 128] = low

    vals[...] = jnp.zeros_like(vals)
    wide = 512

    def gather(i, carry):
        k, lanes = i // 2, pl.ds(pl.multiple_of((i % 2) * wide, wide), wide)
        node = meta[pl.ds(k, 1), lanes].astype(jnp.int32)
        found = dot(table[...], hot[:, pl.ds(pl.multiple_of(i * wide, wide), wide)], ((1,), (0,)))
        found = found[: CX * CY] + found[CX * CY :]
        at = lax.broadcasted_iota(jnp.int32, found.shape, 0)
        found = jnp.sum(jnp.where(at == node >> 10, found, 0.0), axis=0, keepdims=True)
        vals[0:1, lanes] += meta[pl.ds(k + 4, 1), lanes] * found
        return carry

    lax.fori_loop(0, 8, gather, 0)

    owner, sensor = meta[8:9, :].astype(jnp.int32), meta[9:10, :].astype(jnp.int32)
    at = lax.broadcasted_iota(jnp.int32, (8, 1024), 0)
    owned = jnp.where(at == sensor, vals[0:1, :], 0.0)
    parts = jnp.concatenate(three_parts(owned), axis=0)
    sums = dot(parts, one_hot(owner, 128), ((1,), (1,)))
    readings = sums[0:8] + sums[8:16] + sums[16:24]
    block = jnp.concatenate([readings, weights[...]] * 8, axis=0)
    for i in range(out.shape[0] // 72):
        out[i * 72 : (i + 1) * 72, :] = block


def scatter(meta, values, rows, cols, per, tiles, lhs, keep, hot=None):
    for k in range(4):
        node = meta[k : k + 1, :].astype(jnp.int32)
        high, low = two_parts(values[k : k + 1, :])
        hit = lax.broadcasted_iota(jnp.int32, (per, 1024), 0) == rows(node)
        lanes = slice(k * 1024, (k + 1) * 1024)
        lhs[0:per, lanes] = jnp.where(hit, high.astype(F32), 0.0).astype(BF16)
        lhs[per : 2 * per, lanes] = jnp.where(hit, low.astype(F32), 0.0).astype(BF16)

    def tile(t, carry):
        total = None
        for k in range(4):
            lanes = slice(k * 1024, (k + 1) * 1024)
            if hot is None:
                node = meta[k : k + 1, :].astype(jnp.int32)
                hits = one_hot(cols(node) - t * 256, 256)
            else:
                hits = hot[pl.ds(pl.multiple_of(t * 256, 256), 256), lanes]
            part = dot(lhs[0 : 2 * per, lanes], hits, ((1,), (1,)))
            total = part if total is None else total + part
        keep(t, total[0:per] + total[per : 2 * per])
        return carry

    if tiles == 1:
        tile(0, 0)
    else:
        lax.fori_loop(0, tiles, tile, 0)


def adjoint_kernel(
    got,
    px_low,
    px_high,
    py_low,
    py_high,
    c_low,
    c_high,
    meta,
    hot,
    q,
    bg,
    cz,
    out,
    src,
    y1,
    y2,
    lhs,
    near,
    values,
):
    count = got.shape[0] // 9
    sums = [jnp.sum(got[pl.ds(i, count, stride=9), :], axis=0, keepdims=True) for i in range(8)]
    readings = jnp.concatenate(sums, axis=0)
    weights = jnp.transpose(got[pl.ds(8, count, stride=9), :])[0:8]
    weighted = jnp.concatenate(three_parts(readings * weights), axis=0)

    def returned(table):
        owner, sensor = table[8:9, :].astype(jnp.int32), table[9:10, :].astype(jnp.int32)
        found = dot(weighted, one_hot(owner, 128), ((1,), (0,)))
        found = found[0:8] + found[8:16] + found[16:24]
        at = lax.broadcasted_iota(jnp.int32, found.shape, 0)
        found = jnp.sum(jnp.where(at == sensor, found, 0.0), axis=0, keepdims=True)
        values[0:4, :] = table[4:8, :] * found

    flat = src.reshape(EX * EY * 8, 128)

    def xy(node):
        return node >> 15, (node >> 10) & (CY - 1)

    def put_planes(x0, planes):
        def keep(t, sums):
            for x in range(planes):
                for half in range(2):
                    flat[pl.ds(((x + x0) * EY + D) * 8 + t * 2 + half, CY, stride=8), :] = sums[
                        x * CY : (x + 1) * CY, half * 128 : (half + 1) * 128
                    ]

        return keep

    def put_strip(x0, planes, y0):
        def keep(t, sums):
            for zq in range(4):
                for x in range(0, planes):
                    block = sums[zq * planes * D + x * D : zq * planes * D + (x + 1) * D]
                    for half in range(2):
                        flat[
                            pl.ds(((x + x0) * EY + y0) * 8 + zq * 2 + half, D, stride=8), :
                        ] = block[:, half * 128 : (half + 1) * 128]

        return keep

    def column(node):
        return node & (CZ - 1)

    def low_column(node):
        return node & 255

    returned(meta)
    scatter(meta, values, lambda n: n >> 10, column, CX * CY, 4, lhs, put_planes(D, CX), hot)

    for ref, x0, first in ((px_low, 0, CX - D), (px_high, D + CX, 0)):
        take_meta(ref, 3 * HALO_X, near)
        returned(near)
        scatter(
            near,
            values,
            lambda n, first=first: (n >> 10) - first * CY,
            column,
            D * CY,
            4,
            lhs,
            put_planes(x0, D),
        )

    def strip(first_x, planes, first_y):
        def rows(node):
            x, y = xy(node)
            x, y = x - first_x, y - first_y
            good = (x >= 0) & (x < planes) & (y >= 0) & (y < D)
            return jnp.where(good, ((node >> 8) & 3) * (planes * D) + x * D + y, -1)

        return rows

    for ref, y0, first in ((py_low, 0, CY - D), (py_high, D + CY, 0)):
        take_meta(ref, 3 * HALO_Y, near)
        returned(near)
        scatter(
            near, values, strip(0, CX, first), low_column, 4 * CX * D, 1, lhs, put_strip(D, CX, y0)
        )

    part = 3 * HALO_C + META
    for ref, x0, first_x in ((c_low, 0, CX - D), (c_high, D + CX, 0)):
        for side, y0, first_y in ((0, 0, CY - D), (1, D + CY, 0)):
            take_meta(ref, side * part + 3 * HALO_C, near)
            returned(near)
            scatter(
                near,
                values,
                strip(first_x, D, first_y),
                low_column,
                4 * D * D,
                1,
                lhs,
                put_strip(x0, D, y0),
            )

    def first(x, y, n):
        f, acc = fluxes(src, q, cz, x, y, n)
        y1[x, pl.ds(y, n)] = (A2 - A3) * f - A3 * acc

    def second(x, y, n):
        f, acc = fluxes(y1, q, cz, x, y, n)
        y2[x, pl.ds(y, n)] = A1 * src[x, pl.ds(y, n)] - f - acc

    def third(x, y, n):
        f, acc = fluxes(y2, q, cz, x, y, n)
        y1[x, pl.ds(y, n)] = A0 * src[x, pl.ds(y, n)] - f - acc

    sweep(1, 4, first)
    sweep(2, 4, second)
    sweep(3, 4, third)

    def last(x, y, n):
        ae, be = y1[x, pl.ds(y - 1, n + 2)], bg[x, pl.ds(y - 1, n + 2)]
        a, k = ae[1:-1], be[1:-1]
        sy = (ae[1:] - ae[:-1]) * (be[1:] - be[:-1])
        total = sy[1:] + sy[:-1]
        total += (y1[x + 1, pl.ds(y, n)] - a) * (bg[x + 1, pl.ds(y, n)] - k)
        total += (y1[x - 1, pl.ds(y, n)] - a) * (bg[x - 1, pl.ds(y, n)] - k)
        sub = lax.broadcasted_iota(jnp.int32, (n, 8, 128), 1)
        end = (sub == 7) & (lane_of(n) == 127)
        sz = jnp.where(end, 0.0, (z_up(a) - a) * (z_up(k) - k))
        total = -0.5 * (total + (sz + z_down(sz)))
        yy = y - D
        for i in range(n):
            row = (x - D) * (CY // 8) + (yy + i) // 8
            out[pl.ds(row * 64 + (yy + i) % 8, 8, stride=8), :] = total[i]

    sweep(4, 4, last)


def by_tiles(block):
    lead = block.shape[:-2]
    rows, cols = block.shape[-2:]
    split = block.reshape(*lead, rows // 8, 8, cols // 128, 128)
    return jnp.swapaxes(split, -3, -2).reshape(-1, 128)


def from_tiles(rows):
    split = rows.reshape(CX, CY // 8, CZ // 128, 8, 128)
    return jnp.swapaxes(split, -3, -2).reshape(CX, CY, CZ)


def row_of(ref, x, y):
    return ref[pl.ds((x * (CY // 8) + y // 8) * 64 + y % 8, 8, stride=8), :]


def pack_kernel(
    permit,
    back,
    perturb,
    nodes,
    probe_weights,
    owner,
    sensor,
    low_x,
    high_x,
    low_y,
    high_y,
    meta,
):
    meta[0:4, :] = nodes[...].astype(F32)
    meta[4:8, :] = probe_weights[...]
    meta[8:9, :] = owner[...].astype(F32)
    meta[9:10, :] = sensor[...].astype(F32)
    meta[10:16, :] = jnp.zeros((6, 1024), F32)
    for field, ref in enumerate((permit, back, perturb)):

        def plane(x, carry, field=field, ref=ref):
            for y in range(CY):
                at = pl.ds(field * HALO_X + (x * CY + y) * 8, 8)
                low_x[at, :] = row_of(ref, x, y)
                high_x[at, :] = row_of(ref, x + CX - D, y)
            return carry

        lax.fori_loop(0, D, plane, 0)
        for x in range(CX):
            for y in range(D):
                at = pl.ds(field * HALO_Y + (x * D + y) * 8, 8)
                low_y[at, :] = row_of(ref, x, y)
                high_y[at, :] = row_of(ref, x, y + CY - D)
    for half in range(2):
        for c in range(8):
            v = meta[half * 8 : half * 8 + 8, c * 128 : (c + 1) * 128]
            at = half * 64 + c * 8
            low_x[3 * HALO_X + at : 3 * HALO_X + at + 8, :] = v
            high_x[3 * HALO_X + at : 3 * HALO_X + at + 8, :] = v
            low_y[3 * HALO_Y + at : 3 * HALO_Y + at + 8, :] = v
            high_y[3 * HALO_Y + at : 3 * HALO_Y + at + 8, :] = v


def own_kernel(permit, back, perturb, meta, q, bg, qp, hot):
    def plane(x, carry):
        for y in range(CY):
            q[x, y] = row_of(permit, x, y) * (0.5 / HALF)
            bg[x, y] = row_of(back, x, y)
            qp[x, y] = row_of(perturb, x, y) * 0.5
        return carry

    lax.fori_loop(0, CX, plane, 0)

    def entries(i, carry):
        k, lanes = i // 2, pl.ds(pl.multiple_of((i % 2) * 512, 512), 512)
        node = meta[pl.ds(k, 1), lanes].astype(jnp.int32)
        hot[:, pl.ds(pl.multiple_of(i * 512, 512), 512)] = one_hot(node & (CZ - 1), CZ)
        return carry

    lax.fori_loop(0, 8, entries, 0)


def corner_kernel(py_low, py_high, low, high):
    part = 3 * HALO_C + META
    for side, ref in enumerate((py_low, py_high)):
        for field in range(3):
            at, first = side * part + field * HALO_C, field * HALO_Y
            low[at : at + HALO_C, :] = ref[first : first + HALO_C, :]
            high[at : at + HALO_C, :] = ref[first + HALO_Y - HALO_C : first + HALO_Y, :]
        at = side * part + 3 * HALO_C
        low[at : at + META, :] = ref[3 * HALO_Y :, :]
        high[at : at + META, :] = ref[3 * HALO_Y :, :]


def vmem(count):
    return [pl.BlockSpec(memory_space=pltpu.VMEM)] * count


def shift(x, axis, by):
    count = lax.axis_size(axis)
    return lax.ppermute(x, axis, [(i, (i + by) % count) for i in range(count)])


def body(
    background_field,
    perturbation,
    permittivity,
    probe_nodes,
    probe_weights,
    probe_owner,
    probe_sensor,
    sensor_weight,
):
    devices = lax.axis_size("px") * lax.axis_size("py")
    fields = [by_tiles(f) for f in (permittivity, background_field, perturbation)]
    weights = jnp.pad(sensor_weight, (0, 128 - sensor_weight.shape[0]))[None, :]

    def rows(*counts):
        return [jax.ShapeDtypeStruct((n, 128), F32) for n in counts]

    def call(kernel, outs, *args, scratch=(), limit, bytes_accessed=0):
        return pl.pallas_call(
            kernel,
            out_shape=tuple(outs),
            in_specs=vmem(len(args)),
            out_specs=tuple(vmem(len(outs))),
            scratch_shapes=scratch,
            compiler_params=pltpu.CompilerParams(vmem_limit_bytes=limit * 2**20),
            cost_estimate=pl.CostEstimate(
                flops=0, bytes_accessed=bytes_accessed, transcendentals=0
            ),
        )(*args)

    size_x, size_y, size_c = 3 * HALO_X + META, 3 * HALO_Y + META, 2 * (3 * HALO_C + META)
    table = jax.ShapeDtypeStruct((16, 1024), F32)
    low_x, high_x, low_y, high_y, meta = call(
        pack_kernel,
        rows(size_x, size_x, size_y, size_y) + [table],
        *fields,
        probe_nodes,
        probe_weights,
        probe_owner.reshape(1, -1),
        probe_sensor.reshape(1, -1),
        limit=4,
    )
    px_low, px_high = shift(high_x, "px", 1), shift(low_x, "px", -1)
    py_low, py_high = shift(high_y, "py", 1), shift(low_y, "py", -1)
    compact = jax.ShapeDtypeStruct((CX, CY, 8, 128), F32)
    full = jax.ShapeDtypeStruct((EX, EY, 8, 128), F32)
    own_q, own_bg, own_qp, hot = call(
        own_kernel,
        [compact] * 3 + [jax.ShapeDtypeStruct((CZ, 4096), BF16)],
        *fields,
        meta,
        limit=8,
        bytes_accessed=8 * 2**20,
    )
    low_c, high_c = call(corner_kernel, rows(size_c, size_c), py_low, py_high, limit=4)
    c_low, c_high = shift(high_c, "px", 1), shift(low_c, "px", -1)
    sides = (px_low, px_high, py_low, py_high, c_low, c_high)

    block = pltpu.VMEM((EX, EY, 8, 128), F32)
    readings, q, bg, cz = call(
        tangent_kernel,
        rows(devices * 9) + [full] * 3,
        own_q,
        own_bg,
        own_qp,
        *sides,
        meta,
        hot,
        weights,
        scratch=[block] * 4
        + [pltpu.VMEM((2 * CX * CY, CZ), BF16), pltpu.VMEM((8, 1024), F32)],
        limit=18,
    )
    got = lax.all_to_all(
        readings.reshape(devices, 1, 9 * 128),
        ("px", "py"),
        split_axis=0,
        concat_axis=0,
        tiled=True,
    ).reshape(devices * 9, 128)
    (result,) = call(
        adjoint_kernel,
        rows(ROWS),
        got,
        *sides,
        meta,
        hot,
        q,
        bg,
        cz,
        scratch=[block] * 3
        + [
            pltpu.VMEM((2 * CX * CY, 4096), BF16),
            pltpu.VMEM((16, 1024), F32),
            pltpu.VMEM((8, 1024), F32),
        ],
        limit=24,
    )
    return from_tiles(result)


def solution(mesh):
    placed = (
        P("px", "py", None),
        P("px", "py", None),
        P("px", "py", None),
        P(None, ("px", "py")),
        P(None, ("px", "py")),
        P(("px", "py"), None),
        P(("px", "py")),
        P(("px", "py")),
    )
    return jax.shard_map(
        body, mesh=mesh, in_specs=placed, out_specs=P("px", "py", None), check_vma=False
    )
```

```python
import jax
import jax.numpy as jnp
import numpy as np
from jax import lax
from jax.experimental import pallas as pl
from jax.experimental.pallas import tpu as pltpu
from jax.sharding import PartitionSpec as P

SWEEPS = 4
MASS = 1.0
LOW = 1.0
HIGH = 25.0
CENTRE = 0.5 * (HIGH + LOW)
HALF = 0.5 * (HIGH - LOW)

CX, CY, CZ = 8, 32, 1024
D = 4
EX, EY = CX + 2 * D, CY + 2 * D
ROWS = CX * CY * 8
PLANE = CY * 8
PX_AT = (0, D * PLANE, (2 * D - 1) * PLANE)
PX_FLUX = (3 * D - 2) * PLANE
PX_META = (3 * D - 1) * PLANE
HALO_Y = CX * D * 8
CELLS = tuple((dx, dy) for dx in range(1, D) for dy in range(1, D) if dx + dy <= D)
HALO_C = len(CELLS) * 8
META = 80
PART = 3 * HALO_C + META
F32 = jnp.float32
BF16 = jnp.bfloat16


def horner_terms():
    spread = CENTRE / HALF
    size = SWEEPS
    iterate = np.zeros(size)
    remain = np.eye(size)[0]
    search = remain / CENTRE
    ratio = 1.0 / spread
    for sweep in range(SWEEPS):
        iterate = iterate + search
        if sweep < SWEEPS - 1:
            shifted = np.concatenate([[0.0], search[:-1]])
            remain = remain - (CENTRE * search + HALF * shifted)
            following = 1.0 / (2.0 * spread - ratio)
            search = following * ratio * search + 2.0 * following / HALF * remain
            ratio = following
    return [float(v) for v in iterate]


A0, A1, A2, A3 = horner_terms()


def lane_of(n):
    return lax.broadcasted_iota(jnp.int32, (n, 8, 128), 2)


def z_up(f):
    r = pltpu.roll(f, 127, 2)
    return jnp.where(lane_of(f.shape[0]) == 127, pltpu.roll(r, 7, 1), r)


def z_down(f):
    r = pltpu.roll(f, 1, 2)
    return jnp.where(lane_of(f.shape[0]) == 0, pltpu.roll(r, 1, 1), r)


def z_face(q):
    n = q.shape[0]
    sub = lax.broadcasted_iota(jnp.int32, (n, 8, 128), 1)
    last = (sub == 7) & (lane_of(n) == 127)
    return jnp.where(last, 0.0, q + z_up(q))


def fluxes(src, q, cz, x, y, n):
    fe, qe = src[x, pl.ds(y - 1, n + 2)], q[x, pl.ds(y - 1, n + 2)]
    f, qc = fe[1:-1], qe[1:-1]
    fy = (fe[1:] - fe[:-1]) * (qe[1:] + qe[:-1])
    acc = fy[1:] - fy[:-1]
    acc += (src[x + 1, pl.ds(y, n)] - f) * (q[x + 1, pl.ds(y, n)] + qc)
    acc += (src[x - 1, pl.ds(y, n)] - f) * (q[x - 1, pl.ds(y, n)] + qc)
    fz = (z_up(f) - f) * (z_face(qc) if cz is None else cz[x, pl.ds(y, n)])
    return f, acc + (fz - z_down(fz))


def cover(low, high, n):
    starts = list(range(low, high - n + 1, n))
    if starts[-1] + n < high:
        starts.append(high - n)
    return starts


def sweep(margin, n, step):
    def plane(x, carry):
        for y in cover(margin, EY - margin, n):
            step(x, y, n)
        return carry

    lax.fori_loop(margin, EX - margin, plane, 0)


def extend(field, own, sides, out, scale):
    px_low, px_high, py_low, py_high, c_low, c_high = sides
    middle_x, middle_y = slice(D, D + CX), slice(D, D + CY)
    out[middle_x, middle_y] = own[...]
    planes = D if field == 0 else D - 1
    for ref, at in ((px_low, D - planes), (px_high, D + CX)):
        v = ref[PX_AT[field] : PX_AT[field] + planes * PLANE, :]
        out[at : at + planes, middle_y] = v.reshape(planes, CY, 8, 128) * scale
    for ref, at in ((py_low, 0), (py_high, D + CY)):
        v = ref[field * HALO_Y : (field + 1) * HALO_Y, :]
        out[middle_x, at : at + D] = v.reshape(CX, D, 8, 128) * scale
    blank = jnp.zeros((D, D, 8, 128), F32)
    for x, ref in ((0, c_low), (D + CX, c_high)):
        for side, y in enumerate((0, D + CY)):
            out[x : x + D, y : y + D] = blank
            for i, (dx, dy) in enumerate(CELLS):
                at = side * PART + field * HALO_C + i * 8
                cell_x = x + D - dx if x == 0 else x + dx - 1
                cell_y = y + D - dy if y == 0 else y + dy - 1
                out[cell_x, cell_y] = ref[at : at + 8, :] * scale


def far_planes(sides, bg, qp):
    middle_y = slice(D, D + CY)
    for ref, at, beside in ((sides[0], 0, 1), (sides[1], EX - 1, EX - 2)):
        flux = ref[PX_FLUX : PX_FLUX + PLANE, :].reshape(CY, 8, 128)
        bg[at, middle_y] = bg[beside, middle_y] + flux
        qp[at, middle_y] = 1.0 - qp[beside, middle_y]


def close_edges(out, sign):
    px, py = lax.axis_index("px"), lax.axis_index("py")
    last_x, last_y = lax.axis_size("px") - 1, lax.axis_size("py") - 1

    @pl.when(px == 0)
    def _():
        out[D - 1] = out[D] * sign

    @pl.when(px == last_x)
    def _():
        out[D + CX] = out[D + CX - 1] * sign

    @pl.when(py == 0)
    def _():
        out[:, D - 1] = out[:, D] * sign

    @pl.when(py == last_y)
    def _():
        out[:, D + CY] = out[:, D + CY - 1] * sign


def take_meta(ref, base, out):
    for c in range(8):
        lanes = slice(c * 128, (c + 1) * 128)
        out[0:8, lanes] = ref[base + c * 8 : base + c * 8 + 8, :]
        for i in range(2):
            at = base + 64 + i * 8 + c
            out[8 + i : 9 + i, lanes] = ref[at : at + 1, :]


def two_parts(v):
    high = v.astype(BF16)
    return high, (v - high.astype(F32)).astype(BF16)


def three_parts(v):
    high = v.astype(BF16)
    rest = v - high.astype(F32)
    mid = rest.astype(BF16)
    return high, mid, (rest - mid.astype(F32)).astype(BF16)


def one_hot(index, count):
    at = lax.broadcasted_iota(jnp.int32, (count, index.shape[1]), 0)
    return jnp.where(at == index, 1.0, 0.0).astype(BF16)


def dot(a, b, over):
    return lax.dot_general(a, b, (over, ((), ())), preferred_element_type=F32)


def tangent_kernel(
    permit,
    back,
    perturb,
    px_low,
    px_high,
    py_low,
    py_high,
    c_low,
    c_high,
    meta,
    hot,
    weights,
    out,
    q,
    bg,
    cz,
    qp,
    b,
    y1,
    y2,
    table,
    vals,
):
    sides = (px_low, px_high, py_low, py_high, c_low, c_high)
    extend(0, permit, sides, q, 0.5 / HALF)
    extend(1, back, sides, bg, 1.0)
    extend(2, perturb, sides, qp, 0.5)
    far_planes(sides, bg, qp)
    close_edges(q, -1.0)
    close_edges(qp, -1.0)
    close_edges(bg, 1.0)

    def first(x, y, n):
        _, acc = fluxes(bg, qp, None, x, y, n)
        b[x, pl.ds(y, n)] = acc
        cz[x, pl.ds(y, n)] = z_face(q[x, pl.ds(y, n)])

    def second(x, y, n):
        f, acc = fluxes(b, q, cz, x, y, n)
        y1[x, pl.ds(y, n)] = (A2 - A3) * f - A3 * acc

    def third(x, y, n):
        f, acc = fluxes(y1, q, cz, x, y, n)
        y2[x, pl.ds(y, n)] = A1 * b[x, pl.ds(y, n)] - f - acc

    def fourth(x, y, n):
        f, acc = fluxes(y2, q, cz, x, y, n)
        y1[x, pl.ds(y, n)] = A0 * b[x, pl.ds(y, n)] - f - acc

    sweep(1, 4, first)
    sweep(2, 4, second)
    sweep(3, 4, third)
    sweep(4, 4, fourth)

    flat = y1.reshape(EX * EY * 8, 128)
    for x in range(CX):
        for c in range(8):
            v = flat[pl.ds(((x + D) * EY + D) * 8 + c, CY, stride=8), :]
            high, low = two_parts(v)
            table[x * CY : (x + 1) * CY, c * 128 : (c + 1) * 128] = high
            table[CX * CY + x * CY : CX * CY + (x + 1) * CY, c * 128 : (c + 1) * 128] = low

    vals[...] = jnp.zeros_like(vals)
    wide = 512

    def gather(i, carry):
        k, lanes = i // 2, pl.ds(pl.multiple_of((i % 2) * wide, wide), wide)
        node = meta[pl.ds(k, 1), lanes].astype(jnp.int32)
        found = dot(table[...], hot[:, pl.ds(pl.multiple_of(i * wide, wide), wide)], ((1,), (0,)))
        found = found[: CX * CY] + found[CX * CY :]
        at = lax.broadcasted_iota(jnp.int32, found.shape, 0)
        found = jnp.sum(jnp.where(at == node >> 10, found, 0.0), axis=0, keepdims=True)
        vals[0:1, lanes] += meta[pl.ds(k + 4, 1), lanes] * found
        return carry

    lax.fori_loop(0, 8, gather, 0)

    owner, sensor = meta[8:9, :].astype(jnp.int32), meta[9:10, :].astype(jnp.int32)
    at = lax.broadcasted_iota(jnp.int32, (8, 1024), 0)
    owned = jnp.where(at == sensor, vals[0:1, :], 0.0)
    parts = jnp.concatenate(three_parts(owned), axis=0)
    sums = dot(parts, one_hot(owner, 128), ((1,), (1,)))
    readings = sums[0:8] + sums[8:16] + sums[16:24]
    block = jnp.concatenate([readings, weights[...]] * 8, axis=0)
    for i in range(out.shape[0] // 72):
        out[i * 72 : (i + 1) * 72, :] = block


def scatter(meta, values, rows, cols, per, tiles, lhs, keep, hot=None):
    for k in range(4):
        node = meta[k : k + 1, :].astype(jnp.int32)
        high, low = two_parts(values[k : k + 1, :])
        hit = lax.broadcasted_iota(jnp.int32, (per, 1024), 0) == rows(node)
        lanes = slice(k * 1024, (k + 1) * 1024)
        lhs[0:per, lanes] = jnp.where(hit, high.astype(F32), 0.0).astype(BF16)
        lhs[per : 2 * per, lanes] = jnp.where(hit, low.astype(F32), 0.0).astype(BF16)

    def tile(t, carry):
        total = None
        for k in range(4):
            lanes = slice(k * 1024, (k + 1) * 1024)
            if hot is None:
                node = meta[k : k + 1, :].astype(jnp.int32)
                hits = one_hot(cols(node) - t * 256, 256)
            else:
                hits = hot[pl.ds(pl.multiple_of(t * 256, 256), 256), lanes]
            part = dot(lhs[0 : 2 * per, lanes], hits, ((1,), (1,)))
            total = part if total is None else total + part
        keep(t, total[0:per] + total[per : 2 * per])
        return carry

    if tiles == 1:
        tile(0, 0)
    else:
        lax.fori_loop(0, tiles, tile, 0)


def adjoint_kernel(
    got,
    px_low,
    px_high,
    py_low,
    py_high,
    c_low,
    c_high,
    meta,
    hot,
    q,
    bg,
    cz,
    out,
    src,
    y1,
    y2,
    lhs,
    near,
    values,
):
    count = got.shape[0] // 9
    sums = [jnp.sum(got[pl.ds(i, count, stride=9), :], axis=0, keepdims=True) for i in range(8)]
    readings = jnp.concatenate(sums, axis=0)
    weights = jnp.transpose(got[pl.ds(8, count, stride=9), :])[0:8]
    weighted = jnp.concatenate(three_parts(readings * weights), axis=0)

    def returned(table):
        owner, sensor = table[8:9, :].astype(jnp.int32), table[9:10, :].astype(jnp.int32)
        found = dot(weighted, one_hot(owner, 128), ((1,), (0,)))
        found = found[0:8] + found[8:16] + found[16:24]
        at = lax.broadcasted_iota(jnp.int32, found.shape, 0)
        found = jnp.sum(jnp.where(at == sensor, found, 0.0), axis=0, keepdims=True)
        values[0:4, :] = table[4:8, :] * found

    flat = src.reshape(EX * EY * 8, 128)

    def xy(node):
        return node >> 15, (node >> 10) & (CY - 1)

    def put_planes(x0, planes):
        def keep(t, sums):
            for x in range(planes):
                for half in range(2):
                    flat[pl.ds(((x + x0) * EY + D) * 8 + t * 2 + half, CY, stride=8), :] = sums[
                        x * CY : (x + 1) * CY, half * 128 : (half + 1) * 128
                    ]

        return keep

    def put_strip(x0, planes, y0):
        def keep(t, sums):
            for zq in range(4):
                for x in range(0, planes):
                    block = sums[zq * planes * D + x * D : zq * planes * D + (x + 1) * D]
                    for half in range(2):
                        flat[
                            pl.ds(((x + x0) * EY + y0) * 8 + zq * 2 + half, D, stride=8), :
                        ] = block[:, half * 128 : (half + 1) * 128]

        return keep

    def column(node):
        return node & (CZ - 1)

    def low_column(node):
        return node & 255

    returned(meta)
    scatter(meta, values, lambda n: n >> 10, column, CX * CY, 4, lhs, put_planes(D, CX), hot)

    for ref, x0, first in ((px_low, 0, CX - D), (px_high, D + CX, 0)):
        take_meta(ref, PX_META, near)
        returned(near)
        scatter(
            near,
            values,
            lambda n, first=first: (n >> 10) - first * CY,
            column,
            D * CY,
            4,
            lhs,
            put_planes(x0, D),
        )

    def strip(first_x, planes, first_y):
        def rows(node):
            x, y = xy(node)
            x, y = x - first_x, y - first_y
            good = (x >= 0) & (x < planes) & (y >= 0) & (y < D)
            return jnp.where(good, ((node >> 8) & 3) * (planes * D) + x * D + y, -1)

        return rows

    for ref, y0, first in ((py_low, 0, CY - D), (py_high, D + CY, 0)):
        take_meta(ref, 3 * HALO_Y, near)
        returned(near)
        scatter(
            near, values, strip(0, CX, first), low_column, 4 * CX * D, 1, lhs, put_strip(D, CX, y0)
        )

    for ref, x0, first_x in ((c_low, 0, CX - D), (c_high, D + CX, 0)):
        for side, y0, first_y in ((0, 0, CY - D), (1, D + CY, 0)):
            take_meta(ref, side * PART + 3 * HALO_C, near)
            returned(near)
            scatter(
                near,
                values,
                strip(first_x, D, first_y),
                low_column,
                4 * D * D,
                1,
                lhs,
                put_strip(x0, D, y0),
            )

    def first(x, y, n):
        f, acc = fluxes(src, q, cz, x, y, n)
        y1[x, pl.ds(y, n)] = (A2 - A3) * f - A3 * acc

    def second(x, y, n):
        f, acc = fluxes(y1, q, cz, x, y, n)
        y2[x, pl.ds(y, n)] = A1 * src[x, pl.ds(y, n)] - f - acc

    def third(x, y, n):
        f, acc = fluxes(y2, q, cz, x, y, n)
        y1[x, pl.ds(y, n)] = A0 * src[x, pl.ds(y, n)] - f - acc

    sweep(1, 4, first)
    sweep(2, 4, second)
    sweep(3, 4, third)

    def last(x, y, n):
        ae, be = y1[x, pl.ds(y - 1, n + 2)], bg[x, pl.ds(y - 1, n + 2)]
        a, k = ae[1:-1], be[1:-1]
        sy = (ae[1:] - ae[:-1]) * (be[1:] - be[:-1])
        total = sy[1:] + sy[:-1]
        total += (y1[x + 1, pl.ds(y, n)] - a) * (bg[x + 1, pl.ds(y, n)] - k)
        total += (y1[x - 1, pl.ds(y, n)] - a) * (bg[x - 1, pl.ds(y, n)] - k)
        sub = lax.broadcasted_iota(jnp.int32, (n, 8, 128), 1)
        end = (sub == 7) & (lane_of(n) == 127)
        sz = jnp.where(end, 0.0, (z_up(a) - a) * (z_up(k) - k))
        total = -0.5 * (total + (sz + z_down(sz)))
        yy = y - D
        for i in range(n):
            row = (x - D) * (CY // 8) + (yy + i) // 8
            out[pl.ds(row * 64 + (yy + i) % 8, 8, stride=8), :] = total[i]

    sweep(4, 4, last)


def by_tiles(block):
    lead = block.shape[:-2]
    rows, cols = block.shape[-2:]
    split = block.reshape(*lead, rows // 8, 8, cols // 128, 128)
    return jnp.swapaxes(split, -3, -2).reshape(-1, 128)


def from_tiles(rows):
    split = rows.reshape(CX, CY // 8, CZ // 128, 8, 128)
    return jnp.swapaxes(split, -3, -2).reshape(CX, CY, CZ)


def row_of(ref, x, y):
    return ref[pl.ds((x * (CY // 8) + y // 8) * 64 + y % 8, 8, stride=8), :]


def line_of(ref, x, y):
    return ref[pl.ds((x * (CY // 8) + y // 8) * 64 + y % 8, 8, stride=8), :]


def pack_kernel(
    permit_hbm,
    back_hbm,
    perturb_hbm,
    nodes_hbm,
    weights_hbm,
    owner_hbm,
    sensor_hbm,
    low_x,
    high_x,
    low_y,
    high_y,
    meta,
    permit,
    back,
    perturb,
    nodes,
    weights,
    owner,
    sensor,
    sems,
):
    pairs = (
        (nodes_hbm, nodes),
        (weights_hbm, weights),
        (owner_hbm, owner),
        (sensor_hbm, sensor),
        (permit_hbm, permit),
        (back_hbm, back),
        (perturb_hbm, perturb),
    )
    copies = [pltpu.make_async_copy(a, b, sems.at[i]) for i, (a, b) in enumerate(pairs)]
    for copy in copies:
        copy.start()
    for copy in copies[:4]:
        copy.wait()
    meta[0:4, :] = nodes[...].astype(F32)
    meta[4:8, :] = weights[...]
    meta[8:9, :] = owner[...].astype(F32)
    meta[9:10, :] = sensor[...].astype(F32)
    meta[10:16, :] = jnp.zeros((6, 1024), F32)
    for out, at in ((low_x, PX_META), (high_x, PX_META), (low_y, 3 * HALO_Y), (high_y, 3 * HALO_Y)):
        for c in range(8):
            lanes = slice(c * 128, (c + 1) * 128)
            out[at + c * 8 : at + c * 8 + 8, :] = meta[0:8, lanes]
            for i in range(2):
                out[at + 64 + i * 8 + c : at + 65 + i * 8 + c, :] = meta[8 + i : 9 + i, lanes]

    for field, ref in enumerate((permit, back, perturb)):
        copies[4 + field].wait()
        planes = D if field == 0 else D - 1

        def plane(x, carry, field=field, ref=ref, planes=planes):
            for y in range(CY):
                at = pl.ds(PX_AT[field] + (x * CY + y) * 8, 8)
                low_x[at, :] = row_of(ref, x, y)
                high_x[at, :] = row_of(ref, x + CX - planes, y)
            return carry

        lax.fori_loop(0, planes, plane, 0)
        for x in range(CX):
            for y in range(D):
                at = pl.ds(field * HALO_Y + (x * D + y) * 8, 8)
                low_y[at, :] = row_of(ref, x, y)
                high_y[at, :] = row_of(ref, x, y + CY - D)

    def flux(y, carry):
        for out, near, far in ((low_x, D - 2, D - 1), (high_x, CX - D + 1, CX - D)):
            face = 0.5 * (line_of(perturb, near, y) + line_of(perturb, far, y))
            at = pl.ds(pl.multiple_of(PX_FLUX + y * 8, 8), 8)
            out[at, :] = face * (line_of(back, far, y) - line_of(back, near, y))
        return carry

    lax.fori_loop(0, CY, flux, 0)


def own_kernel(permit_hbm, back_hbm, perturb_hbm, meta, q, bg, qp, hot, permit, back, perturb, sems):
    pairs = ((permit_hbm, permit), (back_hbm, back), (perturb_hbm, perturb))
    copies = [pltpu.make_async_copy(a, b, sems.at[i]) for i, (a, b) in enumerate(pairs)]
    for copy in copies:
        copy.start()

    def entries(i, carry):
        k, lanes = i // 2, pl.ds(pl.multiple_of((i % 2) * 512, 512), 512)
        node = meta[pl.ds(k, 1), lanes].astype(jnp.int32)
        hot[:, pl.ds(pl.multiple_of(i * 512, 512), 512)] = one_hot(node & (CZ - 1), CZ)
        return carry

    lax.fori_loop(0, 8, entries, 0)
    for copy in copies:
        copy.wait()

    def plane(x, carry):
        for y in range(CY):
            q[x, y] = row_of(permit, x, y) * (0.5 / HALF)
            bg[x, y] = row_of(back, x, y)
            qp[x, y] = row_of(perturb, x, y) * 0.5
        return carry

    lax.fori_loop(0, CX, plane, 0)


def corner_kernel(py_low, py_high, low, high):
    for side, ref in enumerate((py_low, py_high)):
        for field in range(3):
            for i, (dx, dy) in enumerate(CELLS):
                y = D - dy if side == 0 else dy - 1
                at = side * PART + field * HALO_C + i * 8
                for out, x in ((low, dx - 1), (high, CX - dx)):
                    first = field * HALO_Y + (x * D + y) * 8
                    out[at : at + 8, :] = ref[first : first + 8, :]
        at = side * PART + 3 * HALO_C
        low[at : at + META, :] = ref[3 * HALO_Y :, :]
        high[at : at + META, :] = ref[3 * HALO_Y :, :]


def vmem(count):
    return [pl.BlockSpec(memory_space=pltpu.VMEM)] * count


def shift(x, axis, by):
    count = lax.axis_size(axis)
    return lax.ppermute(x, axis, [(i, (i + by) % count) for i in range(count)])


def body(
    background_field,
    perturbation,
    permittivity,
    probe_nodes,
    probe_weights,
    probe_owner,
    probe_sensor,
    sensor_weight,
):
    devices = lax.axis_size("px") * lax.axis_size("py")
    fields = [by_tiles(f) for f in (permittivity, background_field, perturbation)]
    weights = jnp.pad(sensor_weight, (0, 128 - sensor_weight.shape[0]))[None, :]

    def rows(*counts):
        return [jax.ShapeDtypeStruct((n, 128), F32) for n in counts]

    def call(kernel, outs, *args, hbm=0, scratch=(), limit, bytes_accessed=0):
        held = [pltpu.with_memory_space_constraint(a, pltpu.HBM) for a in args[:hbm]]
        args = held + list(args[hbm:])
        return pl.pallas_call(
            kernel,
            out_shape=tuple(outs),
            in_specs=[pl.BlockSpec(memory_space=pltpu.HBM)] * hbm + vmem(len(args) - hbm),
            out_specs=tuple(vmem(len(outs))),
            scratch_shapes=scratch,
            compiler_params=pltpu.CompilerParams(vmem_limit_bytes=limit * 2**20),
            cost_estimate=pl.CostEstimate(
                flops=0, bytes_accessed=bytes_accessed, transcendentals=0
            ),
        )(*args)

    size_x, size_y, size_c = PX_META + META, 3 * HALO_Y + META, 2 * PART
    raw = [pltpu.VMEM((ROWS, 128), F32)] * 3
    table = jax.ShapeDtypeStruct((16, 1024), F32)
    low_x, high_x, low_y, high_y, meta = call(
        pack_kernel,
        rows(size_x, size_x, size_y, size_y) + [table],
        *fields,
        probe_nodes,
        probe_weights,
        probe_owner.reshape(1, -1),
        probe_sensor.reshape(1, -1),
        hbm=7,
        scratch=raw
        + [
            pltpu.VMEM((4, 1024), jnp.int32),
            pltpu.VMEM((4, 1024), F32),
            pltpu.VMEM((1, 1024), jnp.int32),
            pltpu.VMEM((1, 1024), jnp.int32),
            pltpu.SemaphoreType.DMA((7,)),
        ],
        limit=6,
    )
    px_low, px_high = shift(high_x, "px", 1), shift(low_x, "px", -1)
    py_low, py_high = shift(high_y, "py", 1), shift(low_y, "py", -1)
    compact = jax.ShapeDtypeStruct((CX, CY, 8, 128), F32)
    full = jax.ShapeDtypeStruct((EX, EY, 8, 128), F32)
    own_q, own_bg, own_qp, hot = call(
        own_kernel,
        [compact] * 3 + [jax.ShapeDtypeStruct((CZ, 4096), BF16)],
        *fields,
        meta,
        hbm=3,
        scratch=raw + [pltpu.SemaphoreType.DMA((3,))],
        limit=10,
        bytes_accessed=8 * 2**20,
    )
    low_c, high_c = call(corner_kernel, rows(size_c, size_c), py_low, py_high, limit=4)
    c_low, c_high = shift(high_c, "px", 1), shift(low_c, "px", -1)
    sides = (px_low, px_high, py_low, py_high, c_low, c_high)

    block = pltpu.VMEM((EX, EY, 8, 128), F32)
    readings, q, bg, cz = call(
        tangent_kernel,
        rows(devices * 9) + [full] * 3,
        own_q,
        own_bg,
        own_qp,
        *sides,
        meta,
        hot,
        weights,
        scratch=[block] * 4
        + [pltpu.VMEM((2 * CX * CY, CZ), BF16), pltpu.VMEM((8, 1024), F32)],
        limit=18,
    )
    got = lax.all_to_all(
        readings.reshape(devices, 1, 9 * 128),
        ("px", "py"),
        split_axis=0,
        concat_axis=0,
        tiled=True,
    ).reshape(devices * 9, 128)
    (result,) = call(
        adjoint_kernel,
        rows(ROWS),
        got,
        *sides,
        meta,
        hot,
        q,
        bg,
        cz,
        scratch=[block] * 3
        + [
            pltpu.VMEM((2 * CX * CY, 4096), BF16),
            pltpu.VMEM((16, 1024), F32),
            pltpu.VMEM((8, 1024), F32),
        ],
        limit=24,
    )
    return from_tiles(result)


def solution(mesh):
    placed = (
        P("px", "py", None),
        P("px", "py", None),
        P("px", "py", None),
        P(None, ("px", "py")),
        P(None, ("px", "py")),
        P(("px", "py"), None),
        P(("px", "py")),
        P(("px", "py")),
    )
    return jax.shard_map(
        body, mesh=mesh, in_specs=placed, out_specs=P("px", "py", None), check_vma=False
    )
```

```python
import jax
import jax.numpy as jnp
import numpy as np
from jax import lax
from jax.experimental import pallas as pl
from jax.experimental.pallas import tpu as pltpu
from jax.sharding import PartitionSpec as P

SWEEPS = 4
MASS = 1.0
LOW = 1.0
HIGH = 25.0
CENTRE = 0.5 * (HIGH + LOW)
HALF = 0.5 * (HIGH - LOW)

CX, CY, CZ = 8, 32, 1024
D = 4
EX, EY = CX + 2 * D, CY + 2 * D
ROWS = CX * CY * 8
PLANE = CY * 8
PX_AT = (0, D * PLANE, (2 * D - 1) * PLANE)
PX_FLUX = (3 * D - 2) * PLANE
PX_META = (3 * D - 1) * PLANE
HALO_Y = CX * D * 8
CELLS = tuple((dx, dy) for dx in range(1, D) for dy in range(1, D) if dx + dy <= D)
HALO_C = len(CELLS) * 8
META = 80
PART = 3 * HALO_C + META
F32 = jnp.float32
BF16 = jnp.bfloat16


def horner_terms():
    spread = CENTRE / HALF
    size = SWEEPS
    iterate = np.zeros(size)
    remain = np.eye(size)[0]
    search = remain / CENTRE
    ratio = 1.0 / spread
    for sweep in range(SWEEPS):
        iterate = iterate + search
        if sweep < SWEEPS - 1:
            shifted = np.concatenate([[0.0], search[:-1]])
            remain = remain - (CENTRE * search + HALF * shifted)
            following = 1.0 / (2.0 * spread - ratio)
            search = following * ratio * search + 2.0 * following / HALF * remain
            ratio = following
    return [float(v) for v in iterate]


A0, A1, A2, A3 = horner_terms()


def lane_of(n):
    return lax.broadcasted_iota(jnp.int32, (n, 8, 128), 2)


def z_up(f):
    r = pltpu.roll(f, 127, 2)
    return jnp.where(lane_of(f.shape[0]) == 127, pltpu.roll(r, 7, 1), r)


def z_down(f):
    r = pltpu.roll(f, 1, 2)
    return jnp.where(lane_of(f.shape[0]) == 0, pltpu.roll(r, 1, 1), r)


def z_face(q):
    n = q.shape[0]
    sub = lax.broadcasted_iota(jnp.int32, (n, 8, 128), 1)
    last = (sub == 7) & (lane_of(n) == 127)
    return jnp.where(last, 0.0, q + z_up(q))


def side_fluxes(src, q, x, y, n):
    fe, qe = src[x, pl.ds(y - 1, n + 2)], q[x, pl.ds(y - 1, n + 2)]
    f, qc = fe[1:-1], qe[1:-1]
    fy = (fe[1:] - fe[:-1]) * (qe[1:] + qe[:-1])
    acc = fy[1:] - fy[:-1]
    acc += (src[x + 1, pl.ds(y, n)] - f) * (q[x + 1, pl.ds(y, n)] + qc)
    acc += (src[x - 1, pl.ds(y, n)] - f) * (q[x - 1, pl.ds(y, n)] + qc)
    return f, acc


def z_fluxes(f, faces):
    fz = (z_up(f) - f) * faces
    return fz - z_down(fz)


def fluxes(src, q, cz, x, y, n):
    f, acc = side_fluxes(src, q, x, y, n)
    return f, acc + z_fluxes(f, cz[x, pl.ds(y, n)])


def cover(low, high, n):
    starts = list(range(low, high - n + 1, n))
    if starts[-1] + n < high:
        starts.append(high - n)
    return starts


def sweep(margin, n, step):
    def plane(x, carry):
        for y in cover(margin, EY - margin, n):
            step(x, y, n)
        return carry

    lax.fori_loop(margin, EX - margin, plane, 0)


def extend(field, own, sides, out, scale):
    px_low, px_high, py_low, py_high, c_low, c_high = sides
    middle_x, middle_y = slice(D, D + CX), slice(D, D + CY)
    out[middle_x, middle_y] = own[...]
    planes = D if field == 0 else D - 1
    for ref, at in ((px_low, D - planes), (px_high, D + CX)):
        v = ref[PX_AT[field] : PX_AT[field] + planes * PLANE, :]
        out[at : at + planes, middle_y] = v.reshape(planes, CY, 8, 128) * scale
    for ref, at in ((py_low, 0), (py_high, D + CY)):
        v = ref[field * HALO_Y : (field + 1) * HALO_Y, :]
        out[middle_x, at : at + D] = v.reshape(CX, D, 8, 128) * scale
    blank = jnp.zeros((D, D, 8, 128), F32)
    for x, ref in ((0, c_low), (D + CX, c_high)):
        for side, y in enumerate((0, D + CY)):
            out[x : x + D, y : y + D] = blank
            for i, (dx, dy) in enumerate(CELLS):
                at = side * PART + field * HALO_C + i * 8
                cell_x = x + D - dx if x == 0 else x + dx - 1
                cell_y = y + D - dy if y == 0 else y + dy - 1
                out[cell_x, cell_y] = ref[at : at + 8, :] * scale


def far_planes(sides, bg, qp):
    middle_y = slice(D, D + CY)
    for ref, at, beside in ((sides[0], 0, 1), (sides[1], EX - 1, EX - 2)):
        flux = ref[PX_FLUX : PX_FLUX + PLANE, :].reshape(CY, 8, 128)
        bg[at, middle_y] = bg[beside, middle_y] + flux
        qp[at, middle_y] = 1.0 - qp[beside, middle_y]


def close_edges(out, sign):
    px, py = lax.axis_index("px"), lax.axis_index("py")
    last_x, last_y = lax.axis_size("px") - 1, lax.axis_size("py") - 1

    @pl.when(px == 0)
    def _():
        out[D - 1] = out[D] * sign

    @pl.when(px == last_x)
    def _():
        out[D + CX] = out[D + CX - 1] * sign

    @pl.when(py == 0)
    def _():
        out[:, D - 1] = out[:, D] * sign

    @pl.when(py == last_y)
    def _():
        out[:, D + CY] = out[:, D + CY - 1] * sign


def take_meta(ref, base, out):
    for c in range(8):
        lanes = slice(c * 128, (c + 1) * 128)
        out[0:8, lanes] = ref[base + c * 8 : base + c * 8 + 8, :]
        for i in range(2):
            at = base + 64 + i * 8 + c
            out[8 + i : 9 + i, lanes] = ref[at : at + 1, :]


def two_parts(v):
    high = v.astype(BF16)
    return high, (v - high.astype(F32)).astype(BF16)


def three_parts(v):
    high = v.astype(BF16)
    rest = v - high.astype(F32)
    mid = rest.astype(BF16)
    return high, mid, (rest - mid.astype(F32)).astype(BF16)


def one_hot(index, count):
    at = lax.broadcasted_iota(jnp.int32, (count, index.shape[1]), 0)
    return jnp.where(at == index, 1.0, 0.0).astype(BF16)


def rows16(index):
    shape = (16, index.shape[1])
    numbers = lax.broadcasted_iota(jnp.int32, shape, 0).astype(jnp.int16)
    return jnp.broadcast_to(index, shape).astype(jnp.int16), numbers


def put_one_hot(index, count, out, first, lanes):
    wanted, numbers = rows16(index)
    one, zero = jnp.ones(wanted.shape, BF16), jnp.zeros(wanted.shape, BF16)
    for r in range(count // 16):
        hit = numbers + jnp.int16(r * 16) == wanted
        out[first + r * 16 : first + (r + 1) * 16, lanes] = jnp.where(hit, one, zero)


def dot(a, b, over):
    return lax.dot_general(a, b, (over, ((), ())), preferred_element_type=F32)


def tangent_kernel(
    permit,
    back,
    perturb,
    own_cz,
    own_bz,
    px_low,
    px_high,
    py_low,
    py_high,
    c_low,
    c_high,
    meta,
    hot,
    weights,
    out,
    q,
    bg,
    cz,
    qp,
    b,
    y1,
    y2,
    table,
    vals,
):
    sides = (px_low, px_high, py_low, py_high, c_low, c_high)
    extend(0, permit, sides, q, 0.5 / HALF)
    extend(1, back, sides, bg, 1.0)
    extend(2, perturb, sides, qp, 0.5)
    far_planes(sides, bg, qp)
    close_edges(q, -1.0)
    close_edges(qp, -1.0)
    close_edges(bg, 1.0)

    cz[D : D + CX, D : D + CY] = own_cz[...]

    def outer(x, y, n):
        f, acc = side_fluxes(bg, qp, x, y, n)
        b[x, pl.ds(y, n)] = acc + z_fluxes(f, z_face(qp[x, pl.ds(y, n)]))
        cz[x, pl.ds(y, n)] = z_face(q[x, pl.ds(y, n)])

    def outer_planes(i, carry):
        for x in (1 + i, D + CX + i):
            for y in cover(1, EY - 1, 4):
                outer(x, y, 4)
        return carry

    def own_planes(x, carry):
        outer(x, 1, D - 1)
        outer(x, D + CY, D - 1)
        for y in cover(D, D + CY, 4):
            _, acc = side_fluxes(bg, qp, x, y, 4)
            b[x, pl.ds(y, 4)] = acc + own_bz[x - D, pl.ds(y - D, 4)]
        return carry

    lax.fori_loop(0, D - 1, outer_planes, 0)
    lax.fori_loop(D, D + CX, own_planes, 0)

    def second(x, y, n):
        f, acc = fluxes(b, q, cz, x, y, n)
        y1[x, pl.ds(y, n)] = (A2 - A3) * f - A3 * acc

    def third(x, y, n):
        f, acc = fluxes(y1, q, cz, x, y, n)
        y2[x, pl.ds(y, n)] = A1 * b[x, pl.ds(y, n)] - f - acc

    def fourth(x, y, n):
        f, acc = fluxes(y2, q, cz, x, y, n)
        y1[x, pl.ds(y, n)] = A0 * b[x, pl.ds(y, n)] - f - acc

    sweep(2, 4, second)
    sweep(3, 4, third)
    sweep(4, 4, fourth)

    flat = y1.reshape(EX * EY * 8, 128)
    for x in range(CX):
        for c in range(8):
            v = flat[pl.ds(((x + D) * EY + D) * 8 + c, CY, stride=8), :]
            high, low = two_parts(v)
            table[x * CY : (x + 1) * CY, c * 128 : (c + 1) * 128] = high
            table[CX * CY + x * CY : CX * CY + (x + 1) * CY, c * 128 : (c + 1) * 128] = low

    vals[...] = jnp.zeros_like(vals)
    wide = 512

    def gather(i, carry):
        k, lanes = i // 2, pl.ds(pl.multiple_of((i % 2) * wide, wide), wide)
        node = meta[pl.ds(k, 1), lanes].astype(jnp.int32)
        found = dot(table[...], hot[:, pl.ds(pl.multiple_of(i * wide, wide), wide)], ((1,), (0,)))
        found = found[: CX * CY] + found[CX * CY :]
        at = lax.broadcasted_iota(jnp.int32, found.shape, 0)
        found = jnp.sum(jnp.where(at == node >> 10, found, 0.0), axis=0, keepdims=True)
        vals[0:1, lanes] += meta[pl.ds(k + 4, 1), lanes] * found
        return carry

    lax.fori_loop(0, 8, gather, 0)

    owner, sensor = meta[8:9, :].astype(jnp.int32), meta[9:10, :].astype(jnp.int32)
    at = lax.broadcasted_iota(jnp.int32, (8, 1024), 0)
    owned = jnp.where(at == sensor, vals[0:1, :], 0.0)
    parts = jnp.concatenate(three_parts(owned), axis=0)
    sums = dot(parts, one_hot(owner, 128), ((1,), (1,)))
    readings = sums[0:8] + sums[8:16] + sums[16:24]
    block = jnp.concatenate([readings, weights[...]] * 8, axis=0)
    for i in range(out.shape[0] // 72):
        out[i * 72 : (i + 1) * 72, :] = block


def scatter(meta, values, rows, per, tiles, lhs, keep, hot):
    for k in range(4):
        wanted, numbers = rows16(rows(meta[k : k + 1, :].astype(jnp.int32)))
        value = jnp.broadcast_to(values[k : k + 1, :], wanted.shape)
        high, low = two_parts(value)
        zero = jnp.zeros(wanted.shape, BF16)
        lanes = slice(k * 1024, (k + 1) * 1024)
        for r in range(per // 16):
            hit = numbers + jnp.int16(r * 16) == wanted
            lhs[r * 16 : (r + 1) * 16, lanes] = jnp.where(hit, high, zero)
            lhs[per + r * 16 : per + (r + 1) * 16, lanes] = jnp.where(hit, low, zero)

    def tile(t, carry):
        total = None
        for k in range(4):
            lanes = slice(k * 1024, (k + 1) * 1024)
            hits = hot[pl.ds(pl.multiple_of(t * 256, 256), 256), lanes]
            part = dot(lhs[0 : 2 * per, lanes], hits, ((1,), (1,)))
            total = part if total is None else total + part
        keep(t, total[0:per] + total[per : 2 * per])
        return carry

    if tiles == 1:
        tile(0, 0)
    else:
        lax.fori_loop(0, tiles, tile, 0)


def adjoint_kernel(
    got,
    px_low,
    px_high,
    py_low,
    py_high,
    c_low,
    c_high,
    meta,
    hot,
    q,
    bg,
    cz,
    out,
    src,
    y1,
    y2,
    lhs,
    near_hot,
    near,
    values,
):
    count = got.shape[0] // 9
    sums = [jnp.sum(got[pl.ds(i, count, stride=9), :], axis=0, keepdims=True) for i in range(8)]
    readings = jnp.concatenate(sums, axis=0)
    weights = jnp.transpose(got[pl.ds(8, count, stride=9), :])[0:8]
    weighted = jnp.concatenate(three_parts(readings * weights), axis=0)

    def returned(table):
        owner, sensor = table[8:9, :].astype(jnp.int32), table[9:10, :].astype(jnp.int32)
        found = dot(weighted, one_hot(owner, 128), ((1,), (0,)))
        found = found[0:8] + found[8:16] + found[16:24]
        at = lax.broadcasted_iota(jnp.int32, found.shape, 0)
        found = jnp.sum(jnp.where(at == sensor, found, 0.0), axis=0, keepdims=True)
        values[0:4, :] = table[4:8, :] * found

    flat = src.reshape(EX * EY * 8, 128)

    def put_planes(x0, planes, tiles):
        def keep(t, sums):
            for zq in range(4 // tiles):
                for x in range(planes):
                    first = (zq * planes + x) * CY
                    for half in range(2):
                        c = zq * tiles * 2 + t * 2 + half
                        flat[pl.ds(((x + x0) * EY + D) * 8 + c, CY, stride=8), :] = sums[
                            first : first + CY, half * 128 : (half + 1) * 128
                        ]

        return keep

    def put_strip(x0, planes, y0):
        def keep(t, sums):
            for zq in range(4):
                for x in range(planes):
                    first = (zq * planes + x) * D
                    for half in range(2):
                        flat[
                            pl.ds(((x + x0) * EY + y0) * 8 + zq * 2 + half, D, stride=8), :
                        ] = sums[first : first + D, half * 128 : (half + 1) * 128]

        return keep

    def box(first_x, planes, first_y, lines, bits):
        def rows(node):
            x, y = (node >> 15) - first_x, ((node >> 10) & (CY - 1)) - first_y
            good = (x >= 0) & (x < planes) & (y >= 0) & (y < lines)
            z = (node & (CZ - 1)) >> bits
            return jnp.where(good, (z * planes + x) * lines + y, -1)

        return rows

    returned(meta)
    scatter(meta, values, lambda n: n >> 10, CX * CY, 4, lhs, put_planes(D, CX, 4), hot)

    def columns(count):
        for k in range(4):
            node = near[k : k + 1, :].astype(jnp.int32)
            put_one_hot(node & (count - 1), count, near_hot, 0, slice(k * 1024, (k + 1) * 1024))

    low_x, high_x = (0, CX - D), (D + CX, 0)
    low_y, high_y = (0, CY - D), (D + CY, 0)
    for ref, (x0, first) in ((px_low, low_x), (px_high, high_x)):
        take_meta(ref, PX_META, near)
        returned(near)
        columns(512)
        rows = box(first, D, 0, CY, 9)
        scatter(near, values, rows, 2 * D * CY, 2, lhs, put_planes(x0, D, 2), near_hot)
    strips = [(ref, 3 * HALO_Y, D, 0, CX) + y for ref, y in ((py_low, low_y), (py_high, high_y))]
    for ref, (x0, first) in ((c_low, low_x), (c_high, high_x)):
        for side, y in enumerate((low_y, high_y)):
            strips.append((ref, side * PART + 3 * HALO_C, x0, first, D) + y)
    for ref, base, x0, first_x, planes, y0, first_y in strips:
        take_meta(ref, base, near)
        returned(near)
        columns(256)
        rows = box(first_x, planes, first_y, D, 8)
        keep = put_strip(x0, planes, y0)
        scatter(near, values, rows, 4 * planes * D, 1, lhs, keep, near_hot)

    def first(x, y, n):
        f, acc = fluxes(src, q, cz, x, y, n)
        y1[x, pl.ds(y, n)] = (A2 - A3) * f - A3 * acc

    def second(x, y, n):
        f, acc = fluxes(y1, q, cz, x, y, n)
        y2[x, pl.ds(y, n)] = A1 * src[x, pl.ds(y, n)] - f - acc

    def third(x, y, n):
        f, acc = fluxes(y2, q, cz, x, y, n)
        y1[x, pl.ds(y, n)] = A0 * src[x, pl.ds(y, n)] - f - acc

    sweep(1, 4, first)
    sweep(2, 4, second)
    sweep(3, 4, third)

    def last(x, y, n):
        ae, be = y1[x, pl.ds(y - 1, n + 2)], bg[x, pl.ds(y - 1, n + 2)]
        a, k = ae[1:-1], be[1:-1]
        sy = (ae[1:] - ae[:-1]) * (be[1:] - be[:-1])
        total = sy[1:] + sy[:-1]
        total += (y1[x + 1, pl.ds(y, n)] - a) * (bg[x + 1, pl.ds(y, n)] - k)
        total += (y1[x - 1, pl.ds(y, n)] - a) * (bg[x - 1, pl.ds(y, n)] - k)
        sub = lax.broadcasted_iota(jnp.int32, (n, 8, 128), 1)
        end = (sub == 7) & (lane_of(n) == 127)
        sz = jnp.where(end, 0.0, (z_up(a) - a) * (z_up(k) - k))
        total = -0.5 * (total + (sz + z_down(sz)))
        yy = y - D
        for i in range(n):
            row = (x - D) * (CY // 8) + (yy + i) // 8
            out[pl.ds(row * 64 + (yy + i) % 8, 8, stride=8), :] = total[i]

    sweep(4, 4, last)


def by_tiles(block):
    lead = block.shape[:-2]
    rows, cols = block.shape[-2:]
    split = block.reshape(*lead, rows // 8, 8, cols // 128, 128)
    return jnp.swapaxes(split, -3, -2).reshape(-1, 128)


def from_tiles(rows):
    split = rows.reshape(CX, CY // 8, CZ // 128, 8, 128)
    return jnp.swapaxes(split, -3, -2).reshape(CX, CY, CZ)


def row_of(ref, x, y):
    return ref[pl.ds((x * (CY // 8) + y // 8) * 64 + y % 8, 8, stride=8), :]


def line_of(ref, x, y):
    return ref[pl.ds((x * (CY // 8) + y // 8) * 64 + y % 8, 8, stride=8), :]


def pack_kernel(
    permit_hbm,
    back_hbm,
    perturb_hbm,
    nodes_hbm,
    weights_hbm,
    owner_hbm,
    sensor_hbm,
    low_x,
    high_x,
    low_y,
    high_y,
    meta,
    permit,
    back,
    perturb,
    nodes,
    weights,
    owner,
    sensor,
    sems,
):
    pairs = (
        (nodes_hbm, nodes),
        (weights_hbm, weights),
        (owner_hbm, owner),
        (sensor_hbm, sensor),
        (permit_hbm, permit),
        (back_hbm, back),
        (perturb_hbm, perturb),
    )
    copies = [pltpu.make_async_copy(a, b, sems.at[i]) for i, (a, b) in enumerate(pairs)]
    for copy in copies:
        copy.start()
    for copy in copies[:4]:
        copy.wait()
    meta[0:4, :] = nodes[...].astype(F32)
    meta[4:8, :] = weights[...]
    meta[8:9, :] = owner[...].astype(F32)
    meta[9:10, :] = sensor[...].astype(F32)
    meta[10:16, :] = jnp.zeros((6, 1024), F32)
    for out, at in ((low_x, PX_META), (high_x, PX_META), (low_y, 3 * HALO_Y), (high_y, 3 * HALO_Y)):
        for c in range(8):
            lanes = slice(c * 128, (c + 1) * 128)
            out[at + c * 8 : at + c * 8 + 8, :] = meta[0:8, lanes]
            for i in range(2):
                out[at + 64 + i * 8 + c : at + 65 + i * 8 + c, :] = meta[8 + i : 9 + i, lanes]

    for field, ref in enumerate((permit, back, perturb)):
        copies[4 + field].wait()
        planes = D if field == 0 else D - 1

        def plane(x, carry, field=field, ref=ref, planes=planes):
            for y in range(CY):
                at = pl.ds(PX_AT[field] + (x * CY + y) * 8, 8)
                low_x[at, :] = row_of(ref, x, y)
                high_x[at, :] = row_of(ref, x + CX - planes, y)
            return carry

        lax.fori_loop(0, planes, plane, 0)
        for x in range(CX):
            for y in range(D):
                at = pl.ds(field * HALO_Y + (x * D + y) * 8, 8)
                low_y[at, :] = row_of(ref, x, y)
                high_y[at, :] = row_of(ref, x, y + CY - D)

    def flux(y, carry):
        for out, near, far in ((low_x, D - 2, D - 1), (high_x, CX - D + 1, CX - D)):
            face = 0.5 * (line_of(perturb, near, y) + line_of(perturb, far, y))
            at = pl.ds(pl.multiple_of(PX_FLUX + y * 8, 8), 8)
            out[at, :] = face * (line_of(back, far, y) - line_of(back, near, y))
        return carry

    lax.fori_loop(0, CY, flux, 0)


def own_kernel(
    permit_hbm,
    back_hbm,
    perturb_hbm,
    meta,
    q,
    bg,
    qp,
    cz,
    bz,
    hot,
    permit,
    back,
    perturb,
    sems,
):
    pairs = ((permit_hbm, permit), (back_hbm, back), (perturb_hbm, perturb))
    copies = [pltpu.make_async_copy(a, b, sems.at[i]) for i, (a, b) in enumerate(pairs)]
    for copy in copies:
        copy.start()

    def entries(i, carry):
        k, lanes = i // 2, pl.ds(pl.multiple_of((i % 2) * 512, 512), 512)
        node = meta[pl.ds(k, 1), lanes].astype(jnp.int32)
        at = pl.ds(pl.multiple_of(i * 512, 512), 512)
        put_one_hot(node & (CZ - 1), CZ, hot, 0, at)
        return carry

    lax.fori_loop(0, 8, entries, 0)
    for copy in copies:
        copy.wait()

    def plane(x, carry):
        for y in range(CY):
            q[x, y] = row_of(permit, x, y) * (0.5 / HALF)
            bg[x, y] = row_of(back, x, y)
            qp[x, y] = row_of(perturb, x, y) * 0.5
        for y in range(0, CY, 4):
            at = pl.ds(y, 4)
            cz[x, at] = z_face(q[x, at])
            bz[x, at] = z_fluxes(bg[x, at], z_face(qp[x, at]))
        return carry

    lax.fori_loop(0, CX, plane, 0)


def corner_kernel(py_low, py_high, after, low, high):
    del after
    for side, ref in enumerate((py_low, py_high)):
        for field in range(3):
            for i, (dx, dy) in enumerate(CELLS):
                y = D - dy if side == 0 else dy - 1
                at = side * PART + field * HALO_C + i * 8
                for out, x in ((low, dx - 1), (high, CX - dx)):
                    first = field * HALO_Y + (x * D + y) * 8
                    out[at : at + 8, :] = ref[first : first + 8, :]
        at = side * PART + 3 * HALO_C
        low[at : at + META, :] = ref[3 * HALO_Y :, :]
        high[at : at + META, :] = ref[3 * HALO_Y :, :]


def vmem(count):
    return [pl.BlockSpec(memory_space=pltpu.VMEM)] * count


def shift(x, axis, by):
    count = lax.axis_size(axis)
    return lax.ppermute(x, axis, [(i, (i + by) % count) for i in range(count)])


def body(
    background_field,
    perturbation,
    permittivity,
    probe_nodes,
    probe_weights,
    probe_owner,
    probe_sensor,
    sensor_weight,
):
    devices = lax.axis_size("px") * lax.axis_size("py")
    fields = [by_tiles(f) for f in (permittivity, background_field, perturbation)]
    weights = jnp.pad(sensor_weight, (0, 128 - sensor_weight.shape[0]))[None, :]

    def rows(*counts):
        return [jax.ShapeDtypeStruct((n, 128), F32) for n in counts]

    def call(kernel, outs, *args, hbm=0, scratch=(), limit, bytes_accessed=0):
        held = [pltpu.with_memory_space_constraint(a, pltpu.HBM) for a in args[:hbm]]
        args = held + list(args[hbm:])
        return pl.pallas_call(
            kernel,
            out_shape=tuple(outs),
            in_specs=[pl.BlockSpec(memory_space=pltpu.HBM)] * hbm + vmem(len(args) - hbm),
            out_specs=tuple(vmem(len(outs))),
            scratch_shapes=scratch,
            compiler_params=pltpu.CompilerParams(vmem_limit_bytes=limit * 2**20),
            cost_estimate=pl.CostEstimate(
                flops=0, bytes_accessed=bytes_accessed, transcendentals=0
            ),
        )(*args)

    size_x, size_y, size_c = PX_META + META, 3 * HALO_Y + META, 2 * PART
    raw = [pltpu.VMEM((ROWS, 128), F32)] * 3
    table = jax.ShapeDtypeStruct((16, 1024), F32)
    low_x, high_x, low_y, high_y, meta = call(
        pack_kernel,
        rows(size_x, size_x, size_y, size_y) + [table],
        *fields,
        probe_nodes,
        probe_weights,
        probe_owner.reshape(1, -1),
        probe_sensor.reshape(1, -1),
        hbm=7,
        scratch=raw
        + [
            pltpu.VMEM((4, 1024), jnp.int32),
            pltpu.VMEM((4, 1024), F32),
            pltpu.VMEM((1, 1024), jnp.int32),
            pltpu.VMEM((1, 1024), jnp.int32),
            pltpu.SemaphoreType.DMA((7,)),
        ],
        limit=6,
    )
    px_low, px_high = shift(high_x, "px", 1), shift(low_x, "px", -1)
    py_low, py_high = shift(high_y, "py", 1), shift(low_y, "py", -1)
    compact = jax.ShapeDtypeStruct((CX, CY, 8, 128), F32)
    full = jax.ShapeDtypeStruct((EX, EY, 8, 128), F32)
    own_q, own_bg, own_qp, own_cz, own_bz, hot = call(
        own_kernel,
        [compact] * 5 + [jax.ShapeDtypeStruct((CZ, 4096), BF16)],
        *fields,
        meta,
        hbm=3,
        scratch=raw + [pltpu.SemaphoreType.DMA((3,))],
        limit=10,
        bytes_accessed=8 * 2**20,
    )
    low_c, high_c = call(corner_kernel, rows(size_c, size_c), py_low, py_high, own_cz, limit=4)
    c_low, c_high = shift(high_c, "px", 1), shift(low_c, "px", -1)
    sides = (px_low, px_high, py_low, py_high, c_low, c_high)

    block = pltpu.VMEM((EX, EY, 8, 128), F32)
    readings, q, bg, cz = call(
        tangent_kernel,
        rows(devices * 9) + [full] * 3,
        own_q,
        own_bg,
        own_qp,
        own_cz,
        own_bz,
        *sides,
        meta,
        hot,
        weights,
        scratch=[block] * 4
        + [pltpu.VMEM((2 * CX * CY, CZ), BF16), pltpu.VMEM((8, 1024), F32)],
        limit=20,
    )
    got = lax.all_to_all(
        readings.reshape(devices, 1, 9 * 128),
        ("px", "py"),
        split_axis=0,
        concat_axis=0,
        tiled=True,
    ).reshape(devices * 9, 128)
    (result,) = call(
        adjoint_kernel,
        rows(ROWS),
        got,
        *sides,
        meta,
        hot,
        q,
        bg,
        cz,
        scratch=[block] * 3
        + [
            pltpu.VMEM((2 * CX * CY, 4096), BF16),
            pltpu.VMEM((512, 4096), BF16),
            pltpu.VMEM((16, 1024), F32),
            pltpu.VMEM((8, 1024), F32),
        ],
        limit=28,
    )
    return from_tiles(result)


def solution(mesh):
    placed = (
        P("px", "py", None),
        P("px", "py", None),
        P("px", "py", None),
        P(None, ("px", "py")),
        P(None, ("px", "py")),
        P(("px", "py"), None),
        P(("px", "py")),
        P(("px", "py")),
    )
    return jax.shard_map(
        body, mesh=mesh, in_specs=placed, out_specs=P("px", "py", None), check_vma=False
    )
```

```python
import jax
import jax.numpy as jnp
import numpy as np
from jax import lax
from jax.experimental import pallas as pl
from jax.experimental.pallas import tpu as pltpu
from jax.sharding import PartitionSpec as P

SWEEPS = 4
MASS = 1.0
LOW = 1.0
HIGH = 25.0
CENTRE = 0.5 * (HIGH + LOW)
HALF = 0.5 * (HIGH - LOW)

CX, CY, CZ = 8, 32, 1024
D = 4
EX, EY = CX + 2 * D, CY + 2 * D
ROWS = CX * CY * 8
PLANE = CY * 8
PX_AT = (0, D * PLANE, (2 * D - 1) * PLANE)
PX_FLUX = (3 * D - 2) * PLANE
PX_ROWS = (3 * D - 1) * PLANE
HALO_Y = CX * D * 8
CELLS = tuple((dx, dy) for dx in range(1, D) for dy in range(1, D) if dx + dy <= D)
HALO_C = len(CELLS) * 8
META = 80
PART = 3 * HALO_C + META
F32 = jnp.float32
BF16 = jnp.bfloat16


def horner_terms():
    spread = CENTRE / HALF
    size = SWEEPS
    iterate = np.zeros(size)
    remain = np.eye(size)[0]
    search = remain / CENTRE
    ratio = 1.0 / spread
    for sweep in range(SWEEPS):
        iterate = iterate + search
        if sweep < SWEEPS - 1:
            shifted = np.concatenate([[0.0], search[:-1]])
            remain = remain - (CENTRE * search + HALF * shifted)
            following = 1.0 / (2.0 * spread - ratio)
            search = following * ratio * search + 2.0 * following / HALF * remain
            ratio = following
    return [float(v) for v in iterate]


A0, A1, A2, A3 = horner_terms()


def lane_of(n):
    return lax.broadcasted_iota(jnp.int32, (n, 8, 128), 2)


def z_up(f):
    r = pltpu.roll(f, 127, 2)
    return jnp.where(lane_of(f.shape[0]) == 127, pltpu.roll(r, 7, 1), r)


def z_down(f):
    r = pltpu.roll(f, 1, 2)
    return jnp.where(lane_of(f.shape[0]) == 0, pltpu.roll(r, 1, 1), r)


def z_face(q):
    n = q.shape[0]
    sub = lax.broadcasted_iota(jnp.int32, (n, 8, 128), 1)
    last = (sub == 7) & (lane_of(n) == 127)
    return jnp.where(last, 0.0, q + z_up(q))


def side_fluxes(src, q, x, y, n):
    fe, qe = src[x, pl.ds(y - 1, n + 2)], q[x, pl.ds(y - 1, n + 2)]
    f, qc = fe[1:-1], qe[1:-1]
    fy = (fe[1:] - fe[:-1]) * (qe[1:] + qe[:-1])
    acc = fy[1:] - fy[:-1]
    acc += (src[x + 1, pl.ds(y, n)] - f) * (q[x + 1, pl.ds(y, n)] + qc)
    acc += (src[x - 1, pl.ds(y, n)] - f) * (q[x - 1, pl.ds(y, n)] + qc)
    return f, acc


def z_fluxes(f, faces):
    fz = (z_up(f) - f) * faces
    return fz - z_down(fz)


def fluxes(src, q, cz, x, y, n):
    f, acc = side_fluxes(src, q, x, y, n)
    return f, acc + z_fluxes(f, cz[x, pl.ds(y, n)])


def cover(low, high, n):
    starts = list(range(low, high - n + 1, n))
    if starts[-1] + n < high:
        starts.append(high - n)
    return starts


def sweep(margin, n, step):
    def plane(x, carry):
        for y in cover(margin, EY - margin, n):
            step(x, y, n)
        return carry

    lax.fori_loop(margin, EX - margin, plane, 0)


def extend(field, own, sides, out, scale):
    px_low, px_high, py_low, py_high, c_low, c_high = sides
    middle_x, middle_y = slice(D, D + CX), slice(D, D + CY)
    out[middle_x, middle_y] = own[...]
    planes = D if field == 0 else D - 1
    for ref, at in ((px_low, D - planes), (px_high, D + CX)):
        v = ref[PX_AT[field] : PX_AT[field] + planes * PLANE, :]
        out[at : at + planes, middle_y] = v.reshape(planes, CY, 8, 128) * scale
    for ref, at in ((py_low, 0), (py_high, D + CY)):
        v = ref[field * HALO_Y : (field + 1) * HALO_Y, :]
        out[middle_x, at : at + D] = v.reshape(CX, D, 8, 128) * scale
    blank = jnp.zeros((D, D, 8, 128), F32)
    for x, ref in ((0, c_low), (D + CX, c_high)):
        for side, y in enumerate((0, D + CY)):
            out[x : x + D, y : y + D] = blank
            for i, (dx, dy) in enumerate(CELLS):
                at = side * PART + field * HALO_C + i * 8
                cell_x = x + D - dx if x == 0 else x + dx - 1
                cell_y = y + D - dy if y == 0 else y + dy - 1
                out[cell_x, cell_y] = ref[at : at + 8, :] * scale


def far_planes(sides, bg, qp):
    middle_y = slice(D, D + CY)
    for ref, at, beside in ((sides[0], 0, 1), (sides[1], EX - 1, EX - 2)):
        flux = ref[PX_FLUX : PX_FLUX + PLANE, :].reshape(CY, 8, 128)
        bg[at, middle_y] = bg[beside, middle_y] + flux
        qp[at, middle_y] = 1.0 - qp[beside, middle_y]


def close_edges(out, sign):
    px, py = lax.axis_index("px"), lax.axis_index("py")
    last_x, last_y = lax.axis_size("px") - 1, lax.axis_size("py") - 1

    @pl.when(px == 0)
    def _():
        out[D - 1] = out[D] * sign

    @pl.when(px == last_x)
    def _():
        out[D + CX] = out[D + CX - 1] * sign

    @pl.when(py == 0)
    def _():
        out[:, D - 1] = out[:, D] * sign

    @pl.when(py == last_y)
    def _():
        out[:, D + CY] = out[:, D + CY - 1] * sign


def take_meta(ref, base, out):
    for c in range(8):
        lanes = slice(c * 128, (c + 1) * 128)
        out[0:8, lanes] = ref[base + c * 8 : base + c * 8 + 8, :]
        for i in range(2):
            at = base + 64 + i * 8 + c
            out[8 + i : 9 + i, lanes] = ref[at : at + 1, :]


def two_parts(v):
    high = v.astype(BF16)
    return high, (v - high.astype(F32)).astype(BF16)


def three_parts(v):
    high = v.astype(BF16)
    rest = v - high.astype(F32)
    mid = rest.astype(BF16)
    return high, mid, (rest - mid.astype(F32)).astype(BF16)


def one_hot(index, count):
    at = lax.broadcasted_iota(jnp.int32, (count, index.shape[1]), 0)
    return jnp.where(at == index, 1.0, 0.0).astype(BF16)


def rows16(index):
    shape = (16, index.shape[1])
    numbers = lax.broadcasted_iota(jnp.int32, shape, 0).astype(jnp.int16)
    return jnp.broadcast_to(index, shape).astype(jnp.int16), numbers


def put_one_hot(index, count, out, first, lanes):
    wanted, numbers = rows16(index)
    one, zero = jnp.ones(wanted.shape, BF16), jnp.zeros(wanted.shape, BF16)
    for r in range(count // 16):
        hit = numbers + jnp.int16(r * 16) == wanted
        out[first + r * 16 : first + (r + 1) * 16, lanes] = jnp.where(hit, one, zero)


def dot(a, b, over):
    return lax.dot_general(a, b, (over, ((), ())), preferred_element_type=F32)


def tangent_kernel(
    permit,
    back,
    perturb,
    own_cz,
    own_bz,
    px_low,
    px_high,
    py_low,
    py_high,
    c_low,
    c_high,
    meta,
    hot,
    weights,
    out,
    q,
    bg,
    cz,
    qp,
    b,
    y1,
    y2,
    table,
    vals,
):
    sides = (px_low, px_high, py_low, py_high, c_low, c_high)
    extend(0, permit, sides, q, 0.5 / HALF)
    extend(1, back, sides, bg, 1.0)
    extend(2, perturb, sides, qp, 0.5)
    far_planes(sides, bg, qp)
    close_edges(q, -1.0)
    close_edges(qp, -1.0)
    close_edges(bg, 1.0)

    cz[D : D + CX, D : D + CY] = own_cz[...]

    def outer(x, y, n):
        f, acc = side_fluxes(bg, qp, x, y, n)
        b[x, pl.ds(y, n)] = acc + z_fluxes(f, z_face(qp[x, pl.ds(y, n)]))
        cz[x, pl.ds(y, n)] = z_face(q[x, pl.ds(y, n)])

    def outer_planes(i, carry):
        x = jnp.where(i < D - 1, 1 + i, CX + 1 + i)
        for y in cover(1, EY - 1, 4):
            outer(x, y, 4)
        return carry

    def own_planes(x, carry):
        outer(x, 1, D - 1)
        outer(x, D + CY, D - 1)
        for y in cover(D, D + CY, 4):
            _, acc = side_fluxes(bg, qp, x, y, 4)
            b[x, pl.ds(y, 4)] = acc + own_bz[x - D, pl.ds(y - D, 4)]
        return carry

    lax.fori_loop(0, 2 * (D - 1), outer_planes, 0)
    lax.fori_loop(D, D + CX, own_planes, 0)

    def second(x, y, n):
        f, acc = fluxes(b, q, cz, x, y, n)
        y1[x, pl.ds(y, n)] = (A2 - A3) * f - A3 * acc

    def third(x, y, n):
        f, acc = fluxes(y1, q, cz, x, y, n)
        y2[x, pl.ds(y, n)] = A1 * b[x, pl.ds(y, n)] - f - acc

    def fourth(x, y, n):
        f, acc = fluxes(y2, q, cz, x, y, n)
        y1[x, pl.ds(y, n)] = A0 * b[x, pl.ds(y, n)] - f - acc

    sweep(2, 4, second)
    sweep(3, 4, third)
    sweep(4, 4, fourth)

    flat = y1.reshape(EX * EY * 8, 128)
    for x in range(CX):
        for c in range(8):
            v = flat[pl.ds(((x + D) * EY + D) * 8 + c, CY, stride=8), :]
            high, low = two_parts(v)
            table[x * CY : (x + 1) * CY, c * 128 : (c + 1) * 128] = high
            table[CX * CY + x * CY : CX * CY + (x + 1) * CY, c * 128 : (c + 1) * 128] = low

    vals[...] = jnp.zeros_like(vals)
    wide = 512

    def gather(i, carry):
        k, lanes = i // 2, pl.ds(pl.multiple_of((i % 2) * wide, wide), wide)
        node = meta[pl.ds(k, 1), lanes].astype(jnp.int32)
        found = dot(table[...], hot[:, pl.ds(pl.multiple_of(i * wide, wide), wide)], ((1,), (0,)))
        found = found[: CX * CY] + found[CX * CY :]
        at = lax.broadcasted_iota(jnp.int32, found.shape, 0)
        found = jnp.sum(jnp.where(at == node >> 10, found, 0.0), axis=0, keepdims=True)
        vals[0:1, lanes] += meta[pl.ds(k + 4, 1), lanes] * found
        return carry

    lax.fori_loop(0, 8, gather, 0)

    owner, sensor = meta[8:9, :].astype(jnp.int32), meta[9:10, :].astype(jnp.int32)
    at = lax.broadcasted_iota(jnp.int32, (8, 1024), 0)
    owned = jnp.where(at == sensor, vals[0:1, :], 0.0)
    parts = jnp.concatenate(three_parts(owned), axis=0)
    sums = dot(parts, one_hot(owner, 128), ((1,), (1,)))
    readings = sums[0:8] + sums[8:16] + sums[16:24]
    block = jnp.concatenate([readings, weights[...]] * 8, axis=0)
    for i in range(out.shape[0] // 72):
        out[i * 72 : (i + 1) * 72, :] = block


def scatter(meta, values, rows, per, tiles, width, lhs, keep, hot):
    for k in range(4):
        wanted, numbers = rows16(rows(meta[k : k + 1, :].astype(jnp.int32)))
        value = jnp.broadcast_to(values[k : k + 1, :], wanted.shape)
        high, low = two_parts(value)
        zero = jnp.zeros(wanted.shape, BF16)
        lanes = slice(k * 1024, (k + 1) * 1024)
        for r in range(per // 16):
            hit = numbers + jnp.int16(r * 16) == wanted
            lhs[r * 16 : (r + 1) * 16, lanes] = jnp.where(hit, high, zero)
            lhs[per + r * 16 : per + (r + 1) * 16, lanes] = jnp.where(hit, low, zero)

    def tile(t, carry):
        total = None
        for k in range(4):
            lanes = slice(k * 1024, (k + 1) * 1024)
            hits = hot[pl.ds(pl.multiple_of(t * width, width), width), lanes]
            part = dot(lhs[0 : 2 * per, lanes], hits, ((1,), (1,)))
            total = part if total is None else total + part
        keep(t, total[0:per] + total[per : 2 * per])
        return carry

    if tiles == 1:
        tile(0, 0)
    else:
        lax.fori_loop(0, tiles, tile, 0)


def returned(weighted, table, values):
    owner, sensor = table[8:9, :].astype(jnp.int32), table[9:10, :].astype(jnp.int32)
    parts = jnp.concatenate(three_parts(weighted), axis=0)
    found = dot(parts, one_hot(owner, 128), ((1,), (0,)))
    found = found[0:8] + found[8:16] + found[16:24]
    at = lax.broadcasted_iota(jnp.int32, found.shape, 0)
    found = jnp.sum(jnp.where(at == sensor, found, 0.0), axis=0, keepdims=True)
    values[0:4, :] = table[4:8, :] * found


def source_kernel(got, meta, hot, weighted, own, low, high, lhs, values):
    count = got.shape[0] // 9
    sums = [jnp.sum(got[pl.ds(i, count, stride=9), :], axis=0, keepdims=True) for i in range(8)]
    readings = jnp.concatenate(sums, axis=0)
    weights = jnp.transpose(got[pl.ds(8, count, stride=9), :])[0:8]
    weighted[...] = readings * weights

    def keep(t, sums):
        for x in range(CX):
            for i in range(4):
                block = sums[x * CY : (x + 1) * CY, i * 128 : (i + 1) * 128]
                own[pl.ds(x * PLANE + t * 4 + i, CY, stride=8), :] = block
                side, at = (low, x) if x < D else (high, x - (CX - D))
                side[pl.ds(at * PLANE + t * 4 + i, CY, stride=8), :] = block

    returned(weighted[...], meta, values)
    scatter(meta, values, lambda n: n >> 10, CX * CY, 2, 512, lhs, keep, hot)


def strips_kernel(
    weighted, py_low, py_high, c_low, c_high, strips, corners, lhs, near_hot, near, values
):
    def box(first_x, planes, first_y):
        def rows(node):
            x, y = (node >> 15) - first_x, ((node >> 10) & (CY - 1)) - first_y
            good = (x >= 0) & (x < planes) & (y >= 0) & (y < D)
            return jnp.where(good, (((node >> 8) & 3) * planes + x) * D + y, -1)

        return rows

    low_x, high_x, low_y, high_y = CX - D, 0, CY - D, 0
    tasks = [
        (py_low, 3 * HALO_Y, 0, CX, low_y, strips, 0),
        (py_high, 3 * HALO_Y, 0, CX, high_y, strips, HALO_Y),
    ]
    for i, (ref, first_x) in enumerate(((c_low, low_x), (c_high, high_x))):
        for side, first_y in enumerate((low_y, high_y)):
            base, to = side * PART + 3 * HALO_C, (2 * i + side) * D * D * 8
            tasks.append((ref, base, first_x, D, first_y, corners, to))
    for ref, base, first_x, planes, first_y, out, to in tasks:
        take_meta(ref, base, near)
        returned(weighted[...], near, values)
        for k in range(4):
            node = near[k : k + 1, :].astype(jnp.int32)
            put_one_hot(node & 255, 256, near_hot, 0, slice(k * 1024, (k + 1) * 1024))

        def keep(t, sums, planes=planes, out=out, to=to):
            lines = planes * D
            for zq in range(4):
                for half in range(2):
                    out[pl.ds(to + zq * 2 + half, lines, stride=8), :] = sums[
                        zq * lines : (zq + 1) * lines, half * 128 : (half + 1) * 128
                    ]

        rows = box(first_x, planes, first_y)
        scatter(near, values, rows, 4 * planes * D, 1, 256, lhs, keep, near_hot)


def adjoint_kernel(own, px_low, px_high, strips, corners, q, bg, cz, out, src, y1, y2):
    middle_x, middle_y = slice(D, D + CX), slice(D, D + CY)
    src[middle_x, middle_y] = own[...].reshape(CX, CY, 8, 128)
    for x, ref in ((0, px_low), (D + CX, px_high)):
        src[x : x + D, middle_y] = ref[...].reshape(D, CY, 8, 128)
    for side, y in enumerate((0, D + CY)):
        v = strips[side * HALO_Y : (side + 1) * HALO_Y, :]
        src[middle_x, y : y + D] = v.reshape(CX, D, 8, 128)
        for i, x in enumerate((0, D + CX)):
            at = (2 * i + side) * D * D * 8
            v = corners[at : at + D * D * 8, :]
            src[x : x + D, y : y + D] = v.reshape(D, D, 8, 128)

    def first(x, y, n):
        f, acc = fluxes(src, q, cz, x, y, n)
        y1[x, pl.ds(y, n)] = (A2 - A3) * f - A3 * acc

    def second(x, y, n):
        f, acc = fluxes(y1, q, cz, x, y, n)
        y2[x, pl.ds(y, n)] = A1 * src[x, pl.ds(y, n)] - f - acc

    def third(x, y, n):
        f, acc = fluxes(y2, q, cz, x, y, n)
        y1[x, pl.ds(y, n)] = A0 * src[x, pl.ds(y, n)] - f - acc

    sweep(1, 4, first)
    sweep(2, 4, second)
    sweep(3, 4, third)

    def last(x, y, n):
        ae, be = y1[x, pl.ds(y - 1, n + 2)], bg[x, pl.ds(y - 1, n + 2)]
        a, k = ae[1:-1], be[1:-1]
        sy = (ae[1:] - ae[:-1]) * (be[1:] - be[:-1])
        total = sy[1:] + sy[:-1]
        total += (y1[x + 1, pl.ds(y, n)] - a) * (bg[x + 1, pl.ds(y, n)] - k)
        total += (y1[x - 1, pl.ds(y, n)] - a) * (bg[x - 1, pl.ds(y, n)] - k)
        sub = lax.broadcasted_iota(jnp.int32, (n, 8, 128), 1)
        end = (sub == 7) & (lane_of(n) == 127)
        sz = jnp.where(end, 0.0, (z_up(a) - a) * (z_up(k) - k))
        total = -0.5 * (total + (sz + z_down(sz)))
        yy = y - D
        for i in range(n):
            row = (x - D) * (CY // 8) + (yy + i) // 8
            out[pl.ds(row * 64 + (yy + i) % 8, 8, stride=8), :] = total[i]

    sweep(4, 4, last)


def by_tiles(block):
    lead = block.shape[:-2]
    rows, cols = block.shape[-2:]
    split = block.reshape(*lead, rows // 8, 8, cols // 128, 128)
    return jnp.swapaxes(split, -3, -2).reshape(-1, 128)


def from_tiles(rows):
    split = rows.reshape(CX, CY // 8, CZ // 128, 8, 128)
    return jnp.swapaxes(split, -3, -2).reshape(CX, CY, CZ)


def row_of(ref, x, y):
    return ref[pl.ds((x * (CY // 8) + y // 8) * 64 + y % 8, 8, stride=8), :]


def line_of(ref, x, y):
    return ref[pl.ds((x * (CY // 8) + y // 8) * 64 + y % 8, 8, stride=8), :]


def pack_kernel(
    permit_hbm,
    back_hbm,
    perturb_hbm,
    nodes_hbm,
    weights_hbm,
    owner_hbm,
    sensor_hbm,
    low_x,
    high_x,
    low_y,
    high_y,
    meta,
    permit,
    back,
    perturb,
    nodes,
    weights,
    owner,
    sensor,
    sems,
):
    pairs = (
        (nodes_hbm, nodes),
        (weights_hbm, weights),
        (owner_hbm, owner),
        (sensor_hbm, sensor),
        (permit_hbm, permit),
        (back_hbm, back),
        (perturb_hbm, perturb),
    )
    copies = [pltpu.make_async_copy(a, b, sems.at[i]) for i, (a, b) in enumerate(pairs)]
    for copy in copies:
        copy.start()
    for copy in copies[:4]:
        copy.wait()
    meta[0:4, :] = nodes[...].astype(F32)
    meta[4:8, :] = weights[...]
    meta[8:9, :] = owner[...].astype(F32)
    meta[9:10, :] = sensor[...].astype(F32)
    meta[10:16, :] = jnp.zeros((6, 1024), F32)
    for out, at in ((low_y, 3 * HALO_Y), (high_y, 3 * HALO_Y)):
        for c in range(8):
            lanes = slice(c * 128, (c + 1) * 128)
            out[at + c * 8 : at + c * 8 + 8, :] = meta[0:8, lanes]
            for i in range(2):
                out[at + 64 + i * 8 + c : at + 65 + i * 8 + c, :] = meta[8 + i : 9 + i, lanes]

    for field, ref in enumerate((permit, back, perturb)):
        copies[4 + field].wait()
        planes = D if field == 0 else D - 1

        def plane(x, carry, field=field, ref=ref, planes=planes):
            for y in range(CY):
                at = pl.ds(PX_AT[field] + (x * CY + y) * 8, 8)
                low_x[at, :] = row_of(ref, x, y)
                high_x[at, :] = row_of(ref, x + CX - planes, y)
            return carry

        lax.fori_loop(0, planes, plane, 0)
        for x in range(CX):
            for y in range(D):
                at = pl.ds(field * HALO_Y + (x * D + y) * 8, 8)
                low_y[at, :] = row_of(ref, x, y)
                high_y[at, :] = row_of(ref, x, y + CY - D)

    def flux(y, carry):
        for out, near, far in ((low_x, D - 2, D - 1), (high_x, CX - D + 1, CX - D)):
            face = 0.5 * (line_of(perturb, near, y) + line_of(perturb, far, y))
            at = pl.ds(pl.multiple_of(PX_FLUX + y * 8, 8), 8)
            out[at, :] = face * (line_of(back, far, y) - line_of(back, near, y))
        return carry

    lax.fori_loop(0, CY, flux, 0)


def own_kernel(
    permit_hbm,
    back_hbm,
    perturb_hbm,
    meta,
    q,
    bg,
    qp,
    cz,
    bz,
    hot,
    permit,
    back,
    perturb,
    sems,
):
    pairs = ((permit_hbm, permit), (back_hbm, back), (perturb_hbm, perturb))
    copies = [pltpu.make_async_copy(a, b, sems.at[i]) for i, (a, b) in enumerate(pairs)]
    for copy in copies:
        copy.start()

    def entries(i, carry):
        k, lanes = i // 2, pl.ds(pl.multiple_of((i % 2) * 512, 512), 512)
        node = meta[pl.ds(k, 1), lanes].astype(jnp.int32)
        at = pl.ds(pl.multiple_of(i * 512, 512), 512)
        put_one_hot(node & (CZ - 1), CZ, hot, 0, at)
        return carry

    lax.fori_loop(0, 8, entries, 0)
    for copy in copies:
        copy.wait()

    def plane(x, carry):
        for y in range(CY):
            q[x, y] = row_of(permit, x, y) * (0.5 / HALF)
            bg[x, y] = row_of(back, x, y)
            qp[x, y] = row_of(perturb, x, y) * 0.5
        for y in range(0, CY, 4):
            at = pl.ds(y, 4)
            cz[x, at] = z_face(q[x, at])
            bz[x, at] = z_fluxes(bg[x, at], z_face(qp[x, at]))
        return carry

    lax.fori_loop(0, CX, plane, 0)


def corner_kernel(py_low, py_high, after, low, high):
    del after
    for side, ref in enumerate((py_low, py_high)):
        for field in range(3):
            for i, (dx, dy) in enumerate(CELLS):
                y = D - dy if side == 0 else dy - 1
                at = side * PART + field * HALO_C + i * 8
                for out, x in ((low, dx - 1), (high, CX - dx)):
                    first = field * HALO_Y + (x * D + y) * 8
                    out[at : at + 8, :] = ref[first : first + 8, :]
        at = side * PART + 3 * HALO_C
        low[at : at + META, :] = ref[3 * HALO_Y :, :]
        high[at : at + META, :] = ref[3 * HALO_Y :, :]


def vmem(count):
    return [pl.BlockSpec(memory_space=pltpu.VMEM)] * count


def shift(x, axis, by):
    count = lax.axis_size(axis)
    return lax.ppermute(x, axis, [(i, (i + by) % count) for i in range(count)])


def body(
    background_field,
    perturbation,
    permittivity,
    probe_nodes,
    probe_weights,
    probe_owner,
    probe_sensor,
    sensor_weight,
):
    devices = lax.axis_size("px") * lax.axis_size("py")
    fields = [by_tiles(f) for f in (permittivity, background_field, perturbation)]
    weights = jnp.pad(sensor_weight, (0, 128 - sensor_weight.shape[0]))[None, :]

    def rows(*counts):
        return [jax.ShapeDtypeStruct((n, 128), F32) for n in counts]

    def call(kernel, outs, *args, hbm=0, scratch=(), limit, bytes_accessed=0):
        held = [pltpu.with_memory_space_constraint(a, pltpu.HBM) for a in args[:hbm]]
        args = held + list(args[hbm:])
        return pl.pallas_call(
            kernel,
            out_shape=tuple(outs),
            in_specs=[pl.BlockSpec(memory_space=pltpu.HBM)] * hbm + vmem(len(args) - hbm),
            out_specs=tuple(vmem(len(outs))),
            scratch_shapes=scratch,
            compiler_params=pltpu.CompilerParams(vmem_limit_bytes=limit * 2**20),
            cost_estimate=pl.CostEstimate(
                flops=0, bytes_accessed=bytes_accessed, transcendentals=0
            ),
        )(*args)

    size_x, size_y, size_c = PX_ROWS, 3 * HALO_Y + META, 2 * PART
    raw = [pltpu.VMEM((ROWS, 128), F32)] * 3
    table = jax.ShapeDtypeStruct((16, 1024), F32)
    low_x, high_x, low_y, high_y, meta = call(
        pack_kernel,
        rows(size_x, size_x, size_y, size_y) + [table],
        *fields,
        probe_nodes,
        probe_weights,
        probe_owner.reshape(1, -1),
        probe_sensor.reshape(1, -1),
        hbm=7,
        scratch=raw
        + [
            pltpu.VMEM((4, 1024), jnp.int32),
            pltpu.VMEM((4, 1024), F32),
            pltpu.VMEM((1, 1024), jnp.int32),
            pltpu.VMEM((1, 1024), jnp.int32),
            pltpu.SemaphoreType.DMA((7,)),
        ],
        limit=6,
    )
    px_low, px_high = shift(high_x, "px", 1), shift(low_x, "px", -1)
    py_low, py_high = shift(high_y, "py", 1), shift(low_y, "py", -1)
    compact = jax.ShapeDtypeStruct((CX, CY, 8, 128), F32)
    full = jax.ShapeDtypeStruct((EX, EY, 8, 128), F32)
    own_q, own_bg, own_qp, own_cz, own_bz, hot = call(
        own_kernel,
        [compact] * 5 + [jax.ShapeDtypeStruct((CZ, 4096), BF16)],
        *fields,
        meta,
        hbm=3,
        scratch=raw + [pltpu.SemaphoreType.DMA((3,))],
        limit=10,
        bytes_accessed=8 * 2**20,
    )
    low_c, high_c = call(corner_kernel, rows(size_c, size_c), py_low, py_high, own_cz, limit=4)
    c_low, c_high = shift(high_c, "px", 1), shift(low_c, "px", -1)
    sides = (px_low, px_high, py_low, py_high, c_low, c_high)

    block = pltpu.VMEM((EX, EY, 8, 128), F32)
    readings, q, bg, cz = call(
        tangent_kernel,
        rows(devices * 9) + [full] * 3,
        own_q,
        own_bg,
        own_qp,
        own_cz,
        own_bz,
        *sides,
        meta,
        hot,
        weights,
        scratch=[block] * 4
        + [pltpu.VMEM((2 * CX * CY, CZ), BF16), pltpu.VMEM((8, 1024), F32)],
        limit=20,
    )
    got = lax.all_to_all(
        readings.reshape(devices, 1, 9 * 128),
        ("px", "py"),
        split_axis=0,
        concat_axis=0,
        tiled=True,
    ).reshape(devices * 9, 128)
    weighted, own_source, low_s, high_s = call(
        source_kernel,
        rows(8, ROWS, D * PLANE, D * PLANE),
        got,
        meta,
        hot,
        scratch=[pltpu.VMEM((2 * CX * CY, 4096), BF16), pltpu.VMEM((8, 1024), F32)],
        limit=18,
    )
    source_low, source_high = shift(high_s, "px", 1), shift(low_s, "px", -1)
    strips, corners = call(
        strips_kernel,
        rows(2 * HALO_Y, 4 * D * D * 8),
        weighted,
        *sides[2:],
        scratch=[
            pltpu.VMEM((2 * 4 * CX * D, 4096), BF16),
            pltpu.VMEM((256, 4096), BF16),
            pltpu.VMEM((16, 1024), F32),
            pltpu.VMEM((8, 1024), F32),
        ],
        limit=16,
        bytes_accessed=16 * 2**20,
    )
    (result,) = call(
        adjoint_kernel,
        rows(ROWS),
        own_source,
        source_low,
        source_high,
        strips,
        corners,
        q,
        bg,
        cz,
        scratch=[block] * 3,
        limit=16,
    )
    return from_tiles(result)


def solution(mesh):
    placed = (
        P("px", "py", None),
        P("px", "py", None),
        P("px", "py", None),
        P(None, ("px", "py")),
        P(None, ("px", "py")),
        P(("px", "py"), None),
        P(("px", "py")),
        P(("px", "py")),
    )
    return jax.shard_map(
        body, mesh=mesh, in_specs=placed, out_specs=P("px", "py", None), check_vma=False
    )
```

```python
import jax
import jax.numpy as jnp
import numpy as np
from jax import lax
from jax.experimental import pallas as pl
from jax.experimental.pallas import tpu as pltpu
from jax.sharding import PartitionSpec as P

SWEEPS = 4
MASS = 1.0
LOW = 1.0
HIGH = 25.0
CENTRE = 0.5 * (HIGH + LOW)
HALF = 0.5 * (HIGH - LOW)

CX, CY, CZ = 8, 32, 1024
D = 4
EX, EY = CX + 2 * D, CY + 2 * D
ROWS = CX * CY * 8
PLANE = CY * 8
PX_AT = (0, D * PLANE, (2 * D - 1) * PLANE)
PX_FLUX = (3 * D - 2) * PLANE
PX_ROWS = (3 * D - 1) * PLANE
HALO_Y = CX * D * 8
CELLS = tuple((dx, dy) for dx in range(1, D) for dy in range(1, D) if dx + dy <= D)
HALO_C = len(CELLS) * 8
META = 80
PART = 3 * HALO_C + META
F32 = jnp.float32
BF16 = jnp.bfloat16


def horner_terms():
    spread = CENTRE / HALF
    size = SWEEPS
    iterate = np.zeros(size)
    remain = np.eye(size)[0]
    search = remain / CENTRE
    ratio = 1.0 / spread
    for sweep in range(SWEEPS):
        iterate = iterate + search
        if sweep < SWEEPS - 1:
            shifted = np.concatenate([[0.0], search[:-1]])
            remain = remain - (CENTRE * search + HALF * shifted)
            following = 1.0 / (2.0 * spread - ratio)
            search = following * ratio * search + 2.0 * following / HALF * remain
            ratio = following
    return [float(v) for v in iterate]


A0, A1, A2, A3 = horner_terms()


def lane_of(n):
    return lax.broadcasted_iota(jnp.int32, (n, 8, 128), 2)


def z_up(f):
    r = pltpu.roll(f, 127, 2)
    return jnp.where(lane_of(f.shape[0]) == 127, pltpu.roll(r, 7, 1), r)


def z_down(f):
    r = pltpu.roll(f, 1, 2)
    return jnp.where(lane_of(f.shape[0]) == 0, pltpu.roll(r, 1, 1), r)


def z_face(q):
    n = q.shape[0]
    sub = lax.broadcasted_iota(jnp.int32, (n, 8, 128), 1)
    last = (sub == 7) & (lane_of(n) == 127)
    return jnp.where(last, 0.0, q + z_up(q))


def side_fluxes(src, q, x, y, n):
    fe, qe = src[x, pl.ds(y - 1, n + 2)], q[x, pl.ds(y - 1, n + 2)]
    f, qc = fe[1:-1], qe[1:-1]
    fy = (fe[1:] - fe[:-1]) * (qe[1:] + qe[:-1])
    acc = fy[1:] - fy[:-1]
    acc += (src[x + 1, pl.ds(y, n)] - f) * (q[x + 1, pl.ds(y, n)] + qc)
    acc += (src[x - 1, pl.ds(y, n)] - f) * (q[x - 1, pl.ds(y, n)] + qc)
    return f, acc


def z_fluxes(f, faces):
    fz = (z_up(f) - f) * faces
    return fz - z_down(fz)


def fluxes(src, q, cz, x, y, n):
    f, acc = side_fluxes(src, q, x, y, n)
    return f, acc + z_fluxes(f, cz[x, pl.ds(y, n)])


def cover(low, high, n):
    starts = list(range(low, high - n + 1, n))
    if starts[-1] + n < high:
        starts.append(high - n)
    return starts


def early(margin, plane):
    def step(x, carry):
        plane(x)
        return carry

    lax.fori_loop(margin + D, EX - D - margin, step, 0)


def late(margin, plane):
    def step(i, carry):
        plane(jnp.where(i < D, margin + i, EX - 2 * D - margin + i))
        return carry

    lax.fori_loop(0, 2 * D, step, 0)


def lines(margin, n, step):
    def plane(x):
        for y in cover(margin, EY - margin, n):
            step(x, y, n)

    return plane


def put_py(field, py_low, py_high, out, scale):
    for ref, at in ((py_low, 0), (py_high, D + CY)):
        v = ref[field * HALO_Y : (field + 1) * HALO_Y, :]
        out[D : D + CX, at : at + D] = v.reshape(CX, D, 8, 128) * scale


def put_px(field, sides, out, scale):
    px_low, px_high, c_low, c_high = sides
    middle_y = slice(D, D + CY)
    planes = D if field == 0 else D - 1
    for ref, at in ((px_low, D - planes), (px_high, D + CX)):
        v = ref[PX_AT[field] : PX_AT[field] + planes * PLANE, :]
        out[at : at + planes, middle_y] = v.reshape(planes, CY, 8, 128) * scale
    blank = jnp.zeros((D, D, 8, 128), F32)
    for x, ref in ((0, c_low), (D + CX, c_high)):
        for side, y in enumerate((0, D + CY)):
            out[x : x + D, y : y + D] = blank
            for i, (dx, dy) in enumerate(CELLS):
                at = side * PART + field * HALO_C + i * 8
                cell_x = x + D - dx if x == 0 else x + dx - 1
                cell_y = y + D - dy if y == 0 else y + dy - 1
                out[cell_x, cell_y] = ref[at : at + 8, :] * scale


def far_planes(sides, bg, qp):
    middle_y = slice(D, D + CY)
    for ref, at, beside in ((sides[0], 0, 1), (sides[1], EX - 1, EX - 2)):
        flux = ref[PX_FLUX : PX_FLUX + PLANE, :].reshape(CY, 8, 128)
        bg[at, middle_y] = bg[beside, middle_y] + flux
        qp[at, middle_y] = 1.0 - qp[beside, middle_y]


def close_py(out, sign, planes):
    py, last_y = lax.axis_index("py"), lax.axis_size("py") - 1

    @pl.when(py == 0)
    def _():
        out[planes, D - 1] = out[planes, D] * sign

    @pl.when(py == last_y)
    def _():
        out[planes, D + CY] = out[planes, D + CY - 1] * sign


def first_solve(q, bg, qp, cz, bz, b, y1, y2):
    def whole(x, y, n):
        f, acc = side_fluxes(bg, qp, x, y, n)
        b[x, pl.ds(y, n)] = acc + z_fluxes(f, z_face(qp[x, pl.ds(y, n)]))
        cz[x, pl.ds(y, n)] = z_face(q[x, pl.ds(y, n)])

    def right_own(x):
        whole(x, 1, D - 1)
        whole(x, D + CY, D - 1)
        for y in cover(D, D + CY, 4):
            _, acc = side_fluxes(bg, qp, x, y, 4)
            b[x, pl.ds(y, 4)] = acc + bz[x - D, pl.ds(y - D, 4)]

    def second(x, y, n):
        f, acc = fluxes(b, q, cz, x, y, n)
        y1[x, pl.ds(y, n)] = (A2 - A3) * f - A3 * acc

    def third(x, y, n):
        f, acc = fluxes(y1, q, cz, x, y, n)
        y2[x, pl.ds(y, n)] = A1 * b[x, pl.ds(y, n)] - f - acc

    return lines(1, 4, whole), right_own, lines(2, 4, second), lines(3, 4, third)


def middle_kernel(
    py_low, py_high, after, bz, q_in, bg_in, qp_in, cz_in, q, bg, qp, cz, b, y1, y2
):
    del after, q_in, bg_in, qp_in, cz_in
    own = slice(D, D + CX)
    for field, out, scale, sign in ((0, q, 0.5 / HALF, -1.0), (1, bg, 1.0, 1.0), (2, qp, 0.5, -1.0)):
        put_py(field, py_low, py_high, out, scale)
        close_py(out, sign, own)
    _, right_own, second, third = first_solve(q, bg, qp, cz, bz, b, y1, y2)
    early(1, right_own)
    early(2, second)
    early(3, third)


def close_edges(out, sign):
    px, last_x = lax.axis_index("px"), lax.axis_size("px") - 1

    @pl.when(px == 0)
    def _():
        out[D - 1] = out[D] * sign

    @pl.when(px == last_x)
    def _():
        out[D + CX] = out[D + CX - 1] * sign

    close_py(out, sign, slice(0, EX))


def take_meta(ref, base, out):
    for c in range(8):
        lanes = slice(c * 128, (c + 1) * 128)
        out[0:8, lanes] = ref[base + c * 8 : base + c * 8 + 8, :]
        for i in range(2):
            at = base + 64 + i * 8 + c
            out[8 + i : 9 + i, lanes] = ref[at : at + 1, :]


def two_parts(v):
    high = v.astype(BF16)
    return high, (v - high.astype(F32)).astype(BF16)


def three_parts(v):
    high = v.astype(BF16)
    rest = v - high.astype(F32)
    mid = rest.astype(BF16)
    return high, mid, (rest - mid.astype(F32)).astype(BF16)


def one_hot(index, count):
    at = lax.broadcasted_iota(jnp.int32, (count, index.shape[1]), 0)
    return jnp.where(at == index, 1.0, 0.0).astype(BF16)


def rows16(index):
    shape = (16, index.shape[1])
    numbers = lax.broadcasted_iota(jnp.int32, shape, 0).astype(jnp.int16)
    return jnp.broadcast_to(index, shape).astype(jnp.int16), numbers


def put_one_hot(index, count, out, first, lanes):
    wanted, numbers = rows16(index)
    one, zero = jnp.ones(wanted.shape, BF16), jnp.zeros(wanted.shape, BF16)
    for r in range(count // 16):
        hit = numbers + jnp.int16(r * 16) == wanted
        out[first + r * 16 : first + (r + 1) * 16, lanes] = jnp.where(hit, one, zero)


def dot(a, b, over):
    return lax.dot_general(a, b, (over, ((), ())), preferred_element_type=F32)


def tangent_kernel(
    px_low,
    px_high,
    c_low,
    c_high,
    bz,
    meta,
    hot,
    weights,
    q_in,
    bg_in,
    qp_in,
    cz_in,
    b_in,
    y1_in,
    y2_in,
    out,
    q,
    bg,
    qp,
    cz,
    b,
    y1,
    y2,
    y3,
    table,
    vals,
):
    del q_in, bg_in, qp_in, cz_in, b_in, y1_in, y2_in
    sides = (px_low, px_high, c_low, c_high)
    put_px(0, sides, q, 0.5 / HALF)
    put_px(1, sides, bg, 1.0)
    put_px(2, sides, qp, 0.5)
    far_planes(sides, bg, qp)
    close_edges(q, -1.0)
    close_edges(qp, -1.0)
    close_edges(bg, 1.0)
    right, right_own, second, third = first_solve(q, bg, qp, cz, bz, b, y1, y2)

    def outer_planes(i, carry):
        right(jnp.where(i < D - 1, 1 + i, CX + 1 + i))
        return carry

    def edge_planes(i, carry):
        right_own(D + i * (CX - 1))
        return carry

    lax.fori_loop(0, 2 * (D - 1), outer_planes, 0)
    lax.fori_loop(0, 2, edge_planes, 0)
    late(2, second)
    late(3, third)

    def fourth(x, y, n):
        f, acc = fluxes(y2, q, cz, x, y, n)
        y3[x, pl.ds(y, n)] = A0 * b[x, pl.ds(y, n)] - f - acc

    late(4, lines(4, 4, fourth))

    flat = y3.reshape(EX * EY * 8, 128)
    for x in range(CX):
        for c in range(8):
            v = flat[pl.ds(((x + D) * EY + D) * 8 + c, CY, stride=8), :]
            high, low = two_parts(v)
            table[x * CY : (x + 1) * CY, c * 128 : (c + 1) * 128] = high
            table[CX * CY + x * CY : CX * CY + (x + 1) * CY, c * 128 : (c + 1) * 128] = low

    vals[...] = jnp.zeros_like(vals)
    wide = 512

    def gather(i, carry):
        k, lanes = i // 2, pl.ds(pl.multiple_of((i % 2) * wide, wide), wide)
        node = meta[pl.ds(k, 1), lanes].astype(jnp.int32)
        found = dot(table[...], hot[:, pl.ds(pl.multiple_of(i * wide, wide), wide)], ((1,), (0,)))
        found = found[: CX * CY] + found[CX * CY :]
        at = lax.broadcasted_iota(jnp.int32, found.shape, 0)
        found = jnp.sum(jnp.where(at == node >> 10, found, 0.0), axis=0, keepdims=True)
        vals[0:1, lanes] += meta[pl.ds(k + 4, 1), lanes] * found
        return carry

    lax.fori_loop(0, 8, gather, 0)

    owner, sensor = meta[8:9, :].astype(jnp.int32), meta[9:10, :].astype(jnp.int32)
    at = lax.broadcasted_iota(jnp.int32, (8, 1024), 0)
    owned = jnp.where(at == sensor, vals[0:1, :], 0.0)
    parts = jnp.concatenate(three_parts(owned), axis=0)
    sums = dot(parts, one_hot(owner, 128), ((1,), (1,)))
    readings = sums[0:8] + sums[8:16] + sums[16:24]
    block = jnp.concatenate([readings, weights[...]] * 8, axis=0)
    for i in range(out.shape[0] // 72):
        out[i * 72 : (i + 1) * 72, :] = block


def scatter(meta, values, rows, per, tiles, width, lhs, keep, hot):
    for k in range(4):
        wanted, numbers = rows16(rows(meta[k : k + 1, :].astype(jnp.int32)))
        value = jnp.broadcast_to(values[k : k + 1, :], wanted.shape)
        high, low = two_parts(value)
        zero = jnp.zeros(wanted.shape, BF16)
        lanes = slice(k * 1024, (k + 1) * 1024)
        for r in range(per // 16):
            hit = numbers + jnp.int16(r * 16) == wanted
            lhs[r * 16 : (r + 1) * 16, lanes] = jnp.where(hit, high, zero)
            lhs[per + r * 16 : per + (r + 1) * 16, lanes] = jnp.where(hit, low, zero)

    def tile(t, carry):
        total = None
        for k in range(4):
            lanes = slice(k * 1024, (k + 1) * 1024)
            hits = hot[pl.ds(pl.multiple_of(t * width, width), width), lanes]
            part = dot(lhs[0 : 2 * per, lanes], hits, ((1,), (1,)))
            total = part if total is None else total + part
        keep(t, total[0:per] + total[per : 2 * per])
        return carry

    if tiles == 1:
        tile(0, 0)
    else:
        lax.fori_loop(0, tiles, tile, 0)


def returned(weighted, table, values):
    owner, sensor = table[8:9, :].astype(jnp.int32), table[9:10, :].astype(jnp.int32)
    parts = jnp.concatenate(three_parts(weighted), axis=0)
    found = dot(parts, one_hot(owner, 128), ((1,), (0,)))
    found = found[0:8] + found[8:16] + found[16:24]
    at = lax.broadcasted_iota(jnp.int32, found.shape, 0)
    found = jnp.sum(jnp.where(at == sensor, found, 0.0), axis=0, keepdims=True)
    values[0:4, :] = table[4:8, :] * found


def source_kernel(got, meta, hot, weighted, own, low, high, lhs, values):
    count = got.shape[0] // 9
    sums = [jnp.sum(got[pl.ds(i, count, stride=9), :], axis=0, keepdims=True) for i in range(8)]
    readings = jnp.concatenate(sums, axis=0)
    weights = jnp.transpose(got[pl.ds(8, count, stride=9), :])[0:8]
    weighted[...] = readings * weights

    def keep(t, sums):
        for x in range(CX):
            for i in range(4):
                block = sums[x * CY : (x + 1) * CY, i * 128 : (i + 1) * 128]
                own[pl.ds(x * PLANE + t * 4 + i, CY, stride=8), :] = block
                side, at = (low, x) if x < D else (high, x - (CX - D))
                side[pl.ds(at * PLANE + t * 4 + i, CY, stride=8), :] = block

    returned(weighted[...], meta, values)
    scatter(meta, values, lambda n: n >> 10, CX * CY, 2, 512, lhs, keep, hot)


def second_solve(src, q, cz, y1, y2, y3):
    def first(x, y, n):
        f, acc = fluxes(src, q, cz, x, y, n)
        y1[x, pl.ds(y, n)] = (A2 - A3) * f - A3 * acc

    def second(x, y, n):
        f, acc = fluxes(y1, q, cz, x, y, n)
        y2[x, pl.ds(y, n)] = A1 * src[x, pl.ds(y, n)] - f - acc

    def third(x, y, n):
        f, acc = fluxes(y2, q, cz, x, y, n)
        y3[x, pl.ds(y, n)] = A0 * src[x, pl.ds(y, n)] - f - acc

    return lines(1, 4, first), lines(2, 4, second), lines(3, 4, third)


def strips_kernel(
    weighted,
    py_low,
    py_high,
    c_low,
    c_high,
    own,
    q,
    cz,
    src,
    y1,
    y2,
    y3,
    lhs,
    near_hot,
    near,
    values,
):
    src[D : D + CX, D : D + CY] = own[...].reshape(CX, CY, 8, 128)
    flat = src.reshape(EX * EY * 8, 128)

    def box(first_x, planes, first_y):
        def rows(node):
            x, y = (node >> 15) - first_x, ((node >> 10) & (CY - 1)) - first_y
            good = (x >= 0) & (x < planes) & (y >= 0) & (y < D)
            return jnp.where(good, (((node >> 8) & 3) * planes + x) * D + y, -1)

        return rows

    low_x, high_x, low_y, high_y = CX - D, 0, CY - D, 0
    tasks = [
        (py_low, 3 * HALO_Y, D, 0, CX, low_y, 0),
        (py_high, 3 * HALO_Y, D, 0, CX, high_y, D + CY),
    ]
    for ref, x0, first_x in ((c_low, 0, low_x), (c_high, D + CX, high_x)):
        for side, (y0, first_y) in enumerate(((0, low_y), (D + CY, high_y))):
            tasks.append((ref, side * PART + 3 * HALO_C, x0, first_x, D, first_y, y0))
    for ref, base, x0, first_x, planes, first_y, y0 in tasks:
        take_meta(ref, base, near)
        returned(weighted[...], near, values)
        for k in range(4):
            node = near[k : k + 1, :].astype(jnp.int32)
            put_one_hot(node & 255, 256, near_hot, 0, slice(k * 1024, (k + 1) * 1024))

        def keep(t, sums, planes=planes, x0=x0, y0=y0):
            for zq in range(4):
                for x in range(planes):
                    first = (zq * planes + x) * D
                    for half in range(2):
                        flat[
                            pl.ds(((x + x0) * EY + y0) * 8 + zq * 2 + half, D, stride=8), :
                        ] = sums[first : first + D, half * 128 : (half + 1) * 128]

        rows = box(first_x, planes, first_y)
        scatter(near, values, rows, 4 * planes * D, 1, 256, lhs, keep, near_hot)

    first, second, third = second_solve(src, q, cz, y1, y2, y3)
    early(1, first)
    early(2, second)
    early(3, third)


def adjoint_kernel(
    px_low, px_high, q, bg, cz, src_in, y1_in, y2_in, y3_in, out, src, y1, y2, y3
):
    del src_in, y1_in, y2_in, y3_in
    for x, ref in ((0, px_low), (D + CX, px_high)):
        src[x : x + D, D : D + CY] = ref[...].reshape(D, CY, 8, 128)
    first, second, third = second_solve(src, q, cz, y1, y2, y3)
    late(1, first)
    late(2, second)
    late(3, third)

    def last(x, y, n):
        ae, be = y3[x, pl.ds(y - 1, n + 2)], bg[x, pl.ds(y - 1, n + 2)]
        a, k = ae[1:-1], be[1:-1]
        sy = (ae[1:] - ae[:-1]) * (be[1:] - be[:-1])
        total = sy[1:] + sy[:-1]
        total += (y3[x + 1, pl.ds(y, n)] - a) * (bg[x + 1, pl.ds(y, n)] - k)
        total += (y3[x - 1, pl.ds(y, n)] - a) * (bg[x - 1, pl.ds(y, n)] - k)
        sub = lax.broadcasted_iota(jnp.int32, (n, 8, 128), 1)
        end = (sub == 7) & (lane_of(n) == 127)
        sz = jnp.where(end, 0.0, (z_up(a) - a) * (z_up(k) - k))
        total = -0.5 * (total + (sz + z_down(sz)))
        yy = y - D
        for i in range(n):
            row = (x - D) * (CY // 8) + (yy + i) // 8
            out[pl.ds(row * 64 + (yy + i) % 8, 8, stride=8), :] = total[i]

    late(4, lines(4, 4, last))


def by_tiles(block):
    lead = block.shape[:-2]
    rows, cols = block.shape[-2:]
    split = block.reshape(*lead, rows // 8, 8, cols // 128, 128)
    return jnp.swapaxes(split, -3, -2).reshape(-1, 128)


def from_tiles(rows):
    split = rows.reshape(CX, CY // 8, CZ // 128, 8, 128)
    return jnp.swapaxes(split, -3, -2).reshape(CX, CY, CZ)


def row_of(ref, x, y):
    return ref[pl.ds((x * (CY // 8) + y // 8) * 64 + y % 8, 8, stride=8), :]


def line_of(ref, x, y):
    return ref[pl.ds((x * (CY // 8) + y // 8) * 64 + y % 8, 8, stride=8), :]


def pack_kernel(
    permit_hbm,
    back_hbm,
    perturb_hbm,
    nodes_hbm,
    weights_hbm,
    owner_hbm,
    sensor_hbm,
    low_x,
    high_x,
    low_y,
    high_y,
    meta,
    permit,
    back,
    perturb,
    nodes,
    weights,
    owner,
    sensor,
    sems,
):
    pairs = (
        (nodes_hbm, nodes),
        (weights_hbm, weights),
        (owner_hbm, owner),
        (sensor_hbm, sensor),
        (permit_hbm, permit),
        (back_hbm, back),
        (perturb_hbm, perturb),
    )
    copies = [pltpu.make_async_copy(a, b, sems.at[i]) for i, (a, b) in enumerate(pairs)]
    for copy in copies:
        copy.start()
    for copy in copies[:4]:
        copy.wait()
    meta[0:4, :] = nodes[...].astype(F32)
    meta[4:8, :] = weights[...]
    meta[8:9, :] = owner[...].astype(F32)
    meta[9:10, :] = sensor[...].astype(F32)
    meta[10:16, :] = jnp.zeros((6, 1024), F32)
    for out, at in ((low_y, 3 * HALO_Y), (high_y, 3 * HALO_Y)):
        for c in range(8):
            lanes = slice(c * 128, (c + 1) * 128)
            out[at + c * 8 : at + c * 8 + 8, :] = meta[0:8, lanes]
            for i in range(2):
                out[at + 64 + i * 8 + c : at + 65 + i * 8 + c, :] = meta[8 + i : 9 + i, lanes]

    for field, ref in enumerate((permit, back, perturb)):
        copies[4 + field].wait()
        planes = D if field == 0 else D - 1

        def plane(x, carry, field=field, ref=ref, planes=planes):
            for y in range(CY):
                at = pl.ds(PX_AT[field] + (x * CY + y) * 8, 8)
                low_x[at, :] = row_of(ref, x, y)
                high_x[at, :] = row_of(ref, x + CX - planes, y)
            return carry

        lax.fori_loop(0, planes, plane, 0)
        for x in range(CX):
            for y in range(D):
                at = pl.ds(field * HALO_Y + (x * D + y) * 8, 8)
                low_y[at, :] = row_of(ref, x, y)
                high_y[at, :] = row_of(ref, x, y + CY - D)

    def flux(y, carry):
        for out, near, far in ((low_x, D - 2, D - 1), (high_x, CX - D + 1, CX - D)):
            face = 0.5 * (line_of(perturb, near, y) + line_of(perturb, far, y))
            at = pl.ds(pl.multiple_of(PX_FLUX + y * 8, 8), 8)
            out[at, :] = face * (line_of(back, far, y) - line_of(back, near, y))
        return carry

    lax.fori_loop(0, CY, flux, 0)


def own_kernel(
    permit_hbm,
    back_hbm,
    perturb_hbm,
    meta,
    q,
    bg,
    qp,
    cz,
    bz,
    hot,
    permit,
    back,
    perturb,
    sems,
):
    pairs = ((permit_hbm, permit), (back_hbm, back), (perturb_hbm, perturb))
    copies = [pltpu.make_async_copy(a, b, sems.at[i]) for i, (a, b) in enumerate(pairs)]
    for copy in copies:
        copy.start()

    def entries(i, carry):
        k, lanes = i // 2, pl.ds(pl.multiple_of((i % 2) * 512, 512), 512)
        node = meta[pl.ds(k, 1), lanes].astype(jnp.int32)
        at = pl.ds(pl.multiple_of(i * 512, 512), 512)
        put_one_hot(node & (CZ - 1), CZ, hot, 0, at)
        return carry

    lax.fori_loop(0, 8, entries, 0)
    for copy in copies:
        copy.wait()

    def plane(x, carry):
        for y in range(CY):
            q[x + D, y + D] = row_of(permit, x, y) * (0.5 / HALF)
            bg[x + D, y + D] = row_of(back, x, y)
            qp[x + D, y + D] = row_of(perturb, x, y) * 0.5
        for y in range(0, CY, 4):
            at = pl.ds(y + D, 4)
            cz[x + D, at] = z_face(q[x + D, at])
            bz[x, pl.ds(y, 4)] = z_fluxes(bg[x + D, at], z_face(qp[x + D, at]))
        return carry

    lax.fori_loop(0, CX, plane, 0)


def corner_kernel(py_low, py_high, after, low, high):
    del after
    for side, ref in enumerate((py_low, py_high)):
        for field in range(3):
            for i, (dx, dy) in enumerate(CELLS):
                y = D - dy if side == 0 else dy - 1
                at = side * PART + field * HALO_C + i * 8
                for out, x in ((low, dx - 1), (high, CX - dx)):
                    first = field * HALO_Y + (x * D + y) * 8
                    out[at : at + 8, :] = ref[first : first + 8, :]
        at = side * PART + 3 * HALO_C
        low[at : at + META, :] = ref[3 * HALO_Y :, :]
        high[at : at + META, :] = ref[3 * HALO_Y :, :]


def vmem(count):
    return [pl.BlockSpec(memory_space=pltpu.VMEM)] * count


def shift(x, axis, by):
    count = lax.axis_size(axis)
    return lax.ppermute(x, axis, [(i, (i + by) % count) for i in range(count)])


def body(
    background_field,
    perturbation,
    permittivity,
    probe_nodes,
    probe_weights,
    probe_owner,
    probe_sensor,
    sensor_weight,
):
    devices = lax.axis_size("px") * lax.axis_size("py")
    fields = [by_tiles(f) for f in (permittivity, background_field, perturbation)]
    weights = jnp.pad(sensor_weight, (0, 128 - sensor_weight.shape[0]))[None, :]

    def rows(*counts):
        return [jax.ShapeDtypeStruct((n, 128), F32) for n in counts]

    def call(kernel, outs, *args, hbm=0, passed=0, at=1, scratch=(), limit, bytes_accessed=0):
        held = [pltpu.with_memory_space_constraint(a, pltpu.HBM) for a in args[:hbm]]
        args = held + list(args[hbm:])
        return pl.pallas_call(
            kernel,
            out_shape=tuple(outs),
            in_specs=[pl.BlockSpec(memory_space=pltpu.HBM)] * hbm + vmem(len(args) - hbm),
            out_specs=tuple(vmem(len(outs))),
            scratch_shapes=scratch,
            input_output_aliases={len(args) - passed + i: at + i for i in range(passed)},
            compiler_params=pltpu.CompilerParams(vmem_limit_bytes=limit * 2**20),
            cost_estimate=pl.CostEstimate(
                flops=0, bytes_accessed=bytes_accessed, transcendentals=0
            ),
        )(*args)

    size_x, size_y, size_c = PX_ROWS, 3 * HALO_Y + META, 2 * PART
    raw = [pltpu.VMEM((ROWS, 128), F32)] * 3
    table = jax.ShapeDtypeStruct((16, 1024), F32)
    low_x, high_x, low_y, high_y, meta = call(
        pack_kernel,
        rows(size_x, size_x, size_y, size_y) + [table],
        *fields,
        probe_nodes,
        probe_weights,
        probe_owner.reshape(1, -1),
        probe_sensor.reshape(1, -1),
        hbm=7,
        scratch=raw
        + [
            pltpu.VMEM((4, 1024), jnp.int32),
            pltpu.VMEM((4, 1024), F32),
            pltpu.VMEM((1, 1024), jnp.int32),
            pltpu.VMEM((1, 1024), jnp.int32),
            pltpu.SemaphoreType.DMA((7,)),
        ],
        limit=6,
    )
    px_low, px_high = shift(high_x, "px", 1), shift(low_x, "px", -1)
    py_low, py_high = shift(high_y, "py", 1), shift(low_y, "py", -1)
    compact = jax.ShapeDtypeStruct((CX, CY, 8, 128), F32)
    full = jax.ShapeDtypeStruct((EX, EY, 8, 128), F32)
    q, bg, qp, cz, bz, hot = call(
        own_kernel,
        [full] * 4 + [compact, jax.ShapeDtypeStruct((CZ, 4096), BF16)],
        *fields,
        meta,
        hbm=3,
        scratch=raw + [pltpu.SemaphoreType.DMA((3,))],
        limit=10,
        bytes_accessed=8 * 2**20,
    )
    low_c, high_c = call(corner_kernel, rows(size_c, size_c), py_low, py_high, bz, limit=4)
    c_low, c_high = shift(high_c, "px", 1), shift(low_c, "px", -1)
    q, bg, qp, cz, b, y1, y2 = call(
        middle_kernel,
        [full] * 7,
        py_low,
        py_high,
        low_c,
        bz,
        q,
        bg,
        qp,
        cz,
        passed=4,
        at=0,
        limit=6,
        bytes_accessed=8 * 2**20,
    )
    block = pltpu.VMEM((EX, EY, 8, 128), F32)
    readings, q, bg, qp, cz, b, y1, y2 = call(
        tangent_kernel,
        rows(devices * 9) + [full] * 7,
        px_low,
        px_high,
        c_low,
        c_high,
        bz,
        meta,
        hot,
        weights,
        q,
        bg,
        qp,
        cz,
        b,
        y1,
        y2,
        passed=7,
        scratch=[block, pltpu.VMEM((2 * CX * CY, CZ), BF16), pltpu.VMEM((8, 1024), F32)],
        limit=14,
    )
    got = lax.all_to_all(
        readings.reshape(devices, 1, 9 * 128),
        ("px", "py"),
        split_axis=0,
        concat_axis=0,
        tiled=True,
    ).reshape(devices * 9, 128)
    weighted, own_source, low_s, high_s = call(
        source_kernel,
        rows(8, ROWS, D * PLANE, D * PLANE),
        got,
        meta,
        hot,
        scratch=[pltpu.VMEM((2 * CX * CY, 4096), BF16), pltpu.VMEM((8, 1024), F32)],
        limit=18,
    )
    source_low, source_high = shift(high_s, "px", 1), shift(low_s, "px", -1)
    src, y1, y2, y3 = call(
        strips_kernel,
        [full] * 4,
        weighted,
        py_low,
        py_high,
        c_low,
        c_high,
        own_source,
        q,
        cz,
        scratch=[
            pltpu.VMEM((2 * 4 * CX * D, 4096), BF16),
            pltpu.VMEM((256, 4096), BF16),
            pltpu.VMEM((16, 1024), F32),
            pltpu.VMEM((8, 1024), F32),
        ],
        limit=16,
        bytes_accessed=24 * 2**20,
    )
    result = call(
        adjoint_kernel,
        rows(ROWS) + [full] * 4,
        source_low,
        source_high,
        q,
        bg,
        cz,
        src,
        y1,
        y2,
        y3,
        passed=4,
        limit=8,
    )[0]
    return from_tiles(result)


def solution(mesh):
    placed = (
        P("px", "py", None),
        P("px", "py", None),
        P("px", "py", None),
        P(None, ("px", "py")),
        P(None, ("px", "py")),
        P(("px", "py"), None),
        P(("px", "py")),
        P(("px", "py")),
    )
    return jax.shard_map(
        body, mesh=mesh, in_specs=placed, out_specs=P("px", "py", None), check_vma=False
    )
```

```python
import jax
import jax.numpy as jnp
import numpy as np
from jax import lax
from jax.experimental import pallas as pl
from jax.experimental.pallas import tpu as pltpu
from jax.sharding import PartitionSpec as P

SWEEPS = 4
MASS = 1.0
LOW = 1.0
HIGH = 25.0
CENTRE = 0.5 * (HIGH + LOW)
HALF = 0.5 * (HIGH - LOW)

CX, CY, CZ = 8, 32, 1024
D = 4
EX, EY = CX + 2 * D, CY + 2 * D
ROWS = CX * CY * 8
PLANE = CY * 8
PX_AT = (0, D * PLANE, (2 * D - 1) * PLANE)
PX_FLUX = (3 * D - 2) * PLANE
PX_ROWS = (3 * D - 1) * PLANE
HALO_Y = CX * D * 8
CELLS = tuple((dx, dy) for dx in range(1, D) for dy in range(1, D) if dx + dy <= D)
HALO_C = len(CELLS) * 8
META = 80
PART = 3 * HALO_C + META
AHEAD_META = 6 * HALO_C
AHEAD = AHEAD_META + META
F32 = jnp.float32
BF16 = jnp.bfloat16


def horner_terms():
    spread = CENTRE / HALF
    size = SWEEPS
    iterate = np.zeros(size)
    remain = np.eye(size)[0]
    search = remain / CENTRE
    ratio = 1.0 / spread
    for sweep in range(SWEEPS):
        iterate = iterate + search
        if sweep < SWEEPS - 1:
            shifted = np.concatenate([[0.0], search[:-1]])
            remain = remain - (CENTRE * search + HALF * shifted)
            following = 1.0 / (2.0 * spread - ratio)
            search = following * ratio * search + 2.0 * following / HALF * remain
            ratio = following
    return [float(v) for v in iterate]


A0, A1, A2, A3 = horner_terms()


def lane_of(n):
    return lax.broadcasted_iota(jnp.int32, (n, 8, 128), 2)


def z_up(f):
    r = pltpu.roll(f, 127, 2)
    return jnp.where(lane_of(f.shape[0]) == 127, pltpu.roll(r, 7, 1), r)


def z_down(f):
    r = pltpu.roll(f, 1, 2)
    return jnp.where(lane_of(f.shape[0]) == 0, pltpu.roll(r, 1, 1), r)


def z_face(q):
    n = q.shape[0]
    sub = lax.broadcasted_iota(jnp.int32, (n, 8, 128), 1)
    last = (sub == 7) & (lane_of(n) == 127)
    return jnp.where(last, 0.0, q + z_up(q))


def side_fluxes(src, q, x, y, n):
    fe, qe = src[x, pl.ds(y - 1, n + 2)], q[x, pl.ds(y - 1, n + 2)]
    f, qc = fe[1:-1], qe[1:-1]
    fy = (fe[1:] - fe[:-1]) * (qe[1:] + qe[:-1])
    acc = fy[1:] - fy[:-1]
    acc += (src[x + 1, pl.ds(y, n)] - f) * (q[x + 1, pl.ds(y, n)] + qc)
    acc += (src[x - 1, pl.ds(y, n)] - f) * (q[x - 1, pl.ds(y, n)] + qc)
    return f, acc


def z_fluxes(f, faces):
    fz = (z_up(f) - f) * faces
    return fz - z_down(fz)


def fluxes(src, q, cz, x, y, n):
    f, acc = side_fluxes(src, q, x, y, n)
    return f, acc + z_fluxes(f, cz[x, pl.ds(y, n)])


def cover(low, high, n):
    starts = list(range(low, high - n + 1, n))
    if starts[-1] + n < high:
        starts.append(high - n)
    return starts


def early(margin, plane):
    def step(x, carry):
        plane(x)
        return carry

    lax.fori_loop(margin + D, EX - D - margin, step, 0)


def late(margin, plane):
    def step(i, carry):
        plane(jnp.where(i < D, margin + i, EX - 2 * D - margin + i))
        return carry

    lax.fori_loop(0, 2 * D, step, 0)


def lines(margin, n, step):
    def plane(x):
        for y in cover(margin, EY - margin, n):
            step(x, y, n)

    return plane


def put_py(field, py_low, py_high, out, scale):
    for ref, at in ((py_low, 0), (py_high, D + CY)):
        v = ref[field * HALO_Y : (field + 1) * HALO_Y, :]
        out[D : D + CX, at : at + D] = v.reshape(CX, D, 8, 128) * scale


def put_px(field, sides, out, scale):
    px_low, px_high, c_low, c_high = sides
    middle_y = slice(D, D + CY)
    planes = D if field == 0 else D - 1
    for ref, at in ((px_low, D - planes), (px_high, D + CX)):
        v = ref[PX_AT[field] : PX_AT[field] + planes * PLANE, :]
        out[at : at + planes, middle_y] = v.reshape(planes, CY, 8, 128) * scale
    blank = jnp.zeros((D, D, 8, 128), F32)
    for x, ref in ((0, c_low), (D + CX, c_high)):
        for side, y in enumerate((0, D + CY)):
            out[x : x + D, y : y + D] = blank
            for i, (dx, dy) in enumerate(CELLS):
                at = side * PART + field * HALO_C + i * 8
                cell_x = x + D - dx if x == 0 else x + dx - 1
                cell_y = y + D - dy if y == 0 else y + dy - 1
                out[cell_x, cell_y] = ref[at : at + 8, :] * scale


def far_planes(sides, bg, qp):
    middle_y = slice(D, D + CY)
    for ref, at, beside in ((sides[0], 0, 1), (sides[1], EX - 1, EX - 2)):
        flux = ref[PX_FLUX : PX_FLUX + PLANE, :].reshape(CY, 8, 128)
        bg[at, middle_y] = bg[beside, middle_y] + flux
        qp[at, middle_y] = 1.0 - qp[beside, middle_y]


def close_py(out, sign, planes):
    py, last_y = lax.axis_index("py"), lax.axis_size("py") - 1

    @pl.when(py == 0)
    def _():
        out[planes, D - 1] = out[planes, D] * sign

    @pl.when(py == last_y)
    def _():
        out[planes, D + CY] = out[planes, D + CY - 1] * sign


def first_solve(q, bg, qp, cz, bz, b, y1, y2):
    def whole(x, y, n):
        f, acc = side_fluxes(bg, qp, x, y, n)
        b[x, pl.ds(y, n)] = acc + z_fluxes(f, z_face(qp[x, pl.ds(y, n)]))
        cz[x, pl.ds(y, n)] = z_face(q[x, pl.ds(y, n)])

    def right_own(x):
        whole(x, 1, D - 1)
        whole(x, D + CY, D - 1)
        for y in cover(D, D + CY, 4):
            _, acc = side_fluxes(bg, qp, x, y, 4)
            b[x, pl.ds(y, 4)] = acc + bz[x - D, pl.ds(y - D, 4)]

    def second(x, y, n):
        f, acc = fluxes(b, q, cz, x, y, n)
        y1[x, pl.ds(y, n)] = (A2 - A3) * f - A3 * acc

    def third(x, y, n):
        f, acc = fluxes(y1, q, cz, x, y, n)
        y2[x, pl.ds(y, n)] = A1 * b[x, pl.ds(y, n)] - f - acc

    return lines(1, 4, whole), right_own, lines(2, 4, second), lines(3, 4, third)


def middle_kernel(
    py_low, py_high, after, bz, q_in, bg_in, qp_in, cz_in, q, bg, qp, cz, b, y1, y2
):
    del after, q_in, bg_in, qp_in, cz_in
    own = slice(D, D + CX)
    for field, out, scale, sign in ((0, q, 0.5 / HALF, -1.0), (1, bg, 1.0, 1.0), (2, qp, 0.5, -1.0)):
        put_py(field, py_low, py_high, out, scale)
        close_py(out, sign, own)
    _, right_own, second, third = first_solve(q, bg, qp, cz, bz, b, y1, y2)
    early(1, right_own)
    early(2, second)
    early(3, third)


def close_edges(out, sign):
    px, last_x = lax.axis_index("px"), lax.axis_size("px") - 1

    @pl.when(px == 0)
    def _():
        out[D - 1] = out[D] * sign

    @pl.when(px == last_x)
    def _():
        out[D + CX] = out[D + CX - 1] * sign

    close_py(out, sign, slice(0, EX))


def take_meta(ref, base, out):
    for c in range(8):
        lanes = slice(c * 128, (c + 1) * 128)
        out[0:8, lanes] = ref[base + c * 8 : base + c * 8 + 8, :]
        for i in range(2):
            at = base + 64 + i * 8 + c
            out[8 + i : 9 + i, lanes] = ref[at : at + 1, :]


def two_parts(v):
    high = v.astype(BF16)
    return high, (v - high.astype(F32)).astype(BF16)


def three_parts(v):
    high = v.astype(BF16)
    rest = v - high.astype(F32)
    mid = rest.astype(BF16)
    return high, mid, (rest - mid.astype(F32)).astype(BF16)


def one_hot(index, count):
    at = lax.broadcasted_iota(jnp.int32, (count, index.shape[1]), 0)
    return jnp.where(at == index, 1.0, 0.0).astype(BF16)


def rows16(index):
    shape = (16, index.shape[1])
    numbers = lax.broadcasted_iota(jnp.int32, shape, 0).astype(jnp.int16)
    return jnp.broadcast_to(index, shape).astype(jnp.int16), numbers


def put_one_hot(index, count, out, first, lanes):
    wanted, numbers = rows16(index)
    one, zero = jnp.ones(wanted.shape, BF16), jnp.zeros(wanted.shape, BF16)
    for r in range(count // 16):
        hit = numbers + jnp.int16(r * 16) == wanted
        out[first + r * 16 : first + (r + 1) * 16, lanes] = jnp.where(hit, one, zero)


def dot(a, b, over):
    return lax.dot_general(a, b, (over, ((), ())), preferred_element_type=F32)


def tangent_kernel(
    px_low,
    px_high,
    c_low,
    c_high,
    bz,
    meta,
    hot,
    weights,
    q_in,
    bg_in,
    qp_in,
    cz_in,
    b_in,
    y1_in,
    y2_in,
    out,
    q,
    bg,
    qp,
    cz,
    b,
    y1,
    y2,
    y3,
    table,
    vals,
):
    del q_in, bg_in, qp_in, cz_in, b_in, y1_in, y2_in
    sides = (px_low, px_high, c_low, c_high)
    put_px(0, sides, q, 0.5 / HALF)
    put_px(1, sides, bg, 1.0)
    put_px(2, sides, qp, 0.5)
    far_planes(sides, bg, qp)
    close_edges(q, -1.0)
    close_edges(qp, -1.0)
    close_edges(bg, 1.0)
    right, right_own, second, third = first_solve(q, bg, qp, cz, bz, b, y1, y2)

    def outer_planes(i, carry):
        right(jnp.where(i < D - 1, 1 + i, CX + 1 + i))
        return carry

    def edge_planes(i, carry):
        right_own(D + i * (CX - 1))
        return carry

    lax.fori_loop(0, 2 * (D - 1), outer_planes, 0)
    lax.fori_loop(0, 2, edge_planes, 0)
    late(2, second)
    late(3, third)

    def fourth(x, y, n):
        f, acc = fluxes(y2, q, cz, x, y, n)
        y3[x, pl.ds(y, n)] = A0 * b[x, pl.ds(y, n)] - f - acc

    late(4, lines(4, 4, fourth))

    flat = y3.reshape(EX * EY * 8, 128)
    for x in range(CX):
        for c in range(8):
            v = flat[pl.ds(((x + D) * EY + D) * 8 + c, CY, stride=8), :]
            high, low = two_parts(v)
            table[x * CY : (x + 1) * CY, c * 128 : (c + 1) * 128] = high
            table[CX * CY + x * CY : CX * CY + (x + 1) * CY, c * 128 : (c + 1) * 128] = low

    vals[...] = jnp.zeros_like(vals)
    wide = 512

    def gather(i, carry):
        k, lanes = i // 2, pl.ds(pl.multiple_of((i % 2) * wide, wide), wide)
        node = meta[pl.ds(k, 1), lanes].astype(jnp.int32)
        found = dot(table[...], hot[:, pl.ds(pl.multiple_of(i * wide, wide), wide)], ((1,), (0,)))
        found = found[: CX * CY] + found[CX * CY :]
        at = lax.broadcasted_iota(jnp.int32, found.shape, 0)
        found = jnp.sum(jnp.where(at == node >> 10, found, 0.0), axis=0, keepdims=True)
        vals[0:1, lanes] += meta[pl.ds(k + 4, 1), lanes] * found
        return carry

    lax.fori_loop(0, 8, gather, 0)

    owner, sensor = meta[8:9, :].astype(jnp.int32), meta[9:10, :].astype(jnp.int32)
    at = lax.broadcasted_iota(jnp.int32, (8, 1024), 0)
    owned = jnp.where(at == sensor, vals[0:1, :], 0.0)
    parts = jnp.concatenate(three_parts(owned), axis=0)
    sums = dot(parts, one_hot(owner, 128), ((1,), (1,)))
    readings = sums[0:8] + sums[8:16] + sums[16:24]
    block = jnp.concatenate([readings, weights[...]] * 8, axis=0)
    for i in range(out.shape[0] // 72):
        out[i * 72 : (i + 1) * 72, :] = block


def scatter(meta, values, rows, per, tiles, width, lhs, keep, hot):
    for k in range(4):
        wanted, numbers = rows16(rows(meta[k : k + 1, :].astype(jnp.int32)))
        value = jnp.broadcast_to(values[k : k + 1, :], wanted.shape)
        high, low = two_parts(value)
        zero = jnp.zeros(wanted.shape, BF16)
        lanes = slice(k * 1024, (k + 1) * 1024)
        for r in range(per // 16):
            hit = numbers + jnp.int16(r * 16) == wanted
            lhs[r * 16 : (r + 1) * 16, lanes] = jnp.where(hit, high, zero)
            lhs[per + r * 16 : per + (r + 1) * 16, lanes] = jnp.where(hit, low, zero)

    def tile(t, carry):
        total = None
        for k in range(4):
            lanes = slice(k * 1024, (k + 1) * 1024)
            hits = hot[pl.ds(pl.multiple_of(t * width, width), width), lanes]
            part = dot(lhs[0 : 2 * per, lanes], hits, ((1,), (1,)))
            total = part if total is None else total + part
        keep(t, total[0:per] + total[per : 2 * per])
        return carry

    if tiles == 1:
        tile(0, 0)
    else:
        lax.fori_loop(0, tiles, tile, 0)


def returned(weighted, table, values):
    owner, sensor = table[8:9, :].astype(jnp.int32), table[9:10, :].astype(jnp.int32)
    parts = jnp.concatenate(three_parts(weighted), axis=0)
    found = dot(parts, one_hot(owner, 128), ((1,), (0,)))
    found = found[0:8] + found[8:16] + found[16:24]
    at = lax.broadcasted_iota(jnp.int32, found.shape, 0)
    found = jnp.sum(jnp.where(at == sensor, found, 0.0), axis=0, keepdims=True)
    values[0:4, :] = table[4:8, :] * found


def source_kernel(got, meta, hot, weighted, own, low, high, lhs, values):
    count = got.shape[0] // 9
    sums = [jnp.sum(got[pl.ds(i, count, stride=9), :], axis=0, keepdims=True) for i in range(8)]
    readings = jnp.concatenate(sums, axis=0)
    weights = jnp.transpose(got[pl.ds(8, count, stride=9), :])[0:8]
    weighted[...] = readings * weights

    def keep(t, sums):
        for x in range(CX):
            for i in range(4):
                block = sums[x * CY : (x + 1) * CY, i * 128 : (i + 1) * 128]
                own[pl.ds(x * PLANE + t * 4 + i, CY, stride=8), :] = block
                side, at = (low, x) if x < D else (high, x - (CX - D))
                side[pl.ds(at * PLANE + t * 4 + i, CY, stride=8), :] = block

    returned(weighted[...], meta, values)
    scatter(meta, values, lambda n: n >> 10, CX * CY, 2, 512, lhs, keep, hot)


def second_solve(src, q, cz, y1, y2, y3):
    def first(x, y, n):
        f, acc = fluxes(src, q, cz, x, y, n)
        y1[x, pl.ds(y, n)] = (A2 - A3) * f - A3 * acc

    def second(x, y, n):
        f, acc = fluxes(y1, q, cz, x, y, n)
        y2[x, pl.ds(y, n)] = A1 * src[x, pl.ds(y, n)] - f - acc

    def third(x, y, n):
        f, acc = fluxes(y2, q, cz, x, y, n)
        y3[x, pl.ds(y, n)] = A0 * src[x, pl.ds(y, n)] - f - acc

    return lines(1, 4, first), lines(2, 4, second), lines(3, 4, third)


def strips_kernel(
    weighted,
    a_low,
    a_high,
    c_low,
    c_high,
    own,
    q,
    cz,
    src,
    y1,
    y2,
    y3,
    lhs,
    near_hot,
    near,
    values,
):
    src[D : D + CX, D : D + CY] = own[...].reshape(CX, CY, 8, 128)
    flat = src.reshape(EX * EY * 8, 128)

    def box(first_x, planes, first_y):
        def rows(node):
            x, y = (node >> 15) - first_x, ((node >> 10) & (CY - 1)) - first_y
            good = (x >= 0) & (x < planes) & (y >= 0) & (y < D)
            return jnp.where(good, (((node >> 8) & 3) * planes + x) * D + y, -1)

        return rows

    low_x, high_x, low_y, high_y = CX - D, 0, CY - D, 0
    tasks = [
        (a_low, AHEAD_META, D, 0, CX, low_y, 0),
        (a_high, AHEAD_META, D, 0, CX, high_y, D + CY),
    ]
    for ref, x0, first_x in ((c_low, 0, low_x), (c_high, D + CX, high_x)):
        for side, (y0, first_y) in enumerate(((0, low_y), (D + CY, high_y))):
            tasks.append((ref, side * PART + 3 * HALO_C, x0, first_x, D, first_y, y0))
    for ref, base, x0, first_x, planes, first_y, y0 in tasks:
        take_meta(ref, base, near)
        returned(weighted[...], near, values)
        for k in range(4):
            node = near[k : k + 1, :].astype(jnp.int32)
            put_one_hot(node & 255, 256, near_hot, 0, slice(k * 1024, (k + 1) * 1024))

        def keep(t, sums, planes=planes, x0=x0, y0=y0):
            for zq in range(4):
                for x in range(planes):
                    first = (zq * planes + x) * D
                    for half in range(2):
                        flat[
                            pl.ds(((x + x0) * EY + y0) * 8 + zq * 2 + half, D, stride=8), :
                        ] = sums[first : first + D, half * 128 : (half + 1) * 128]

        rows = box(first_x, planes, first_y)
        scatter(near, values, rows, 4 * planes * D, 1, 256, lhs, keep, near_hot)

    first, second, third = second_solve(src, q, cz, y1, y2, y3)
    early(1, first)
    early(2, second)
    early(3, third)


def adjoint_kernel(
    px_low, px_high, q, bg, cz, src_in, y1_in, y2_in, y3_in, out, src, y1, y2, y3
):
    del src_in, y1_in, y2_in, y3_in
    for x, ref in ((0, px_low), (D + CX, px_high)):
        src[x : x + D, D : D + CY] = ref[...].reshape(D, CY, 8, 128)
    first, second, third = second_solve(src, q, cz, y1, y2, y3)
    late(1, first)
    late(2, second)
    late(3, third)

    def last(x, y, n):
        ae, be = y3[x, pl.ds(y - 1, n + 2)], bg[x, pl.ds(y - 1, n + 2)]
        a, k = ae[1:-1], be[1:-1]
        sy = (ae[1:] - ae[:-1]) * (be[1:] - be[:-1])
        total = sy[1:] + sy[:-1]
        total += (y3[x + 1, pl.ds(y, n)] - a) * (bg[x + 1, pl.ds(y, n)] - k)
        total += (y3[x - 1, pl.ds(y, n)] - a) * (bg[x - 1, pl.ds(y, n)] - k)
        sub = lax.broadcasted_iota(jnp.int32, (n, 8, 128), 1)
        end = (sub == 7) & (lane_of(n) == 127)
        sz = jnp.where(end, 0.0, (z_up(a) - a) * (z_up(k) - k))
        total = -0.5 * (total + (sz + z_down(sz)))
        yy = y - D
        for i in range(n):
            row = (x - D) * (CY // 8) + (yy + i) // 8
            out[pl.ds(row * 64 + (yy + i) % 8, 8, stride=8), :] = total[i]

    late(4, lines(4, 4, last))


def by_tiles(block):
    lead = block.shape[:-2]
    rows, cols = block.shape[-2:]
    split = block.reshape(*lead, rows // 8, 8, cols // 128, 128)
    return jnp.swapaxes(split, -3, -2).reshape(-1, 128)


def from_tiles(rows):
    split = rows.reshape(CX, CY // 8, CZ // 128, 8, 128)
    return jnp.swapaxes(split, -3, -2).reshape(CX, CY, CZ)


def row_of(ref, x, y):
    return ref[pl.ds((x * (CY // 8) + y // 8) * 64 + y % 8, 8, stride=8), :]


def line_of(ref, x, y):
    return ref[pl.ds((x * (CY // 8) + y // 8) * 64 + y % 8, 8, stride=8), :]


def pack_kernel(
    permit_hbm,
    back_hbm,
    perturb_hbm,
    nodes_hbm,
    weights_hbm,
    owner_hbm,
    sensor_hbm,
    low_x,
    high_x,
    low_a,
    high_a,
    low_y,
    high_y,
    meta,
    permit,
    back,
    perturb,
    nodes,
    weights,
    owner,
    sensor,
    sems,
):
    pairs = (
        (nodes_hbm, nodes),
        (weights_hbm, weights),
        (owner_hbm, owner),
        (sensor_hbm, sensor),
        (permit_hbm, permit),
        (back_hbm, back),
        (perturb_hbm, perturb),
    )
    copies = [pltpu.make_async_copy(a, b, sems.at[i]) for i, (a, b) in enumerate(pairs)]
    for copy in copies:
        copy.start()
    for copy in copies[:4]:
        copy.wait()
    meta[0:4, :] = nodes[...].astype(F32)
    meta[4:8, :] = weights[...]
    meta[8:9, :] = owner[...].astype(F32)
    meta[9:10, :] = sensor[...].astype(F32)
    meta[10:16, :] = jnp.zeros((6, 1024), F32)
    at = AHEAD_META
    for out in (low_a, high_a):
        for c in range(8):
            lanes = slice(c * 128, (c + 1) * 128)
            out[at + c * 8 : at + c * 8 + 8, :] = meta[0:8, lanes]
            for i in range(2):
                out[at + 64 + i * 8 + c : at + 65 + i * 8 + c, :] = meta[8 + i : 9 + i, lanes]

    for field, ref in enumerate((permit, back, perturb)):
        copies[4 + field].wait()
        planes = D if field == 0 else D - 1

        def plane(x, carry, field=field, ref=ref, planes=planes):
            for y in range(CY):
                at = pl.ds(PX_AT[field] + (x * CY + y) * 8, 8)
                low_x[at, :] = row_of(ref, x, y)
                high_x[at, :] = row_of(ref, x + CX - planes, y)
            return carry

        lax.fori_loop(0, planes, plane, 0)
        for x in range(CX):
            for y in range(D):
                at = pl.ds(field * HALO_Y + (x * D + y) * 8, 8)
                low_y[at, :] = row_of(ref, x, y)
                high_y[at, :] = row_of(ref, x, y + CY - D)
        for i, (dx, dy) in enumerate(CELLS):
            for part, x in enumerate((dx - 1, CX - dx)):
                at = (3 * part + field) * HALO_C + i * 8
                low_a[at : at + 8, :] = row_of(ref, x, dy - 1)
                high_a[at : at + 8, :] = row_of(ref, x, CY - dy)

    def flux(y, carry):
        for out, near, far in ((low_x, D - 2, D - 1), (high_x, CX - D + 1, CX - D)):
            face = 0.5 * (line_of(perturb, near, y) + line_of(perturb, far, y))
            at = pl.ds(pl.multiple_of(PX_FLUX + y * 8, 8), 8)
            out[at, :] = face * (line_of(back, far, y) - line_of(back, near, y))
        return carry

    lax.fori_loop(0, CY, flux, 0)


def own_kernel(
    permit_hbm,
    back_hbm,
    perturb_hbm,
    meta,
    low_in,
    high_in,
    q,
    bg,
    qp,
    cz,
    bz,
    hot,
    low_y,
    high_y,
    permit,
    back,
    perturb,
    sems,
):
    del low_in, high_in, low_y, high_y
    pairs = ((permit_hbm, permit), (back_hbm, back), (perturb_hbm, perturb))
    copies = [pltpu.make_async_copy(a, b, sems.at[i]) for i, (a, b) in enumerate(pairs)]
    for copy in copies:
        copy.start()

    def entries(i, carry):
        k, lanes = i // 2, pl.ds(pl.multiple_of((i % 2) * 512, 512), 512)
        node = meta[pl.ds(k, 1), lanes].astype(jnp.int32)
        at = pl.ds(pl.multiple_of(i * 512, 512), 512)
        put_one_hot(node & (CZ - 1), CZ, hot, 0, at)
        return carry

    lax.fori_loop(0, 8, entries, 0)
    for copy in copies:
        copy.wait()

    def plane(x, carry):
        for y in range(CY):
            q[x + D, y + D] = row_of(permit, x, y) * (0.5 / HALF)
            bg[x + D, y + D] = row_of(back, x, y)
            qp[x + D, y + D] = row_of(perturb, x, y) * 0.5
        for y in range(0, CY, 4):
            at = pl.ds(y + D, 4)
            cz[x + D, at] = z_face(q[x + D, at])
            bz[x, pl.ds(y, 4)] = z_fluxes(bg[x + D, at], z_face(qp[x + D, at]))
        return carry

    lax.fori_loop(0, CX, plane, 0)


def corner_kernel(from_low, from_high, after, low, high):
    del after
    for side, ref in enumerate((from_low, from_high)):
        for part, out in enumerate((low, high)):
            at, first = side * PART, part * 3 * HALO_C
            out[at : at + 3 * HALO_C, :] = ref[first : first + 3 * HALO_C, :]
            out[at + 3 * HALO_C : at + PART, :] = ref[AHEAD_META:, :]


def vmem(count):
    return [pl.BlockSpec(memory_space=pltpu.VMEM)] * count


def shift(x, axis, by):
    count = lax.axis_size(axis)
    return lax.ppermute(x, axis, [(i, (i + by) % count) for i in range(count)])


def body(
    background_field,
    perturbation,
    permittivity,
    probe_nodes,
    probe_weights,
    probe_owner,
    probe_sensor,
    sensor_weight,
):
    devices = lax.axis_size("px") * lax.axis_size("py")
    fields = [by_tiles(f) for f in (permittivity, background_field, perturbation)]
    weights = jnp.pad(sensor_weight, (0, 128 - sensor_weight.shape[0]))[None, :]

    def rows(*counts):
        return [jax.ShapeDtypeStruct((n, 128), F32) for n in counts]

    def call(kernel, outs, *args, hbm=0, passed=0, at=1, scratch=(), limit, bytes_accessed=0):
        held = [pltpu.with_memory_space_constraint(a, pltpu.HBM) for a in args[:hbm]]
        args = held + list(args[hbm:])
        return pl.pallas_call(
            kernel,
            out_shape=tuple(outs),
            in_specs=[pl.BlockSpec(memory_space=pltpu.HBM)] * hbm + vmem(len(args) - hbm),
            out_specs=tuple(vmem(len(outs))),
            scratch_shapes=scratch,
            input_output_aliases={len(args) - passed + i: at + i for i in range(passed)},
            compiler_params=pltpu.CompilerParams(vmem_limit_bytes=limit * 2**20),
            cost_estimate=pl.CostEstimate(
                flops=0, bytes_accessed=bytes_accessed, transcendentals=0
            ),
        )(*args)

    size_x, size_y, size_c = PX_ROWS, 3 * HALO_Y, 2 * PART
    raw = [pltpu.VMEM((ROWS, 128), F32)] * 3
    table = jax.ShapeDtypeStruct((16, 1024), F32)
    low_x, high_x, low_a, high_a, low_y, high_y, meta = call(
        pack_kernel,
        rows(size_x, size_x, AHEAD, AHEAD, size_y, size_y) + [table],
        *fields,
        probe_nodes,
        probe_weights,
        probe_owner.reshape(1, -1),
        probe_sensor.reshape(1, -1),
        hbm=7,
        scratch=raw
        + [
            pltpu.VMEM((4, 1024), jnp.int32),
            pltpu.VMEM((4, 1024), F32),
            pltpu.VMEM((1, 1024), jnp.int32),
            pltpu.VMEM((1, 1024), jnp.int32),
            pltpu.SemaphoreType.DMA((7,)),
        ],
        limit=6,
    )
    px_low, px_high = shift(high_x, "px", 1), shift(low_x, "px", -1)
    a_low, a_high = shift(high_a, "py", 1), shift(low_a, "py", -1)
    compact = jax.ShapeDtypeStruct((CX, CY, 8, 128), F32)
    full = jax.ShapeDtypeStruct((EX, EY, 8, 128), F32)
    q, bg, qp, cz, bz, hot, low_y, high_y = call(
        own_kernel,
        [full] * 4 + [compact, jax.ShapeDtypeStruct((CZ, 4096), BF16)] + rows(size_y, size_y),
        *fields,
        meta,
        low_y,
        high_y,
        hbm=3,
        passed=2,
        at=6,
        scratch=raw + [pltpu.SemaphoreType.DMA((3,))],
        limit=10,
        bytes_accessed=8 * 2**20,
    )
    py_low, py_high = shift(high_y, "py", 1), shift(low_y, "py", -1)
    low_c, high_c = call(corner_kernel, rows(size_c, size_c), a_low, a_high, bz, limit=4)
    c_low, c_high = shift(high_c, "px", 1), shift(low_c, "px", -1)
    q, bg, qp, cz, b, y1, y2 = call(
        middle_kernel,
        [full] * 7,
        py_low,
        py_high,
        low_c,
        bz,
        q,
        bg,
        qp,
        cz,
        passed=4,
        at=0,
        limit=6,
        bytes_accessed=8 * 2**20,
    )
    block = pltpu.VMEM((EX, EY, 8, 128), F32)
    readings, q, bg, qp, cz, b, y1, y2 = call(
        tangent_kernel,
        rows(devices * 9) + [full] * 7,
        px_low,
        px_high,
        c_low,
        c_high,
        bz,
        meta,
        hot,
        weights,
        q,
        bg,
        qp,
        cz,
        b,
        y1,
        y2,
        passed=7,
        scratch=[block, pltpu.VMEM((2 * CX * CY, CZ), BF16), pltpu.VMEM((8, 1024), F32)],
        limit=14,
    )
    got = lax.all_to_all(
        readings.reshape(devices, 1, 9 * 128),
        ("px", "py"),
        split_axis=0,
        concat_axis=0,
        tiled=True,
    ).reshape(devices * 9, 128)
    weighted, own_source, low_s, high_s = call(
        source_kernel,
        rows(8, ROWS, D * PLANE, D * PLANE),
        got,
        meta,
        hot,
        scratch=[pltpu.VMEM((2 * CX * CY, 4096), BF16), pltpu.VMEM((8, 1024), F32)],
        limit=18,
    )
    source_low, source_high = shift(high_s, "px", 1), shift(low_s, "px", -1)
    src, y1, y2, y3 = call(
        strips_kernel,
        [full] * 4,
        weighted,
        a_low,
        a_high,
        c_low,
        c_high,
        own_source,
        q,
        cz,
        scratch=[
            pltpu.VMEM((2 * 4 * CX * D, 4096), BF16),
            pltpu.VMEM((256, 4096), BF16),
            pltpu.VMEM((16, 1024), F32),
            pltpu.VMEM((8, 1024), F32),
        ],
        limit=16,
        bytes_accessed=24 * 2**20,
    )
    result = call(
        adjoint_kernel,
        rows(ROWS) + [full] * 4,
        source_low,
        source_high,
        q,
        bg,
        cz,
        src,
        y1,
        y2,
        y3,
        passed=4,
        limit=8,
    )[0]
    return from_tiles(result)


def solution(mesh):
    placed = (
        P("px", "py", None),
        P("px", "py", None),
        P("px", "py", None),
        P(None, ("px", "py")),
        P(None, ("px", "py")),
        P(("px", "py"), None),
        P(("px", "py")),
        P(("px", "py")),
    )
    return jax.shard_map(
        body, mesh=mesh, in_specs=placed, out_specs=P("px", "py", None), check_vma=False
    )
```

```python
import jax
import jax.numpy as jnp
import numpy as np
from jax import lax
from jax.experimental import pallas as pl
from jax.experimental.pallas import tpu as pltpu
from jax.sharding import PartitionSpec as P

SWEEPS = 4
MASS = 1.0
LOW = 1.0
HIGH = 25.0
CENTRE = 0.5 * (HIGH + LOW)
HALF = 0.5 * (HIGH - LOW)

CX, CY, CZ = 8, 32, 1024
D = 4
EX, EY = CX + 2 * D, CY + 2 * D
ROWS = CX * CY * 8
PLANE = CY * 8
PX_AT = (0, D * PLANE, (2 * D - 1) * PLANE)
PX_FLUX = (3 * D - 2) * PLANE
PX_ROWS = (3 * D - 1) * PLANE
HALO_Y = CX * D * 8
CELLS = tuple((dx, dy) for dx in range(1, D) for dy in range(1, D) if dx + dy <= D)
HALO_C = len(CELLS) * 8
META = 80
PART = 3 * HALO_C + META
F32 = jnp.float32
BF16 = jnp.bfloat16


def horner_terms():
    spread = CENTRE / HALF
    size = SWEEPS
    iterate = np.zeros(size)
    remain = np.eye(size)[0]
    search = remain / CENTRE
    ratio = 1.0 / spread
    for sweep in range(SWEEPS):
        iterate = iterate + search
        if sweep < SWEEPS - 1:
            shifted = np.concatenate([[0.0], search[:-1]])
            remain = remain - (CENTRE * search + HALF * shifted)
            following = 1.0 / (2.0 * spread - ratio)
            search = following * ratio * search + 2.0 * following / HALF * remain
            ratio = following
    return [float(v) for v in iterate]


A0, A1, A2, A3 = horner_terms()


def lane_of(n):
    return lax.broadcasted_iota(jnp.int32, (n, 8, 128), 2)


def z_up(f):
    r = pltpu.roll(f, 127, 2)
    return jnp.where(lane_of(f.shape[0]) == 127, pltpu.roll(r, 7, 1), r)


def z_down(f):
    r = pltpu.roll(f, 1, 2)
    return jnp.where(lane_of(f.shape[0]) == 0, pltpu.roll(r, 1, 1), r)


def z_face(q):
    n = q.shape[0]
    sub = lax.broadcasted_iota(jnp.int32, (n, 8, 128), 1)
    last = (sub == 7) & (lane_of(n) == 127)
    return jnp.where(last, 0.0, q + z_up(q))


def side_fluxes(src, q, x, y, n):
    fe, qe = src[x, pl.ds(y - 1, n + 2)], q[x, pl.ds(y - 1, n + 2)]
    f, qc = fe[1:-1], qe[1:-1]
    fy = (fe[1:] - fe[:-1]) * (qe[1:] + qe[:-1])
    acc = fy[1:] - fy[:-1]
    acc += (src[x + 1, pl.ds(y, n)] - f) * (q[x + 1, pl.ds(y, n)] + qc)
    acc += (src[x - 1, pl.ds(y, n)] - f) * (q[x - 1, pl.ds(y, n)] + qc)
    return f, acc


def z_fluxes(f, faces):
    fz = (z_up(f) - f) * faces
    return fz - z_down(fz)


def fluxes(src, q, cz, x, y, n):
    f, acc = side_fluxes(src, q, x, y, n)
    return f, acc + z_fluxes(f, cz[x, pl.ds(y, n)])


def cover(low, high, n):
    starts = list(range(low, high - n + 1, n))
    if starts[-1] + n < high:
        starts.append(high - n)
    return starts


def early(margin, plane):
    def step(x, carry):
        plane(x)
        return carry

    lax.fori_loop(margin + D, EX - D - margin, step, 0)


def late(margin, plane):
    def step(i, carry):
        plane(jnp.where(i < D, margin + i, EX - 2 * D - margin + i))
        return carry

    lax.fori_loop(0, 2 * D, step, 0)


def lines(margin, n, step):
    def plane(x):
        for y in cover(margin, EY - margin, n):
            step(x, y, n)

    return plane


def put_py(field, py_low, py_high, out, scale):
    for ref, at in ((py_low, 0), (py_high, D + CY)):
        v = ref[field * HALO_Y : (field + 1) * HALO_Y, :]
        out[D : D + CX, at : at + D] = v.reshape(CX, D, 8, 128) * scale


def put_px(field, sides, out, scale):
    px_low, px_high, c_low, c_high = sides
    middle_y = slice(D, D + CY)
    planes = D if field == 0 else D - 1
    for ref, at in ((px_low, D - planes), (px_high, D + CX)):
        v = ref[PX_AT[field] : PX_AT[field] + planes * PLANE, :]
        out[at : at + planes, middle_y] = v.reshape(planes, CY, 8, 128) * scale
    blank = jnp.zeros((D, D, 8, 128), F32)
    for x, ref in ((0, c_low), (D + CX, c_high)):
        for side, y in enumerate((0, D + CY)):
            out[x : x + D, y : y + D] = blank
            for i, (dx, dy) in enumerate(CELLS):
                at = side * PART + field * HALO_C + i * 8
                cell_x = x + D - dx if x == 0 else x + dx - 1
                cell_y = y + D - dy if y == 0 else y + dy - 1
                out[cell_x, cell_y] = ref[at : at + 8, :] * scale


def far_planes(sides, bg, qp):
    middle_y = slice(D, D + CY)
    for ref, at, beside in ((sides[0], 0, 1), (sides[1], EX - 1, EX - 2)):
        flux = ref[PX_FLUX : PX_FLUX + PLANE, :].reshape(CY, 8, 128)
        bg[at, middle_y] = bg[beside, middle_y] + flux
        qp[at, middle_y] = 1.0 - qp[beside, middle_y]


def close_py(out, sign, planes):
    py, last_y = lax.axis_index("py"), lax.axis_size("py") - 1

    @pl.when(py == 0)
    def _():
        out[planes, D - 1] = out[planes, D] * sign

    @pl.when(py == last_y)
    def _():
        out[planes, D + CY] = out[planes, D + CY - 1] * sign


def first_solve(q, bg, qp, cz, bz, b, y1, y2):
    def whole(x, y, n):
        f, acc = side_fluxes(bg, qp, x, y, n)
        b[x, pl.ds(y, n)] = acc + z_fluxes(f, z_face(qp[x, pl.ds(y, n)]))
        cz[x, pl.ds(y, n)] = z_face(q[x, pl.ds(y, n)])

    def right_own(x):
        whole(x, 1, D - 1)
        whole(x, D + CY, D - 1)
        for y in cover(D, D + CY, 4):
            _, acc = side_fluxes(bg, qp, x, y, 4)
            b[x, pl.ds(y, 4)] = acc + bz[x - D, pl.ds(y - D, 4)]

    def second(x, y, n):
        f, acc = fluxes(b, q, cz, x, y, n)
        y1[x, pl.ds(y, n)] = (A2 - A3) * f - A3 * acc

    def third(x, y, n):
        f, acc = fluxes(y1, q, cz, x, y, n)
        y2[x, pl.ds(y, n)] = A1 * b[x, pl.ds(y, n)] - f - acc

    return lines(1, 4, whole), right_own, lines(2, 4, second), lines(3, 4, third)


def middle_kernel(
    py_low, py_high, after, bz, q_in, bg_in, qp_in, cz_in, q, bg, qp, cz, b, y1, y2
):
    del after, q_in, bg_in, qp_in, cz_in
    own = slice(D, D + CX)
    for field, out, scale, sign in ((0, q, 0.5 / HALF, -1.0), (1, bg, 1.0, 1.0), (2, qp, 0.5, -1.0)):
        put_py(field, py_low, py_high, out, scale)
        close_py(out, sign, own)
    _, right_own, second, third = first_solve(q, bg, qp, cz, bz, b, y1, y2)
    early(1, right_own)
    early(2, second)
    early(3, third)


def close_edges(out, sign):
    px, last_x = lax.axis_index("px"), lax.axis_size("px") - 1

    @pl.when(px == 0)
    def _():
        out[D - 1] = out[D] * sign

    @pl.when(px == last_x)
    def _():
        out[D + CX] = out[D + CX - 1] * sign

    close_py(out, sign, slice(0, EX))


def take_meta(ref, base, out):
    for c in range(8):
        lanes = slice(c * 128, (c + 1) * 128)
        out[0:8, lanes] = ref[base + c * 8 : base + c * 8 + 8, :]
        for i in range(2):
            at = base + 64 + i * 8 + c
            out[8 + i : 9 + i, lanes] = ref[at : at + 1, :]


def two_parts(v):
    high = v.astype(BF16)
    return high, (v - high.astype(F32)).astype(BF16)


def three_parts(v):
    high = v.astype(BF16)
    rest = v - high.astype(F32)
    mid = rest.astype(BF16)
    return high, mid, (rest - mid.astype(F32)).astype(BF16)


def one_hot(index, count):
    at = lax.broadcasted_iota(jnp.int32, (count, index.shape[1]), 0)
    return jnp.where(at == index, 1.0, 0.0).astype(BF16)


def rows16(index):
    shape = (16, index.shape[1])
    numbers = lax.broadcasted_iota(jnp.int32, shape, 0).astype(jnp.int16)
    return jnp.broadcast_to(index, shape).astype(jnp.int16), numbers


def put_one_hot(index, count, out, first, lanes):
    wanted, numbers = rows16(index)
    one, zero = jnp.ones(wanted.shape, BF16), jnp.zeros(wanted.shape, BF16)
    for r in range(count // 16):
        hit = numbers + jnp.int16(r * 16) == wanted
        out[first + r * 16 : first + (r + 1) * 16, lanes] = jnp.where(hit, one, zero)


def dot(a, b, over):
    return lax.dot_general(a, b, (over, ((), ())), preferred_element_type=F32)


def tangent_kernel(
    px_low,
    px_high,
    c_low,
    c_high,
    bz,
    meta,
    hot,
    weights,
    q_in,
    bg_in,
    qp_in,
    cz_in,
    b_in,
    y1_in,
    y2_in,
    out,
    q,
    bg,
    qp,
    cz,
    b,
    y1,
    y2,
    y3,
    table,
    vals,
):
    del q_in, bg_in, qp_in, cz_in, b_in, y1_in, y2_in
    sides = (px_low, px_high, c_low, c_high)
    put_px(0, sides, q, 0.5 / HALF)
    put_px(1, sides, bg, 1.0)
    put_px(2, sides, qp, 0.5)
    far_planes(sides, bg, qp)
    close_edges(q, -1.0)
    close_edges(qp, -1.0)
    close_edges(bg, 1.0)
    right, right_own, second, third = first_solve(q, bg, qp, cz, bz, b, y1, y2)

    def outer_planes(i, carry):
        right(jnp.where(i < D - 1, 1 + i, CX + 1 + i))
        return carry

    def edge_planes(i, carry):
        right_own(D + i * (CX - 1))
        return carry

    lax.fori_loop(0, 2 * (D - 1), outer_planes, 0)
    lax.fori_loop(0, 2, edge_planes, 0)
    late(2, second)
    late(3, third)

    def fourth(x, y, n):
        f, acc = fluxes(y2, q, cz, x, y, n)
        y3[x, pl.ds(y, n)] = A0 * b[x, pl.ds(y, n)] - f - acc

    late(4, lines(4, 4, fourth))

    flat = y3.reshape(EX * EY * 8, 128)
    for x in range(CX):
        for c in range(8):
            v = flat[pl.ds(((x + D) * EY + D) * 8 + c, CY, stride=8), :]
            high, low = two_parts(v)
            table[x * CY : (x + 1) * CY, c * 128 : (c + 1) * 128] = high
            table[CX * CY + x * CY : CX * CY + (x + 1) * CY, c * 128 : (c + 1) * 128] = low

    vals[...] = jnp.zeros_like(vals)
    wide = 512

    def gather(i, carry):
        k, lanes = i // 2, pl.ds(pl.multiple_of((i % 2) * wide, wide), wide)
        node = meta[pl.ds(k, 1), lanes].astype(jnp.int32)
        found = dot(table[...], hot[:, pl.ds(pl.multiple_of(i * wide, wide), wide)], ((1,), (0,)))
        found = found[: CX * CY] + found[CX * CY :]
        at = lax.broadcasted_iota(jnp.int32, found.shape, 0)
        found = jnp.sum(jnp.where(at == node >> 10, found, 0.0), axis=0, keepdims=True)
        vals[0:1, lanes] += meta[pl.ds(k + 4, 1), lanes] * found
        return carry

    lax.fori_loop(0, 8, gather, 0)

    owner, sensor = meta[8:9, :].astype(jnp.int32), meta[9:10, :].astype(jnp.int32)
    at = lax.broadcasted_iota(jnp.int32, (8, 1024), 0)
    owned = jnp.where(at == sensor, vals[0:1, :], 0.0)
    parts = jnp.concatenate(three_parts(owned), axis=0)
    sums = dot(parts, one_hot(owner, 128), ((1,), (1,)))
    readings = sums[0:8] + sums[8:16] + sums[16:24]
    block = jnp.concatenate([readings, weights[...]] * 8, axis=0)
    for i in range(out.shape[0] // 72):
        out[i * 72 : (i + 1) * 72, :] = block


def scatter(meta, values, rows, per, tiles, width, lhs, keep, hot):
    for k in range(4):
        wanted, numbers = rows16(rows(meta[k : k + 1, :].astype(jnp.int32)))
        value = jnp.broadcast_to(values[k : k + 1, :], wanted.shape)
        high, low = two_parts(value)
        zero = jnp.zeros(wanted.shape, BF16)
        lanes = slice(k * 1024, (k + 1) * 1024)
        for r in range(per // 16):
            hit = numbers + jnp.int16(r * 16) == wanted
            lhs[r * 16 : (r + 1) * 16, lanes] = jnp.where(hit, high, zero)
            lhs[per + r * 16 : per + (r + 1) * 16, lanes] = jnp.where(hit, low, zero)

    def tile(t, carry):
        total = None
        for k in range(4):
            lanes = slice(k * 1024, (k + 1) * 1024)
            hits = hot[pl.ds(pl.multiple_of(t * width, width), width), lanes]
            part = dot(lhs[0 : 2 * per, lanes], hits, ((1,), (1,)))
            total = part if total is None else total + part
        keep(t, total[0:per] + total[per : 2 * per])
        return carry

    if tiles == 1:
        tile(0, 0)
    else:
        lax.fori_loop(0, tiles, tile, 0)


def returned(weighted, table, values):
    owner, sensor = table[8:9, :].astype(jnp.int32), table[9:10, :].astype(jnp.int32)
    parts = jnp.concatenate(three_parts(weighted), axis=0)
    found = dot(parts, one_hot(owner, 128), ((1,), (0,)))
    found = found[0:8] + found[8:16] + found[16:24]
    at = lax.broadcasted_iota(jnp.int32, found.shape, 0)
    found = jnp.sum(jnp.where(at == sensor, found, 0.0), axis=0, keepdims=True)
    values[0:4, :] = table[4:8, :] * found


def source_kernel(got, meta, hot, weighted, own, low, high, lhs, values):
    count = got.shape[0] // 9
    sums = [jnp.sum(got[pl.ds(i, count, stride=9), :], axis=0, keepdims=True) for i in range(8)]
    readings = jnp.concatenate(sums, axis=0)
    weights = jnp.transpose(got[pl.ds(8, count, stride=9), :])[0:8]
    weighted[...] = readings * weights

    def keep(t, sums):
        for x in range(CX):
            for i in range(4):
                block = sums[x * CY : (x + 1) * CY, i * 128 : (i + 1) * 128]
                own[pl.ds(x * PLANE + t * 4 + i, CY, stride=8), :] = block
                side, at = (low, x) if x < D else (high, x - (CX - D))
                side[pl.ds(at * PLANE + t * 4 + i, CY, stride=8), :] = block

    returned(weighted[...], meta, values)
    scatter(meta, values, lambda n: n >> 10, CX * CY, 2, 512, lhs, keep, hot)


def second_solve(src, q, cz, y1, y2, y3):
    def first(x, y, n):
        f, acc = fluxes(src, q, cz, x, y, n)
        y1[x, pl.ds(y, n)] = (A2 - A3) * f - A3 * acc

    def second(x, y, n):
        f, acc = fluxes(y1, q, cz, x, y, n)
        y2[x, pl.ds(y, n)] = A1 * src[x, pl.ds(y, n)] - f - acc

    def third(x, y, n):
        f, acc = fluxes(y2, q, cz, x, y, n)
        y3[x, pl.ds(y, n)] = A0 * src[x, pl.ds(y, n)] - f - acc

    return lines(1, 4, first), lines(2, 4, second), lines(3, 4, third)


def strips_kernel(
    weighted,
    py_low,
    py_high,
    c_low,
    c_high,
    own,
    q,
    cz,
    src,
    y1,
    y2,
    y3,
    lhs,
    near_hot,
    near,
    values,
):
    src[D : D + CX, D : D + CY] = own[...].reshape(CX, CY, 8, 128)
    flat = src.reshape(EX * EY * 8, 128)

    def columns(count):
        for k in range(4):
            node = near[k : k + 1, :].astype(jnp.int32)
            put_one_hot(node & (count - 1), count, near_hot, 0, slice(k * 1024, (k + 1) * 1024))

    for ref, y0, first_y in ((py_low, 0, CY - D), (py_high, D + CY, 0)):
        take_meta(ref, 3 * HALO_Y, near)
        returned(weighted[...], near, values)
        columns(256)

        def rows(node, first_y=first_y):
            x, y = node >> 15, ((node >> 10) & (CY - 1)) - first_y
            good = (y >= 0) & (y < D)
            return jnp.where(good, (((node >> 8) & 3) * CX + x) * D + y, -1)

        def keep(t, sums, y0=y0):
            for zq in range(4):
                for x in range(CX):
                    first = (zq * CX + x) * D
                    for half in range(2):
                        flat[
                            pl.ds(((x + D) * EY + y0) * 8 + zq * 2 + half, D, stride=8), :
                        ] = sums[first : first + D, half * 128 : (half + 1) * 128]

        scatter(near, values, rows, 4 * CX * D, 1, 256, lhs, keep, near_hot)

    for ref, x_low in ((c_low, True), (c_high, False)):
        for side, y_low in enumerate((True, False)):
            take_meta(ref, side * PART + 3 * HALO_C, near)
            returned(weighted[...], near, values)
            columns(128)

            def rows(node, x_low=x_low, y_low=y_low):
                x, y = node >> 15, (node >> 10) & (CY - 1)
                dx = CX - x if x_low else x + 1
                dy = CY - y if y_low else y + 1
                cell = jnp.where(dx == 1, dy - 1, jnp.where(dx == 2, dy + 2, 5))
                return jnp.where(dx + dy <= D, ((node >> 7) & 7) * len(CELLS) + cell, -1)

            def keep(t, sums, x_low=x_low, y_low=y_low):
                x0, y0 = 0 if x_low else D + CX, 0 if y_low else D + CY
                src[x0 : x0 + D, y0 : y0 + D] = jnp.zeros((D, D, 8, 128), F32)
                for i, (dx, dy) in enumerate(CELLS):
                    x = D - dx if x_low else D + CX + dx - 1
                    y = D - dy if y_low else D + CY + dy - 1
                    for c in range(8):
                        row = c * len(CELLS) + i
                        flat[(x * EY + y) * 8 + c : (x * EY + y) * 8 + c + 1, :] = sums[
                            row : row + 1, :
                        ]

            scatter(near, values, rows, 8 * len(CELLS), 1, 128, lhs, keep, near_hot)

    first, second, third = second_solve(src, q, cz, y1, y2, y3)
    early(1, first)
    early(2, second)
    early(3, third)


def adjoint_kernel(
    px_low, px_high, q, bg, cz, src_in, y1_in, y2_in, y3_in, out_hbm, src, y1, y2, y3, out, sems
):
    del src_in, y1_in, y2_in, y3_in
    for x, ref in ((0, px_low), (D + CX, px_high)):
        src[x : x + D, D : D + CY] = ref[...].reshape(D, CY, 8, 128)
    first, second, third = second_solve(src, q, cz, y1, y2, y3)
    late(1, first)
    late(2, second)
    late(3, third)

    def last(x, y, n):
        ae, be = y3[x, pl.ds(y - 1, n + 2)], bg[x, pl.ds(y - 1, n + 2)]
        a, k = ae[1:-1], be[1:-1]
        sy = (ae[1:] - ae[:-1]) * (be[1:] - be[:-1])
        total = sy[1:] + sy[:-1]
        total += (y3[x + 1, pl.ds(y, n)] - a) * (bg[x + 1, pl.ds(y, n)] - k)
        total += (y3[x - 1, pl.ds(y, n)] - a) * (bg[x - 1, pl.ds(y, n)] - k)
        sub = lax.broadcasted_iota(jnp.int32, (n, 8, 128), 1)
        end = (sub == 7) & (lane_of(n) == 127)
        sz = jnp.where(end, 0.0, (z_up(a) - a) * (z_up(k) - k))
        total = -0.5 * (total + (sz + z_down(sz)))
        yy = y - D
        for i in range(n):
            row = (x - D) * (CY // 8) + (yy + i) // 8
            out[pl.ds(row * 64 + (yy + i) % 8, 8, stride=8), :] = total[i]

    def leave(x):
        i = x - D
        at = pl.ds(pl.multiple_of(i * PLANE, PLANE), PLANE)
        return pltpu.make_async_copy(out.at[at], out_hbm.at[at], sems.at[i])

    compute = lines(4, 4, last)

    def plane(x):
        compute(x)
        leave(x).start()

    late(4, plane)
    for x in range(D, D + CX):
        leave(x).wait()


def by_tiles(block):
    lead = block.shape[:-2]
    rows, cols = block.shape[-2:]
    split = block.reshape(*lead, rows // 8, 8, cols // 128, 128)
    return jnp.swapaxes(split, -3, -2).reshape(-1, 128)


def from_tiles(rows):
    split = rows.reshape(CX, CY // 8, CZ // 128, 8, 128)
    return jnp.swapaxes(split, -3, -2).reshape(CX, CY, CZ)


def row_of(ref, x, y):
    return ref[pl.ds((x * (CY // 8) + y // 8) * 64 + y % 8, 8, stride=8), :]


def line_of(ref, x, y):
    return ref[pl.ds((x * (CY // 8) + y // 8) * 64 + y % 8, 8, stride=8), :]


def pack_kernel(
    permit_hbm,
    back_hbm,
    perturb_hbm,
    nodes_hbm,
    weights_hbm,
    owner_hbm,
    sensor_hbm,
    low_x,
    high_x,
    low_y,
    high_y,
    meta,
    permit,
    back,
    perturb,
    nodes,
    weights,
    owner,
    sensor,
    sems,
):
    pairs = (
        (nodes_hbm, nodes),
        (weights_hbm, weights),
        (owner_hbm, owner),
        (sensor_hbm, sensor),
        (permit_hbm, permit),
        (back_hbm, back),
        (perturb_hbm, perturb),
    )
    copies = [pltpu.make_async_copy(a, b, sems.at[i]) for i, (a, b) in enumerate(pairs)]
    for copy in copies:
        copy.start()
    for copy in copies[:4]:
        copy.wait()
    meta[0:4, :] = nodes[...].astype(F32)
    meta[4:8, :] = weights[...]
    meta[8:9, :] = owner[...].astype(F32)
    meta[9:10, :] = sensor[...].astype(F32)
    meta[10:16, :] = jnp.zeros((6, 1024), F32)
    for out, at in ((low_y, 3 * HALO_Y), (high_y, 3 * HALO_Y)):
        for c in range(8):
            lanes = slice(c * 128, (c + 1) * 128)
            out[at + c * 8 : at + c * 8 + 8, :] = meta[0:8, lanes]
            for i in range(2):
                out[at + 64 + i * 8 + c : at + 65 + i * 8 + c, :] = meta[8 + i : 9 + i, lanes]

    for field, ref in enumerate((permit, back, perturb)):
        copies[4 + field].wait()
        planes = D if field == 0 else D - 1

        def plane(x, carry, field=field, ref=ref, planes=planes):
            for y in range(CY):
                at = pl.ds(PX_AT[field] + (x * CY + y) * 8, 8)
                low_x[at, :] = row_of(ref, x, y)
                high_x[at, :] = row_of(ref, x + CX - planes, y)
            return carry

        lax.fori_loop(0, planes, plane, 0)
        for x in range(CX):
            for y in range(D):
                at = pl.ds(field * HALO_Y + (x * D + y) * 8, 8)
                low_y[at, :] = row_of(ref, x, y)
                high_y[at, :] = row_of(ref, x, y + CY - D)

    def flux(y, carry):
        for out, near, far in ((low_x, D - 2, D - 1), (high_x, CX - D + 1, CX - D)):
            face = 0.5 * (line_of(perturb, near, y) + line_of(perturb, far, y))
            at = pl.ds(pl.multiple_of(PX_FLUX + y * 8, 8), 8)
            out[at, :] = face * (line_of(back, far, y) - line_of(back, near, y))
        return carry

    lax.fori_loop(0, CY, flux, 0)


def own_kernel(
    permit_hbm,
    back_hbm,
    perturb_hbm,
    meta,
    q,
    bg,
    qp,
    cz,
    bz,
    hot,
    permit,
    back,
    perturb,
    sems,
):
    pairs = ((permit_hbm, permit), (back_hbm, back), (perturb_hbm, perturb))
    copies = [pltpu.make_async_copy(a, b, sems.at[i]) for i, (a, b) in enumerate(pairs)]
    for copy in copies:
        copy.start()

    def entries(i, carry):
        k, lanes = i // 2, pl.ds(pl.multiple_of((i % 2) * 512, 512), 512)
        node = meta[pl.ds(k, 1), lanes].astype(jnp.int32)
        at = pl.ds(pl.multiple_of(i * 512, 512), 512)
        put_one_hot(node & (CZ - 1), CZ, hot, 0, at)
        return carry

    lax.fori_loop(0, 8, entries, 0)
    for copy in copies:
        copy.wait()

    def plane(x, carry):
        for y in range(CY):
            q[x + D, y + D] = row_of(permit, x, y) * (0.5 / HALF)
            bg[x + D, y + D] = row_of(back, x, y)
            qp[x + D, y + D] = row_of(perturb, x, y) * 0.5
        for y in range(0, CY, 4):
            at = pl.ds(y + D, 4)
            cz[x + D, at] = z_face(q[x + D, at])
            bz[x, pl.ds(y, 4)] = z_fluxes(bg[x + D, at], z_face(qp[x + D, at]))
        return carry

    lax.fori_loop(0, CX, plane, 0)


def corner_kernel(py_low, py_high, after, low, high):
    del after
    for side, ref in enumerate((py_low, py_high)):
        for field in range(3):
            for i, (dx, dy) in enumerate(CELLS):
                y = D - dy if side == 0 else dy - 1
                at = side * PART + field * HALO_C + i * 8
                for out, x in ((low, dx - 1), (high, CX - dx)):
                    first = field * HALO_Y + (x * D + y) * 8
                    out[at : at + 8, :] = ref[first : first + 8, :]
        at = side * PART + 3 * HALO_C
        low[at : at + META, :] = ref[3 * HALO_Y :, :]
        high[at : at + META, :] = ref[3 * HALO_Y :, :]


def vmem(count):
    return [pl.BlockSpec(memory_space=pltpu.VMEM)] * count


def shift(x, axis, by):
    count = lax.axis_size(axis)
    return lax.ppermute(x, axis, [(i, (i + by) % count) for i in range(count)])


def body(
    background_field,
    perturbation,
    permittivity,
    probe_nodes,
    probe_weights,
    probe_owner,
    probe_sensor,
    sensor_weight,
):
    devices = lax.axis_size("px") * lax.axis_size("py")
    fields = [by_tiles(f) for f in (permittivity, background_field, perturbation)]
    weights = jnp.pad(sensor_weight, (0, 128 - sensor_weight.shape[0]))[None, :]

    def rows(*counts):
        return [jax.ShapeDtypeStruct((n, 128), F32) for n in counts]

    def call(kernel, outs, *args, hbm=0, away=0, passed=0, at=1, scratch=(), limit, bytes_accessed=0):
        held = [pltpu.with_memory_space_constraint(a, pltpu.HBM) for a in args[:hbm]]
        args = held + list(args[hbm:])
        return pl.pallas_call(
            kernel,
            out_shape=tuple(outs),
            in_specs=[pl.BlockSpec(memory_space=pltpu.HBM)] * hbm + vmem(len(args) - hbm),
            out_specs=tuple(
                [pl.BlockSpec(memory_space=pl.ANY)] * away + vmem(len(outs) - away)
            ),
            scratch_shapes=scratch,
            input_output_aliases={len(args) - passed + i: at + i for i in range(passed)},
            compiler_params=pltpu.CompilerParams(vmem_limit_bytes=limit * 2**20),
            cost_estimate=pl.CostEstimate(
                flops=0, bytes_accessed=bytes_accessed, transcendentals=0
            ),
        )(*args)

    size_x, size_y, size_c = PX_ROWS, 3 * HALO_Y + META, 2 * PART
    raw = [pltpu.VMEM((ROWS, 128), F32)] * 3
    table = jax.ShapeDtypeStruct((16, 1024), F32)
    low_x, high_x, low_y, high_y, meta = call(
        pack_kernel,
        rows(size_x, size_x, size_y, size_y) + [table],
        *fields,
        probe_nodes,
        probe_weights,
        probe_owner.reshape(1, -1),
        probe_sensor.reshape(1, -1),
        hbm=7,
        scratch=raw
        + [
            pltpu.VMEM((4, 1024), jnp.int32),
            pltpu.VMEM((4, 1024), F32),
            pltpu.VMEM((1, 1024), jnp.int32),
            pltpu.VMEM((1, 1024), jnp.int32),
            pltpu.SemaphoreType.DMA((7,)),
        ],
        limit=6,
    )
    px_low, px_high = shift(high_x, "px", 1), shift(low_x, "px", -1)
    py_low, py_high = shift(high_y, "py", 1), shift(low_y, "py", -1)
    compact = jax.ShapeDtypeStruct((CX, CY, 8, 128), F32)
    full = jax.ShapeDtypeStruct((EX, EY, 8, 128), F32)
    q, bg, qp, cz, bz, hot = call(
        own_kernel,
        [full] * 4 + [compact, jax.ShapeDtypeStruct((CZ, 4096), BF16)],
        *fields,
        meta,
        hbm=3,
        scratch=raw + [pltpu.SemaphoreType.DMA((3,))],
        limit=10,
        bytes_accessed=8 * 2**20,
    )
    low_c, high_c = call(corner_kernel, rows(size_c, size_c), py_low, py_high, bz, limit=4)
    c_low, c_high = shift(high_c, "px", 1), shift(low_c, "px", -1)
    q, bg, qp, cz, b, y1, y2 = call(
        middle_kernel,
        [full] * 7,
        py_low,
        py_high,
        low_c,
        bz,
        q,
        bg,
        qp,
        cz,
        passed=4,
        at=0,
        limit=6,
        bytes_accessed=8 * 2**20,
    )
    block = pltpu.VMEM((EX, EY, 8, 128), F32)
    readings, q, bg, qp, cz, b, y1, y2 = call(
        tangent_kernel,
        rows(devices * 9) + [full] * 7,
        px_low,
        px_high,
        c_low,
        c_high,
        bz,
        meta,
        hot,
        weights,
        q,
        bg,
        qp,
        cz,
        b,
        y1,
        y2,
        passed=7,
        scratch=[block, pltpu.VMEM((2 * CX * CY, CZ), BF16), pltpu.VMEM((8, 1024), F32)],
        limit=14,
    )
    got = lax.all_to_all(
        readings.reshape(devices, 1, 9 * 128),
        ("px", "py"),
        split_axis=0,
        concat_axis=0,
        tiled=True,
    ).reshape(devices * 9, 128)
    weighted, own_source, low_s, high_s = call(
        source_kernel,
        rows(8, ROWS, D * PLANE, D * PLANE),
        got,
        meta,
        hot,
        scratch=[pltpu.VMEM((2 * CX * CY, 4096), BF16), pltpu.VMEM((8, 1024), F32)],
        limit=18,
    )
    source_low, source_high = shift(high_s, "px", 1), shift(low_s, "px", -1)
    src, y1, y2, y3 = call(
        strips_kernel,
        [full] * 4,
        weighted,
        py_low,
        py_high,
        c_low,
        c_high,
        own_source,
        q,
        cz,
        scratch=[
            pltpu.VMEM((2 * 4 * CX * D, 4096), BF16),
            pltpu.VMEM((256, 4096), BF16),
            pltpu.VMEM((16, 1024), F32),
            pltpu.VMEM((8, 1024), F32),
        ],
        limit=16,
        bytes_accessed=24 * 2**20,
    )
    result = call(
        adjoint_kernel,
        rows(ROWS) + [full] * 4,
        source_low,
        source_high,
        q,
        bg,
        cz,
        src,
        y1,
        y2,
        y3,
        passed=4,
        away=1,
        scratch=[pltpu.VMEM((ROWS, 128), F32), pltpu.SemaphoreType.DMA((CX,))],
        limit=8,
    )[0]
    return from_tiles(result)


def solution(mesh):
    placed = (
        P("px", "py", None),
        P("px", "py", None),
        P("px", "py", None),
        P(None, ("px", "py")),
        P(None, ("px", "py")),
        P(("px", "py"), None),
        P(("px", "py")),
        P(("px", "py")),
    )
    return jax.shard_map(
        body, mesh=mesh, in_specs=placed, out_specs=P("px", "py", None), check_vma=False
    )
```

```python
import jax
import jax.numpy as jnp
import numpy as np
from jax import lax
from jax.experimental import pallas as pl
from jax.experimental.pallas import tpu as pltpu
from jax.sharding import PartitionSpec as P

SWEEPS = 4
MASS = 1.0
LOW = 1.0
HIGH = 25.0
CENTRE = 0.5 * (HIGH + LOW)
HALF = 0.5 * (HIGH - LOW)

CX, CY, CZ = 8, 32, 1024
D = 4
EX, EY = CX + 2 * D, CY + 2 * D
ROWS = CX * CY * 8
PLANE = CY * 8
PX_AT = (0, D * PLANE, (2 * D - 1) * PLANE)
PX_FLUX = (3 * D - 2) * PLANE
PX_ROWS = (3 * D - 1) * PLANE
HALO_Y = CX * D * 8
CELLS = tuple((dx, dy) for dx in range(1, D) for dy in range(1, D) if dx + dy <= D)
HALO_C = len(CELLS) * 8
META = 80
PART = 3 * HALO_C + META
F32 = jnp.float32
BF16 = jnp.bfloat16


def horner_terms():
    spread = CENTRE / HALF
    size = SWEEPS
    iterate = np.zeros(size)
    remain = np.eye(size)[0]
    search = remain / CENTRE
    ratio = 1.0 / spread
    for sweep in range(SWEEPS):
        iterate = iterate + search
        if sweep < SWEEPS - 1:
            shifted = np.concatenate([[0.0], search[:-1]])
            remain = remain - (CENTRE * search + HALF * shifted)
            following = 1.0 / (2.0 * spread - ratio)
            search = following * ratio * search + 2.0 * following / HALF * remain
            ratio = following
    return [float(v) for v in iterate]


A0, A1, A2, A3 = horner_terms()


def lane_of(n):
    return lax.broadcasted_iota(jnp.int32, (n, 8, 128), 2)


def z_up(f):
    r = pltpu.roll(f, 127, 2)
    return jnp.where(lane_of(f.shape[0]) == 127, pltpu.roll(r, 7, 1), r)


def z_down(f):
    r = pltpu.roll(f, 1, 2)
    return jnp.where(lane_of(f.shape[0]) == 0, pltpu.roll(r, 1, 1), r)


def z_end(n):
    return (lax.broadcasted_iota(jnp.int32, (n, 8, 128), 1) == 7) & (lane_of(n) == 127)


def z_face(q):
    return jnp.where(z_end(q.shape[0]), 0.0, q + z_up(q))


def side_fluxes(src, q, x, y, n):
    fe, qe = src[x, pl.ds(y - 1, n + 2)], q[x, pl.ds(y - 1, n + 2)]
    f, qc = fe[1:-1], qe[1:-1]
    fy = (fe[1:] - fe[:-1]) * (qe[1:] + qe[:-1])
    acc = fy[1:] - fy[:-1]
    acc += (src[x + 1, pl.ds(y, n)] - f) * (q[x + 1, pl.ds(y, n)] + qc)
    acc += (src[x - 1, pl.ds(y, n)] - f) * (q[x - 1, pl.ds(y, n)] + qc)
    return f, acc


def z_fluxes(f, faces):
    fz = (z_up(f) - f) * faces
    return fz - z_down(fz)


def fluxes(src, q, cz, x, y, n):
    f, acc = side_fluxes(src, q, x, y, n)
    return f, acc + z_fluxes(f, cz[x, pl.ds(y, n)])


def cover(low, high, n):
    starts = list(range(low, high - n + 1, n))
    if starts[-1] + n < high:
        starts.append(high - n)
    return starts


def early(margin, plane):
    def step(x, carry):
        plane(x)
        return carry

    lax.fori_loop(margin + D, EX - D - margin, step, 0)


def late(margin, plane):
    def step(i, carry):
        plane(jnp.where(i < D, margin + i, EX - 2 * D - margin + i))
        return carry

    lax.fori_loop(0, 2 * D, step, 0)


def lines(margin, n, step):
    def plane(x):
        for y in cover(margin, EY - margin, n):
            step(x, y, n)

    return plane


def put_py(field, py_low, py_high, out, scale):
    for ref, at in ((py_low, 0), (py_high, D + CY)):
        v = ref[field * HALO_Y : (field + 1) * HALO_Y, :]
        out[D : D + CX, at : at + D] = v.reshape(CX, D, 8, 128) * scale


def put_px(field, sides, out, scale):
    px_low, px_high, c_low, c_high = sides
    middle_y = slice(D, D + CY)
    planes = D if field == 0 else D - 1
    for ref, at in ((px_low, D - planes), (px_high, D + CX)):
        v = ref[PX_AT[field] : PX_AT[field] + planes * PLANE, :]
        out[at : at + planes, middle_y] = v.reshape(planes, CY, 8, 128) * scale
    blank = jnp.zeros((D, D, 8, 128), F32)
    for x, ref in ((0, c_low), (D + CX, c_high)):
        for side, y in enumerate((0, D + CY)):
            out[x : x + D, y : y + D] = blank
            for i, (dx, dy) in enumerate(CELLS):
                at = side * PART + field * HALO_C + i * 8
                cell_x = x + D - dx if x == 0 else x + dx - 1
                cell_y = y + D - dy if y == 0 else y + dy - 1
                out[cell_x, cell_y] = ref[at : at + 8, :] * scale


def far_planes(sides, bg, qp):
    middle_y = slice(D, D + CY)
    for ref, at, beside in ((sides[0], 0, 1), (sides[1], EX - 1, EX - 2)):
        flux = ref[PX_FLUX : PX_FLUX + PLANE, :].reshape(CY, 8, 128)
        bg[at, middle_y] = bg[beside, middle_y] + flux
        qp[at, middle_y] = 1.0 - qp[beside, middle_y]


def close_py(out, sign, planes):
    py, last_y = lax.axis_index("py"), lax.axis_size("py") - 1

    @pl.when(py == 0)
    def _():
        out[planes, D - 1] = out[planes, D] * sign

    @pl.when(py == last_y)
    def _():
        out[planes, D + CY] = out[planes, D + CY - 1] * sign


def first_solve(q, bg, qp, cz, bz, b, y1, y2):
    def whole(x, y, n):
        f, acc = side_fluxes(bg, qp, x, y, n)
        b[x, pl.ds(y, n)] = acc + z_fluxes(f, z_face(qp[x, pl.ds(y, n)]))
        cz[x, pl.ds(y, n)] = z_face(q[x, pl.ds(y, n)])

    def right_own(x):
        whole(x, 1, D - 1)
        whole(x, D + CY, D - 1)
        for y in cover(D, D + CY, 4):
            _, acc = side_fluxes(bg, qp, x, y, 4)
            b[x, pl.ds(y, 4)] = acc + bz[x - D, pl.ds(y - D, 4)]

    def second(x, y, n):
        f, acc = fluxes(b, q, cz, x, y, n)
        y1[x, pl.ds(y, n)] = (A2 - A3) * f - A3 * acc

    def third(x, y, n):
        f, acc = fluxes(y1, q, cz, x, y, n)
        y2[x, pl.ds(y, n)] = A1 * b[x, pl.ds(y, n)] - f - acc

    return lines(1, 4, whole), right_own, lines(2, 4, second), lines(3, 4, third)


def middle_kernel(
    py_low, py_high, after, bz, q_in, bg_in, qp_in, cz_in, q, bg, qp, cz, b, y1, y2
):
    del after, q_in, bg_in, qp_in, cz_in
    own = slice(D, D + CX)
    for field, out, scale, sign in ((0, q, 0.5 / HALF, -1.0), (1, bg, 1.0, 1.0), (2, qp, 0.5, -1.0)):
        put_py(field, py_low, py_high, out, scale)
        close_py(out, sign, own)
    _, right_own, second, third = first_solve(q, bg, qp, cz, bz, b, y1, y2)
    early(1, right_own)
    early(2, second)
    early(3, third)


def close_edges(out, sign):
    px, last_x = lax.axis_index("px"), lax.axis_size("px") - 1

    @pl.when(px == 0)
    def _():
        out[D - 1] = out[D] * sign

    @pl.when(px == last_x)
    def _():
        out[D + CX] = out[D + CX - 1] * sign

    close_py(out, sign, slice(0, EX))


def take_meta(ref, base, out):
    for c in range(8):
        lanes = slice(c * 128, (c + 1) * 128)
        out[0:8, lanes] = ref[base + c * 8 : base + c * 8 + 8, :]
        for i in range(2):
            at = base + 64 + i * 8 + c
            out[8 + i : 9 + i, lanes] = ref[at : at + 1, :]


def two_parts(v):
    high = v.astype(BF16)
    return high, (v - high.astype(F32)).astype(BF16)


def three_parts(v):
    high = v.astype(BF16)
    rest = v - high.astype(F32)
    mid = rest.astype(BF16)
    return high, mid, (rest - mid.astype(F32)).astype(BF16)


def one_hot(index, count):
    at = lax.broadcasted_iota(jnp.int32, (count, index.shape[1]), 0)
    return jnp.where(at == index, 1.0, 0.0).astype(BF16)


def rows16(index):
    shape = (16, index.shape[1])
    numbers = lax.broadcasted_iota(jnp.int32, shape, 0).astype(jnp.int16)
    return jnp.broadcast_to(index, shape).astype(jnp.int16), numbers


def put_one_hot(index, count, out, first, lanes):
    wanted, numbers = rows16(index)
    one, zero = jnp.ones(wanted.shape, BF16), jnp.zeros(wanted.shape, BF16)
    for r in range(count // 16):
        hit = numbers + jnp.int16(r * 16) == wanted
        out[first + r * 16 : first + (r + 1) * 16, lanes] = jnp.where(hit, one, zero)


def dot(a, b, over):
    return lax.dot_general(a, b, (over, ((), ())), preferred_element_type=F32)


def tangent_kernel(
    px_low,
    px_high,
    c_low,
    c_high,
    bz,
    meta,
    hot,
    weights,
    q_in,
    bg_in,
    qp_in,
    cz_in,
    b_in,
    y1_in,
    y2_in,
    out,
    q,
    bg,
    qp,
    cz,
    b,
    y1,
    y2,
    y3,
    table,
    vals,
):
    del q_in, bg_in, qp_in, cz_in, b_in, y1_in, y2_in
    sides = (px_low, px_high, c_low, c_high)
    put_px(0, sides, q, 0.5 / HALF)
    put_px(1, sides, bg, 1.0)
    put_px(2, sides, qp, 0.5)
    far_planes(sides, bg, qp)
    close_edges(q, -1.0)
    close_edges(qp, -1.0)
    close_edges(bg, 1.0)
    right, right_own, second, third = first_solve(q, bg, qp, cz, bz, b, y1, y2)

    def outer_planes(i, carry):
        right(jnp.where(i < D - 1, 1 + i, CX + 1 + i))
        return carry

    def edge_planes(i, carry):
        right_own(D + i * (CX - 1))
        return carry

    lax.fori_loop(0, 2 * (D - 1), outer_planes, 0)
    lax.fori_loop(0, 2, edge_planes, 0)
    late(2, second)
    late(3, third)

    def fourth(x, y, n):
        f, acc = fluxes(y2, q, cz, x, y, n)
        y3[x, pl.ds(y, n)] = A0 * b[x, pl.ds(y, n)] - f - acc

    late(4, lines(4, 4, fourth))

    flat = y3.reshape(EX * EY * 8, 128)
    for x in range(CX):
        for c in range(8):
            v = flat[pl.ds(((x + D) * EY + D) * 8 + c, CY, stride=8), :]
            high, low = two_parts(v)
            table[x * CY : (x + 1) * CY, c * 128 : (c + 1) * 128] = high
            table[CX * CY + x * CY : CX * CY + (x + 1) * CY, c * 128 : (c + 1) * 128] = low

    vals[...] = jnp.zeros_like(vals)

    def gather(k, carry):
        node = meta[pl.ds(k, 1), :].astype(jnp.int32)
        lanes = pl.ds(pl.multiple_of(k * 1024, 1024), 1024)
        found = dot(table[...], hot[:, lanes], ((1,), (0,)))
        found = found[: CX * CY] + found[CX * CY :]
        at = lax.broadcasted_iota(jnp.int32, found.shape, 0)
        found = jnp.sum(jnp.where(at == node >> 10, found, 0.0), axis=0, keepdims=True)
        vals[0:1, :] += meta[pl.ds(k + 4, 1), :] * found
        return carry

    lax.fori_loop(0, 4, gather, 0)

    owner, sensor = meta[8:9, :].astype(jnp.int32), meta[9:10, :].astype(jnp.int32)
    at = lax.broadcasted_iota(jnp.int32, (8, 1024), 0)
    owned = jnp.where(at == sensor, vals[0:1, :], 0.0)
    parts = jnp.concatenate(three_parts(owned), axis=0)
    sums = dot(parts, one_hot(owner, 128), ((1,), (1,)))
    readings = sums[0:8] + sums[8:16] + sums[16:24]
    block = jnp.concatenate([readings, weights[...]] * 8, axis=0)
    for i in range(out.shape[0] // 72):
        out[i * 72 : (i + 1) * 72, :] = block


def scatter(meta, values, rows, per, tiles, width, lhs, keep, hot):
    for k in range(4):
        wanted, numbers = rows16(rows(meta[k : k + 1, :].astype(jnp.int32)))
        value = jnp.broadcast_to(values[k : k + 1, :], wanted.shape)
        high, low = two_parts(value)
        zero = jnp.zeros(wanted.shape, BF16)
        lanes = slice(k * 1024, (k + 1) * 1024)
        for r in range(per // 16):
            hit = numbers + jnp.int16(r * 16) == wanted
            lhs[r * 16 : (r + 1) * 16, lanes] = jnp.where(hit, high, zero)
            lhs[per + r * 16 : per + (r + 1) * 16, lanes] = jnp.where(hit, low, zero)

    def tile(t, carry):
        total = None
        for k in range(4):
            lanes = slice(k * 1024, (k + 1) * 1024)
            hits = hot[pl.ds(pl.multiple_of(t * width, width), width), lanes]
            part = dot(lhs[0 : 2 * per, lanes], hits, ((1,), (1,)))
            total = part if total is None else total + part
        keep(t, total[0:per] + total[per : 2 * per])
        return carry

    if tiles == 1:
        tile(0, 0)
    else:
        lax.fori_loop(0, tiles, tile, 0)


def returned(weighted, table, values):
    owner, sensor = table[8:9, :].astype(jnp.int32), table[9:10, :].astype(jnp.int32)
    parts = jnp.concatenate(three_parts(weighted), axis=0)
    found = dot(parts, one_hot(owner, 128), ((1,), (0,)))
    found = found[0:8] + found[8:16] + found[16:24]
    at = lax.broadcasted_iota(jnp.int32, found.shape, 0)
    found = jnp.sum(jnp.where(at == sensor, found, 0.0), axis=0, keepdims=True)
    values[0:4, :] = table[4:8, :] * found


def source_kernel(got, meta, hot, weighted, own, low, high, lhs, values):
    count = got.shape[0] // 9
    sums = [jnp.sum(got[pl.ds(i, count, stride=9), :], axis=0, keepdims=True) for i in range(8)]
    readings = jnp.concatenate(sums, axis=0)
    weights = jnp.transpose(got[pl.ds(8, count, stride=9), :])[0:8]
    weighted[...] = readings * weights

    def keep(t, sums):
        for x in range(CX):
            for i in range(4):
                block = sums[x * CY : (x + 1) * CY, i * 128 : (i + 1) * 128]
                own[pl.ds(x * PLANE + t * 4 + i, CY, stride=8), :] = block
                side, at = (low, x) if x < D else (high, x - (CX - D))
                side[pl.ds(at * PLANE + t * 4 + i, CY, stride=8), :] = block

    returned(weighted[...], meta, values)
    scatter(meta, values, lambda n: n >> 10, CX * CY, 2, 512, lhs, keep, hot)


def second_solve(src, q, cz, y1, y2, y3):
    def first(x, y, n):
        f, acc = fluxes(src, q, cz, x, y, n)
        y1[x, pl.ds(y, n)] = (A2 - A3) * f - A3 * acc

    def second(x, y, n):
        f, acc = fluxes(y1, q, cz, x, y, n)
        y2[x, pl.ds(y, n)] = A1 * src[x, pl.ds(y, n)] - f - acc

    def third(x, y, n):
        f, acc = fluxes(y2, q, cz, x, y, n)
        y3[x, pl.ds(y, n)] = A0 * src[x, pl.ds(y, n)] - f - acc

    return lines(1, 4, first), lines(2, 4, second), lines(3, 4, third)


def strips_kernel(
    weighted,
    py_low,
    py_high,
    c_low,
    c_high,
    own,
    q,
    cz,
    src,
    y1,
    y2,
    y3,
    lhs,
    near_hot,
    near,
    values,
):
    src[D : D + CX, D : D + CY] = own[...].reshape(CX, CY, 8, 128)
    flat = src.reshape(EX * EY * 8, 128)

    def columns(count):
        for k in range(4):
            node = near[k : k + 1, :].astype(jnp.int32)
            put_one_hot(node & (count - 1), count, near_hot, 0, slice(k * 1024, (k + 1) * 1024))

    for ref, y0, first_y in ((py_low, 0, CY - D), (py_high, D + CY, 0)):
        take_meta(ref, 3 * HALO_Y, near)
        returned(weighted[...], near, values)
        columns(256)

        def rows(node, first_y=first_y):
            x, y = node >> 15, ((node >> 10) & (CY - 1)) - first_y
            good = (y >= 0) & (y < D)
            return jnp.where(good, (((node >> 8) & 3) * CX + x) * D + y, -1)

        def keep(t, sums, y0=y0):
            for zq in range(4):
                for x in range(CX):
                    first = (zq * CX + x) * D
                    for half in range(2):
                        flat[
                            pl.ds(((x + D) * EY + y0) * 8 + zq * 2 + half, D, stride=8), :
                        ] = sums[first : first + D, half * 128 : (half + 1) * 128]

        scatter(near, values, rows, 4 * CX * D, 1, 256, lhs, keep, near_hot)

    for ref, x_low in ((c_low, True), (c_high, False)):
        for side, y_low in enumerate((True, False)):
            take_meta(ref, side * PART + 3 * HALO_C, near)
            returned(weighted[...], near, values)
            columns(128)

            def rows(node, x_low=x_low, y_low=y_low):
                x, y = node >> 15, (node >> 10) & (CY - 1)
                dx = CX - x if x_low else x + 1
                dy = CY - y if y_low else y + 1
                cell = jnp.where(dx == 1, dy - 1, jnp.where(dx == 2, dy + 2, 5))
                return jnp.where(dx + dy <= D, ((node >> 7) & 7) * len(CELLS) + cell, -1)

            def keep(t, sums, x_low=x_low, y_low=y_low):
                x0, y0 = 0 if x_low else D + CX, 0 if y_low else D + CY
                src[x0 : x0 + D, y0 : y0 + D] = jnp.zeros((D, D, 8, 128), F32)
                for i, (dx, dy) in enumerate(CELLS):
                    x = D - dx if x_low else D + CX + dx - 1
                    y = D - dy if y_low else D + CY + dy - 1
                    for c in range(8):
                        row = c * len(CELLS) + i
                        flat[(x * EY + y) * 8 + c : (x * EY + y) * 8 + c + 1, :] = sums[
                            row : row + 1, :
                        ]

            scatter(near, values, rows, 8 * len(CELLS), 1, 128, lhs, keep, near_hot)

    first, second, third = second_solve(src, q, cz, y1, y2, y3)
    early(1, first)
    early(2, second)
    early(3, third)


def adjoint_kernel(
    px_low, px_high, q, bg, cz, dz, src_in, y1_in, y2_in, y3_in, out_hbm, src, y1, y2, y3, out, sems
):
    del src_in, y1_in, y2_in, y3_in
    for x, ref in ((0, px_low), (D + CX, px_high)):
        src[x : x + D, D : D + CY] = ref[...].reshape(D, CY, 8, 128)
    first, second, third = second_solve(src, q, cz, y1, y2, y3)
    late(1, first)
    late(2, second)
    late(3, third)

    def last(x, y, n):
        ae, be = y3[x, pl.ds(y - 1, n + 2)], bg[x, pl.ds(y - 1, n + 2)]
        a, k = ae[1:-1], be[1:-1]
        sy = (ae[1:] - ae[:-1]) * (be[1:] - be[:-1])
        total = sy[1:] + sy[:-1]
        total += (y3[x + 1, pl.ds(y, n)] - a) * (bg[x + 1, pl.ds(y, n)] - k)
        total += (y3[x - 1, pl.ds(y, n)] - a) * (bg[x - 1, pl.ds(y, n)] - k)
        sz = (z_up(a) - a) * dz[x - D, pl.ds(y - D, n)]
        total = -0.5 * (total + (sz + z_down(sz)))
        yy = y - D
        for i in range(n):
            row = (x - D) * (CY // 8) + (yy + i) // 8
            out[pl.ds(row * 64 + (yy + i) % 8, 8, stride=8), :] = total[i]

    def leave(x):
        i = x - D
        at = pl.ds(pl.multiple_of(i * PLANE, PLANE), PLANE)
        return pltpu.make_async_copy(out.at[at], out_hbm.at[at], sems.at[i])

    compute = lines(4, 4, last)

    def plane(x):
        compute(x)
        leave(x).start()

    late(4, plane)
    for x in range(D, D + CX):
        leave(x).wait()


def by_tiles(block):
    lead = block.shape[:-2]
    rows, cols = block.shape[-2:]
    split = block.reshape(*lead, rows // 8, 8, cols // 128, 128)
    return jnp.swapaxes(split, -3, -2).reshape(-1, 128)


def from_tiles(rows):
    split = rows.reshape(CX, CY // 8, CZ // 128, 8, 128)
    return jnp.swapaxes(split, -3, -2).reshape(CX, CY, CZ)


def row_of(ref, x, y):
    return ref[pl.ds((x * (CY // 8) + y // 8) * 64 + y % 8, 8, stride=8), :]


def line_of(ref, x, y):
    return ref[pl.ds((x * (CY // 8) + y // 8) * 64 + y % 8, 8, stride=8), :]


def pack_kernel(
    permit_hbm,
    back_hbm,
    perturb_hbm,
    nodes_hbm,
    weights_hbm,
    owner_hbm,
    sensor_hbm,
    low_x,
    high_x,
    low_y,
    high_y,
    meta,
    permit,
    back,
    perturb,
    nodes,
    weights,
    owner,
    sensor,
    sems,
):
    pairs = (
        (nodes_hbm, nodes),
        (weights_hbm, weights),
        (owner_hbm, owner),
        (sensor_hbm, sensor),
        (permit_hbm, permit),
        (back_hbm, back),
        (perturb_hbm, perturb),
    )
    copies = [pltpu.make_async_copy(a, b, sems.at[i]) for i, (a, b) in enumerate(pairs)]
    for copy in copies:
        copy.start()
    for copy in copies[:4]:
        copy.wait()
    meta[0:4, :] = nodes[...].astype(F32)
    meta[4:8, :] = weights[...]
    meta[8:9, :] = owner[...].astype(F32)
    meta[9:10, :] = sensor[...].astype(F32)
    meta[10:16, :] = jnp.zeros((6, 1024), F32)
    for out, at in ((low_y, 3 * HALO_Y), (high_y, 3 * HALO_Y)):
        for c in range(8):
            lanes = slice(c * 128, (c + 1) * 128)
            out[at + c * 8 : at + c * 8 + 8, :] = meta[0:8, lanes]
            for i in range(2):
                out[at + 64 + i * 8 + c : at + 65 + i * 8 + c, :] = meta[8 + i : 9 + i, lanes]

    for field, ref in enumerate((permit, back, perturb)):
        copies[4 + field].wait()
        planes = D if field == 0 else D - 1

        def plane(x, carry, field=field, ref=ref, planes=planes):
            for y in range(CY):
                at = pl.ds(PX_AT[field] + (x * CY + y) * 8, 8)
                low_x[at, :] = row_of(ref, x, y)
                high_x[at, :] = row_of(ref, x + CX - planes, y)
            return carry

        lax.fori_loop(0, planes, plane, 0)
        for x in range(CX):
            for y in range(D):
                at = pl.ds(field * HALO_Y + (x * D + y) * 8, 8)
                low_y[at, :] = row_of(ref, x, y)
                high_y[at, :] = row_of(ref, x, y + CY - D)

    def flux(y, carry):
        for out, near, far in ((low_x, D - 2, D - 1), (high_x, CX - D + 1, CX - D)):
            face = 0.5 * (line_of(perturb, near, y) + line_of(perturb, far, y))
            at = pl.ds(pl.multiple_of(PX_FLUX + y * 8, 8), 8)
            out[at, :] = face * (line_of(back, far, y) - line_of(back, near, y))
        return carry

    lax.fori_loop(0, CY, flux, 0)


def own_kernel(
    permit_hbm,
    back_hbm,
    perturb_hbm,
    meta,
    q,
    bg,
    qp,
    cz,
    bz,
    dz,
    hot,
    permit,
    back,
    perturb,
    sems,
):
    pairs = ((permit_hbm, permit), (back_hbm, back), (perturb_hbm, perturb))
    copies = [pltpu.make_async_copy(a, b, sems.at[i]) for i, (a, b) in enumerate(pairs)]
    for copy in copies:
        copy.start()

    def entries(i, carry):
        k, lanes = i // 2, pl.ds(pl.multiple_of((i % 2) * 512, 512), 512)
        node = meta[pl.ds(k, 1), lanes].astype(jnp.int32)
        at = pl.ds(pl.multiple_of(i * 512, 512), 512)
        put_one_hot(node & (CZ - 1), CZ, hot, 0, at)
        return carry

    lax.fori_loop(0, 8, entries, 0)
    for copy in copies:
        copy.wait()

    def plane(x, carry):
        for y in range(CY):
            q[x + D, y + D] = row_of(permit, x, y) * (0.5 / HALF)
            bg[x + D, y + D] = row_of(back, x, y)
            qp[x + D, y + D] = row_of(perturb, x, y) * 0.5
        for y in range(0, CY, 4):
            at = pl.ds(y + D, 4)
            cz[x + D, at] = z_face(q[x + D, at])
            field = bg[x + D, at]
            step = jnp.where(z_end(4), 0.0, z_up(field) - field)
            dz[x, pl.ds(y, 4)] = step
            fz = step * z_face(qp[x + D, at])
            bz[x, pl.ds(y, 4)] = fz - z_down(fz)
        return carry

    lax.fori_loop(0, CX, plane, 0)


def corner_kernel(py_low, py_high, after, low, high):
    del after
    for side, ref in enumerate((py_low, py_high)):
        for field in range(3):
            for i, (dx, dy) in enumerate(CELLS):
                y = D - dy if side == 0 else dy - 1
                at = side * PART + field * HALO_C + i * 8
                for out, x in ((low, dx - 1), (high, CX - dx)):
                    first = field * HALO_Y + (x * D + y) * 8
                    out[at : at + 8, :] = ref[first : first + 8, :]
        at = side * PART + 3 * HALO_C
        low[at : at + META, :] = ref[3 * HALO_Y :, :]
        high[at : at + META, :] = ref[3 * HALO_Y :, :]


def vmem(count):
    return [pl.BlockSpec(memory_space=pltpu.VMEM)] * count


def shift(x, axis, by):
    count = lax.axis_size(axis)
    return lax.ppermute(x, axis, [(i, (i + by) % count) for i in range(count)])


def body(
    background_field,
    perturbation,
    permittivity,
    probe_nodes,
    probe_weights,
    probe_owner,
    probe_sensor,
    sensor_weight,
):
    devices = lax.axis_size("px") * lax.axis_size("py")
    fields = [by_tiles(f) for f in (permittivity, background_field, perturbation)]
    weights = jnp.pad(sensor_weight, (0, 128 - sensor_weight.shape[0]))[None, :]

    def rows(*counts):
        return [jax.ShapeDtypeStruct((n, 128), F32) for n in counts]

    def call(kernel, outs, *args, hbm=0, away=0, passed=0, at=1, scratch=(), limit, bytes_accessed=0):
        held = [pltpu.with_memory_space_constraint(a, pltpu.HBM) for a in args[:hbm]]
        args = held + list(args[hbm:])
        return pl.pallas_call(
            kernel,
            out_shape=tuple(outs),
            in_specs=[pl.BlockSpec(memory_space=pltpu.HBM)] * hbm + vmem(len(args) - hbm),
            out_specs=tuple(
                [pl.BlockSpec(memory_space=pl.ANY)] * away + vmem(len(outs) - away)
            ),
            scratch_shapes=scratch,
            input_output_aliases={len(args) - passed + i: at + i for i in range(passed)},
            compiler_params=pltpu.CompilerParams(vmem_limit_bytes=limit * 2**20),
            cost_estimate=pl.CostEstimate(
                flops=0, bytes_accessed=bytes_accessed, transcendentals=0
            ),
        )(*args)

    size_x, size_y, size_c = PX_ROWS, 3 * HALO_Y + META, 2 * PART
    raw = [pltpu.VMEM((ROWS, 128), F32)] * 3
    table = jax.ShapeDtypeStruct((16, 1024), F32)
    low_x, high_x, low_y, high_y, meta = call(
        pack_kernel,
        rows(size_x, size_x, size_y, size_y) + [table],
        *fields,
        probe_nodes,
        probe_weights,
        probe_owner.reshape(1, -1),
        probe_sensor.reshape(1, -1),
        hbm=7,
        scratch=raw
        + [
            pltpu.VMEM((4, 1024), jnp.int32),
            pltpu.VMEM((4, 1024), F32),
            pltpu.VMEM((1, 1024), jnp.int32),
            pltpu.VMEM((1, 1024), jnp.int32),
            pltpu.SemaphoreType.DMA((7,)),
        ],
        limit=6,
    )
    px_low, px_high = shift(high_x, "px", 1), shift(low_x, "px", -1)
    py_low, py_high = shift(high_y, "py", 1), shift(low_y, "py", -1)
    compact = jax.ShapeDtypeStruct((CX, CY, 8, 128), F32)
    full = jax.ShapeDtypeStruct((EX, EY, 8, 128), F32)
    q, bg, qp, cz, bz, dz, hot = call(
        own_kernel,
        [full] * 4 + [compact] * 2 + [jax.ShapeDtypeStruct((CZ, 4096), BF16)],
        *fields,
        meta,
        hbm=3,
        scratch=raw + [pltpu.SemaphoreType.DMA((3,))],
        limit=10,
        bytes_accessed=8 * 2**20,
    )
    low_c, high_c = call(corner_kernel, rows(size_c, size_c), py_low, py_high, bz, limit=4)
    c_low, c_high = shift(high_c, "px", 1), shift(low_c, "px", -1)
    q, bg, qp, cz, b, y1, y2 = call(
        middle_kernel,
        [full] * 7,
        py_low,
        py_high,
        low_c,
        bz,
        q,
        bg,
        qp,
        cz,
        passed=4,
        at=0,
        limit=6,
        bytes_accessed=8 * 2**20,
    )
    block = pltpu.VMEM((EX, EY, 8, 128), F32)
    readings, q, bg, qp, cz, b, y1, y2 = call(
        tangent_kernel,
        rows(devices * 9) + [full] * 7,
        px_low,
        px_high,
        c_low,
        c_high,
        bz,
        meta,
        hot,
        weights,
        q,
        bg,
        qp,
        cz,
        b,
        y1,
        y2,
        passed=7,
        scratch=[block, pltpu.VMEM((2 * CX * CY, CZ), BF16), pltpu.VMEM((8, 1024), F32)],
        limit=20,
    )
    got = lax.all_to_all(
        readings.reshape(devices, 1, 9 * 128),
        ("px", "py"),
        split_axis=0,
        concat_axis=0,
        tiled=True,
    ).reshape(devices * 9, 128)
    weighted, own_source, low_s, high_s = call(
        source_kernel,
        rows(8, ROWS, D * PLANE, D * PLANE),
        got,
        meta,
        hot,
        scratch=[pltpu.VMEM((2 * CX * CY, 4096), BF16), pltpu.VMEM((8, 1024), F32)],
        limit=18,
    )
    source_low, source_high = shift(high_s, "px", 1), shift(low_s, "px", -1)
    src, y1, y2, y3 = call(
        strips_kernel,
        [full] * 4,
        weighted,
        py_low,
        py_high,
        c_low,
        c_high,
        own_source,
        q,
        cz,
        scratch=[
            pltpu.VMEM((2 * 4 * CX * D, 4096), BF16),
            pltpu.VMEM((256, 4096), BF16),
            pltpu.VMEM((16, 1024), F32),
            pltpu.VMEM((8, 1024), F32),
        ],
        limit=16,
        bytes_accessed=24 * 2**20,
    )
    result = call(
        adjoint_kernel,
        rows(ROWS) + [full] * 4,
        source_low,
        source_high,
        q,
        bg,
        cz,
        dz,
        src,
        y1,
        y2,
        y3,
        passed=4,
        away=1,
        scratch=[pltpu.VMEM((ROWS, 128), F32), pltpu.SemaphoreType.DMA((CX,))],
        limit=8,
    )[0]
    return from_tiles(result)


def solution(mesh):
    placed = (
        P("px", "py", None),
        P("px", "py", None),
        P("px", "py", None),
        P(None, ("px", "py")),
        P(None, ("px", "py")),
        P(("px", "py"), None),
        P(("px", "py")),
        P(("px", "py")),
    )
    return jax.shard_map(
        body, mesh=mesh, in_specs=placed, out_specs=P("px", "py", None), check_vma=False
    )
```

```python
import jax
import jax.numpy as jnp
import numpy as np
from jax import lax
from jax.experimental import pallas as pl
from jax.experimental.pallas import tpu as pltpu
from jax.sharding import PartitionSpec as P

SWEEPS = 4
MASS = 1.0
LOW = 1.0
HIGH = 25.0
CENTRE = 0.5 * (HIGH + LOW)
HALF = 0.5 * (HIGH - LOW)

CX, CY, CZ = 8, 32, 1024
D = 4
EX, EY = CX + 2 * D, CY + 2 * D
ROWS = CX * CY * 8
PLANE = CY * 8
PX_AT = (0, D * PLANE, (2 * D - 1) * PLANE)
PX_FLUX = (3 * D - 2) * PLANE
PX_ROWS = (3 * D - 1) * PLANE
HALO_Y = CX * D * 8
CELLS = tuple((dx, dy) for dx in range(1, D) for dy in range(1, D) if dx + dy <= D)
HALO_C = len(CELLS) * 8
META = 80
PART = 3 * HALO_C + META
F32 = jnp.float32
BF16 = jnp.bfloat16


def horner_terms():
    spread = CENTRE / HALF
    size = SWEEPS
    iterate = np.zeros(size)
    remain = np.eye(size)[0]
    search = remain / CENTRE
    ratio = 1.0 / spread
    for sweep in range(SWEEPS):
        iterate = iterate + search
        if sweep < SWEEPS - 1:
            shifted = np.concatenate([[0.0], search[:-1]])
            remain = remain - (CENTRE * search + HALF * shifted)
            following = 1.0 / (2.0 * spread - ratio)
            search = following * ratio * search + 2.0 * following / HALF * remain
            ratio = following
    return [float(v) for v in iterate]


A0, A1, A2, A3 = horner_terms()


def lane_of(n):
    return lax.broadcasted_iota(jnp.int32, (n, 8, 128), 2)


def z_up(f):
    r = pltpu.roll(f, 127, 2)
    return jnp.where(lane_of(f.shape[0]) == 127, pltpu.roll(r, 7, 1), r)


def z_down(f):
    r = pltpu.roll(f, 1, 2)
    return jnp.where(lane_of(f.shape[0]) == 0, pltpu.roll(r, 1, 1), r)


def z_end(n):
    return (lax.broadcasted_iota(jnp.int32, (n, 8, 128), 1) == 7) & (lane_of(n) == 127)


def z_face(q):
    return jnp.where(z_end(q.shape[0]), 0.0, q + z_up(q))


def side_fluxes(src, q, x, y, n):
    fe, qe = src[x, pl.ds(y - 1, n + 2)], q[x, pl.ds(y - 1, n + 2)]
    f, qc = fe[1:-1], qe[1:-1]
    fy = (fe[1:] - fe[:-1]) * (qe[1:] + qe[:-1])
    acc = fy[1:] - fy[:-1]
    acc += (src[x + 1, pl.ds(y, n)] - f) * (q[x + 1, pl.ds(y, n)] + qc)
    acc += (src[x - 1, pl.ds(y, n)] - f) * (q[x - 1, pl.ds(y, n)] + qc)
    return f, acc


def z_fluxes(f, faces):
    fz = (z_up(f) - f) * faces
    return fz - z_down(fz)


def fluxes(src, q, cz, x, y, n):
    f, acc = side_fluxes(src, q, x, y, n)
    return f, acc + z_fluxes(f, cz[x, pl.ds(y, n)])


def cover(low, high, n):
    starts = list(range(low, high - n + 1, n))
    if starts[-1] + n < high:
        starts.append(high - n)
    return starts


def early(margin, plane):
    def step(x, carry):
        plane(x)
        return carry

    lax.fori_loop(margin + D, EX - D - margin, step, 0)


def late(margin, plane):
    def step(i, carry):
        plane(jnp.where(i < D, margin + i, EX - 2 * D - margin + i))
        return carry

    lax.fori_loop(0, 2 * D, step, 0)


def lines(margin, n, step):
    def plane(x):
        for y in cover(margin, EY - margin, n):
            step(x, y, n)

    return plane


def put_py(field, py_low, py_high, out, scale):
    for ref, at in ((py_low, 0), (py_high, D + CY)):
        v = ref[field * HALO_Y : (field + 1) * HALO_Y, :]
        out[D : D + CX, at : at + D] = v.reshape(CX, D, 8, 128) * scale


def put_px(field, sides, out, scale):
    px_low, px_high, c_low, c_high = sides
    middle_y = slice(D, D + CY)
    planes = D if field == 0 else D - 1
    for ref, at in ((px_low, D - planes), (px_high, D + CX)):
        v = ref[PX_AT[field] : PX_AT[field] + planes * PLANE, :]
        out[at : at + planes, middle_y] = v.reshape(planes, CY, 8, 128) * scale
    blank = jnp.zeros((D, D, 8, 128), F32)
    for x, ref in ((0, c_low), (D + CX, c_high)):
        for side, y in enumerate((0, D + CY)):
            out[x : x + D, y : y + D] = blank
            for i, (dx, dy) in enumerate(CELLS):
                at = side * PART + field * HALO_C + i * 8
                cell_x = x + D - dx if x == 0 else x + dx - 1
                cell_y = y + D - dy if y == 0 else y + dy - 1
                out[cell_x, cell_y] = ref[at : at + 8, :] * scale


def far_planes(sides, bg, qp):
    middle_y = slice(D, D + CY)
    for ref, at, beside in ((sides[0], 0, 1), (sides[1], EX - 1, EX - 2)):
        flux = ref[PX_FLUX : PX_FLUX + PLANE, :].reshape(CY, 8, 128)
        bg[at, middle_y] = bg[beside, middle_y] + flux
        qp[at, middle_y] = 1.0 - qp[beside, middle_y]


def close_py(out, sign, planes):
    py, last_y = lax.axis_index("py"), lax.axis_size("py") - 1

    @pl.when(py == 0)
    def _():
        out[planes, D - 1] = out[planes, D] * sign

    @pl.when(py == last_y)
    def _():
        out[planes, D + CY] = out[planes, D + CY - 1] * sign


def first_solve(q, bg, qp, cz, bz, b, y1, y2):
    def whole(x, y, n):
        f, acc = side_fluxes(bg, qp, x, y, n)
        b[x, pl.ds(y, n)] = acc + z_fluxes(f, z_face(qp[x, pl.ds(y, n)]))
        cz[x, pl.ds(y, n)] = z_face(q[x, pl.ds(y, n)])

    def right_own(x):
        whole(x, 1, D - 1)
        whole(x, D + CY, D - 1)
        for y in cover(D, D + CY, 4):
            _, acc = side_fluxes(bg, qp, x, y, 4)
            b[x, pl.ds(y, 4)] = acc + bz[x - D, pl.ds(y - D, 4)]

    def second(x, y, n):
        f, acc = fluxes(b, q, cz, x, y, n)
        y1[x, pl.ds(y, n)] = (A2 - A3) * f - A3 * acc

    def third(x, y, n):
        f, acc = fluxes(y1, q, cz, x, y, n)
        y2[x, pl.ds(y, n)] = A1 * b[x, pl.ds(y, n)] - f - acc

    return lines(1, 4, whole), right_own, lines(2, 4, second), lines(3, 4, third)


def middle_kernel(
    py_low, py_high, after, bz, q_in, bg_in, qp_in, cz_in, q, bg, qp, cz, b, y1, y2
):
    del after, q_in, bg_in, qp_in, cz_in
    own = slice(D, D + CX)
    for field, out, scale, sign in ((0, q, 0.5 / HALF, -1.0), (1, bg, 1.0, 1.0), (2, qp, 0.5, -1.0)):
        put_py(field, py_low, py_high, out, scale)
        close_py(out, sign, own)
    _, right_own, second, third = first_solve(q, bg, qp, cz, bz, b, y1, y2)
    early(1, right_own)
    early(2, second)
    early(3, third)


def close_edges(out, sign):
    px, last_x = lax.axis_index("px"), lax.axis_size("px") - 1

    @pl.when(px == 0)
    def _():
        out[D - 1] = out[D] * sign

    @pl.when(px == last_x)
    def _():
        out[D + CX] = out[D + CX - 1] * sign

    close_py(out, sign, slice(0, EX))


def take_meta(ref, base, out):
    for c in range(8):
        lanes = slice(c * 128, (c + 1) * 128)
        out[0:8, lanes] = ref[base + c * 8 : base + c * 8 + 8, :]
        for i in range(2):
            at = base + 64 + i * 8 + c
            out[8 + i : 9 + i, lanes] = ref[at : at + 1, :]


def two_parts(v):
    high = v.astype(BF16)
    return high, (v - high.astype(F32)).astype(BF16)


def three_parts(v):
    high = v.astype(BF16)
    rest = v - high.astype(F32)
    mid = rest.astype(BF16)
    return high, mid, (rest - mid.astype(F32)).astype(BF16)


def one_hot(index, count):
    at = lax.broadcasted_iota(jnp.int32, (count, index.shape[1]), 0)
    return jnp.where(at == index, 1.0, 0.0).astype(BF16)


def rows16(index):
    shape = (16, index.shape[1])
    numbers = lax.broadcasted_iota(jnp.int32, shape, 0).astype(jnp.int16)
    return jnp.broadcast_to(index, shape).astype(jnp.int16), numbers


def put_one_hot(index, count, out, first, lanes):
    wanted, numbers = rows16(index)
    one, zero = jnp.ones(wanted.shape, BF16), jnp.zeros(wanted.shape, BF16)
    for r in range(count // 16):
        hit = numbers + jnp.int16(r * 16) == wanted
        out[first + r * 16 : first + (r + 1) * 16, lanes] = jnp.where(hit, one, zero)


def dot(a, b, over):
    return lax.dot_general(a, b, (over, ((), ())), preferred_element_type=F32)


def tangent_kernel(
    px_low,
    px_high,
    c_low,
    c_high,
    bz,
    meta,
    hot,
    weights,
    q_in,
    bg_in,
    qp_in,
    cz_in,
    b_in,
    y1_in,
    y2_in,
    out,
    q,
    bg,
    qp,
    cz,
    b,
    y1,
    y2,
    y3,
    table,
    vals,
):
    del q_in, bg_in, qp_in, cz_in, b_in, y1_in, y2_in
    sides = (px_low, px_high, c_low, c_high)
    put_px(0, sides, q, 0.5 / HALF)
    put_px(1, sides, bg, 1.0)
    put_px(2, sides, qp, 0.5)
    far_planes(sides, bg, qp)
    close_edges(q, -1.0)
    close_edges(qp, -1.0)
    close_edges(bg, 1.0)
    right, right_own, second, third = first_solve(q, bg, qp, cz, bz, b, y1, y2)

    def outer_planes(i, carry):
        right(jnp.where(i < D - 1, 1 + i, CX + 1 + i))
        return carry

    def edge_planes(i, carry):
        right_own(D + i * (CX - 1))
        return carry

    lax.fori_loop(0, 2 * (D - 1), outer_planes, 0)
    lax.fori_loop(0, 2, edge_planes, 0)
    late(2, second)
    late(3, third)

    def fourth(x, y, n):
        f, acc = fluxes(y2, q, cz, x, y, n)
        y3[x, pl.ds(y, n)] = A0 * b[x, pl.ds(y, n)] - f - acc

    late(4, lines(4, 4, fourth))

    flat = y3.reshape(EX * EY * 8, 128)
    for x in range(CX):
        for c in range(8):
            v = flat[pl.ds(((x + D) * EY + D) * 8 + c, CY, stride=8), :]
            high, low = two_parts(v)
            table[x * CY : (x + 1) * CY, c * 128 : (c + 1) * 128] = high
            table[CX * CY + x * CY : CX * CY + (x + 1) * CY, c * 128 : (c + 1) * 128] = low

    vals[...] = jnp.zeros_like(vals)

    def gather(k, carry):
        node = meta[pl.ds(k, 1), :].astype(jnp.int32)
        lanes = pl.ds(pl.multiple_of(k * 1024, 1024), 1024)
        found = dot(table[...], hot[:, lanes], ((1,), (0,)))
        found = found[: CX * CY] + found[CX * CY :]
        at = lax.broadcasted_iota(jnp.int32, found.shape, 0)
        found = jnp.sum(jnp.where(at == node >> 10, found, 0.0), axis=0, keepdims=True)
        vals[0:1, :] += meta[pl.ds(k + 4, 1), :] * found
        return carry

    lax.fori_loop(0, 4, gather, 0)

    owner, sensor = meta[8:9, :].astype(jnp.int32), meta[9:10, :].astype(jnp.int32)
    at = lax.broadcasted_iota(jnp.int32, (8, 1024), 0)
    owned = jnp.where(at == sensor, vals[0:1, :], 0.0)
    parts = jnp.concatenate(three_parts(owned), axis=0)
    sums = dot(parts, one_hot(owner, 128), ((1,), (1,)))
    readings = sums[0:8] + sums[8:16] + sums[16:24]
    block = jnp.concatenate([readings, weights[...]] * 8, axis=0)
    for i in range(out.shape[0] // 72):
        out[i * 72 : (i + 1) * 72, :] = block


def put_values(meta, values, rows, per, lhs):
    for k in range(4):
        wanted, numbers = rows16(rows(meta[k : k + 1, :].astype(jnp.int32)))
        value = jnp.broadcast_to(values[k : k + 1, :], wanted.shape)
        high, low = two_parts(value)
        zero = jnp.zeros(wanted.shape, BF16)
        lanes = slice(k * 1024, (k + 1) * 1024)
        for r in range(per // 16):
            hit = numbers + jnp.int16(r * 16) == wanted
            lhs[r * 16 : (r + 1) * 16, lanes] = jnp.where(hit, high, zero)
            lhs[per + r * 16 : per + (r + 1) * 16, lanes] = jnp.where(hit, low, zero)


def add_up(per, first, width, lhs, hot):
    total = None
    for k in range(4):
        lanes = slice(k * 1024, (k + 1) * 1024)
        part = dot(lhs[0 : 2 * per, lanes], hot[first : first + width, lanes], ((1,), (1,)))
        total = part if total is None else total + part
    return total[0:per] + total[per : 2 * per]


def returned(weighted, table, values):
    owner, sensor = table[8:9, :].astype(jnp.int32), table[9:10, :].astype(jnp.int32)
    parts = jnp.concatenate(three_parts(weighted), axis=0)
    found = dot(parts, one_hot(owner, 128), ((1,), (0,)))
    found = found[0:8] + found[8:16] + found[16:24]
    at = lax.broadcasted_iota(jnp.int32, found.shape, 0)
    found = jnp.sum(jnp.where(at == sensor, found, 0.0), axis=0, keepdims=True)
    values[0:4, :] = table[4:8, :] * found


def source_kernel(got, meta, hot, weighted, lhs, own, low, high, values):
    count = got.shape[0] // 9
    sums = [jnp.sum(got[pl.ds(i, count, stride=9), :], axis=0, keepdims=True) for i in range(8)]
    readings = jnp.concatenate(sums, axis=0)
    weights = jnp.transpose(got[pl.ds(8, count, stride=9), :])[0:8]
    weighted[...] = readings * weights

    returned(weighted[...], meta, values)
    put_values(meta, values, lambda n: n >> 10, CX * CY, lhs)
    put_half(0, add_up(CX * CY, 0, CZ // 2, lhs, hot), own, low, high)


def put_half(half, sums, own, low, high):
    for x in range(CX):
        side, at = (low, x) if x < D else (high, x - (CX - D))
        for i in range(4):
            block = sums[x * CY : (x + 1) * CY, i * 128 : (i + 1) * 128]
            own[pl.ds(x * PLANE + half * 4 + i, CY, stride=8), :] = block
            side[pl.ds(at * CY * 4 + i, CY, stride=4), :] = block


def other_half_kernel(lhs, hot, own_in, own, low, high):
    del own_in
    put_half(1, add_up(CX * CY, CZ // 2, CZ // 2, lhs, hot), own, low, high)


def second_solve(src, q, cz, y1, y2, y3):
    def first(x, y, n):
        f, acc = fluxes(src, q, cz, x, y, n)
        y1[x, pl.ds(y, n)] = (A2 - A3) * f - A3 * acc

    def second(x, y, n):
        f, acc = fluxes(y1, q, cz, x, y, n)
        y2[x, pl.ds(y, n)] = A1 * src[x, pl.ds(y, n)] - f - acc

    def third(x, y, n):
        f, acc = fluxes(y2, q, cz, x, y, n)
        y3[x, pl.ds(y, n)] = A0 * src[x, pl.ds(y, n)] - f - acc

    return lines(1, 4, first), lines(2, 4, second), lines(3, 4, third)


def strips_kernel(
    weighted,
    py_low,
    py_high,
    c_low,
    c_high,
    own,
    q,
    cz,
    src,
    y1,
    y2,
    y3,
    lhs,
    near_hot,
    near,
    values,
):
    src[D : D + CX, D : D + CY] = own[...].reshape(CX, CY, 8, 128)
    flat = src.reshape(EX * EY * 8, 128)

    def columns(count):
        for k in range(4):
            node = near[k : k + 1, :].astype(jnp.int32)
            put_one_hot(node & (count - 1), count, near_hot, 0, slice(k * 1024, (k + 1) * 1024))

    for ref, y0, first_y in ((py_low, 0, CY - D), (py_high, D + CY, 0)):
        take_meta(ref, 3 * HALO_Y, near)
        returned(weighted[...], near, values)
        columns(256)

        def rows(node, first_y=first_y):
            x, y = node >> 15, ((node >> 10) & (CY - 1)) - first_y
            good = (y >= 0) & (y < D)
            return jnp.where(good, (((node >> 8) & 3) * CX + x) * D + y, -1)

        def keep(sums, y0=y0):
            for zq in range(4):
                for x in range(CX):
                    first = (zq * CX + x) * D
                    for half in range(2):
                        flat[
                            pl.ds(((x + D) * EY + y0) * 8 + zq * 2 + half, D, stride=8), :
                        ] = sums[first : first + D, half * 128 : (half + 1) * 128]

        put_values(near, values, rows, 4 * CX * D, lhs)
        keep(add_up(4 * CX * D, 0, 256, lhs, near_hot))

    for ref, x_low in ((c_low, True), (c_high, False)):
        for side, y_low in enumerate((True, False)):
            take_meta(ref, side * PART + 3 * HALO_C, near)
            returned(weighted[...], near, values)
            columns(128)

            def rows(node, x_low=x_low, y_low=y_low):
                x, y = node >> 15, (node >> 10) & (CY - 1)
                dx = CX - x if x_low else x + 1
                dy = CY - y if y_low else y + 1
                cell = jnp.where(dx == 1, dy - 1, jnp.where(dx == 2, dy + 2, 5))
                return jnp.where(dx + dy <= D, ((node >> 7) & 7) * len(CELLS) + cell, -1)

            def keep(sums, x_low=x_low, y_low=y_low):
                x0, y0 = 0 if x_low else D + CX, 0 if y_low else D + CY
                src[x0 : x0 + D, y0 : y0 + D] = jnp.zeros((D, D, 8, 128), F32)
                for i, (dx, dy) in enumerate(CELLS):
                    x = D - dx if x_low else D + CX + dx - 1
                    y = D - dy if y_low else D + CY + dy - 1
                    for c in range(8):
                        row = c * len(CELLS) + i
                        flat[(x * EY + y) * 8 + c : (x * EY + y) * 8 + c + 1, :] = sums[
                            row : row + 1, :
                        ]

            put_values(near, values, rows, 8 * len(CELLS), lhs)
            keep(add_up(8 * len(CELLS), 0, 128, lhs, near_hot))

    first, second, third = second_solve(src, q, cz, y1, y2, y3)
    early(1, first)
    early(2, second)
    early(3, third)


def adjoint_kernel(
    low_0, high_0, low_1, high_1, q, bg, cz, dz, src_in, y1_in, y2_in, y3_in, out_hbm, src, y1, y2, y3, out, sems
):
    del src_in, y1_in, y2_in, y3_in
    for half, x, ref in ((0, 0, low_0), (0, D + CX, high_0), (1, 0, low_1), (1, D + CX, high_1)):
        for i in range(D):
            v = ref[i * CY * 4 : (i + 1) * CY * 4, :].reshape(CY, 4, 128)
            src[x + i, D : D + CY, half * 4 : half * 4 + 4] = v
    first, second, third = second_solve(src, q, cz, y1, y2, y3)
    late(1, first)
    late(2, second)
    late(3, third)

    def last(x, y, n):
        ae, be = y3[x, pl.ds(y - 1, n + 2)], bg[x, pl.ds(y - 1, n + 2)]
        a, k = ae[1:-1], be[1:-1]
        sy = (ae[1:] - ae[:-1]) * (be[1:] - be[:-1])
        total = sy[1:] + sy[:-1]
        total += (y3[x + 1, pl.ds(y, n)] - a) * (bg[x + 1, pl.ds(y, n)] - k)
        total += (y3[x - 1, pl.ds(y, n)] - a) * (bg[x - 1, pl.ds(y, n)] - k)
        sz = (z_up(a) - a) * dz[x - D, pl.ds(y - D, n)]
        total = -0.5 * (total + (sz + z_down(sz)))
        yy = y - D
        for i in range(n):
            row = (x - D) * (CY // 8) + (yy + i) // 8
            out[pl.ds(row * 64 + (yy + i) % 8, 8, stride=8), :] = total[i]

    def leave(x):
        i = x - D
        at = pl.ds(pl.multiple_of(i * PLANE, PLANE), PLANE)
        return pltpu.make_async_copy(out.at[at], out_hbm.at[at], sems.at[i])

    compute = lines(4, 4, last)

    def plane(x):
        compute(x)
        leave(x).start()

    late(4, plane)
    for x in range(D, D + CX):
        leave(x).wait()


def by_tiles(block):
    lead = block.shape[:-2]
    rows, cols = block.shape[-2:]
    split = block.reshape(*lead, rows // 8, 8, cols // 128, 128)
    return jnp.swapaxes(split, -3, -2).reshape(-1, 128)


def from_tiles(rows):
    split = rows.reshape(CX, CY // 8, CZ // 128, 8, 128)
    return jnp.swapaxes(split, -3, -2).reshape(CX, CY, CZ)


def row_of(ref, x, y):
    return ref[pl.ds((x * (CY // 8) + y // 8) * 64 + y % 8, 8, stride=8), :]


def line_of(ref, x, y):
    return ref[pl.ds((x * (CY // 8) + y // 8) * 64 + y % 8, 8, stride=8), :]


def pack_kernel(
    permit_hbm,
    back_hbm,
    perturb_hbm,
    nodes_hbm,
    weights_hbm,
    owner_hbm,
    sensor_hbm,
    low_x,
    high_x,
    low_y,
    high_y,
    meta,
    permit,
    back,
    perturb,
    nodes,
    weights,
    owner,
    sensor,
    sems,
):
    pairs = (
        (nodes_hbm, nodes),
        (weights_hbm, weights),
        (owner_hbm, owner),
        (sensor_hbm, sensor),
        (permit_hbm, permit),
        (back_hbm, back),
        (perturb_hbm, perturb),
    )
    copies = [pltpu.make_async_copy(a, b, sems.at[i]) for i, (a, b) in enumerate(pairs)]
    for copy in copies:
        copy.start()
    for copy in copies[:4]:
        copy.wait()
    meta[0:4, :] = nodes[...].astype(F32)
    meta[4:8, :] = weights[...]
    meta[8:9, :] = owner[...].astype(F32)
    meta[9:10, :] = sensor[...].astype(F32)
    meta[10:16, :] = jnp.zeros((6, 1024), F32)
    for out, at in ((low_y, 3 * HALO_Y), (high_y, 3 * HALO_Y)):
        for c in range(8):
            lanes = slice(c * 128, (c + 1) * 128)
            out[at + c * 8 : at + c * 8 + 8, :] = meta[0:8, lanes]
            for i in range(2):
                out[at + 64 + i * 8 + c : at + 65 + i * 8 + c, :] = meta[8 + i : 9 + i, lanes]

    for field, ref in enumerate((permit, back, perturb)):
        copies[4 + field].wait()
        planes = D if field == 0 else D - 1

        def plane(x, carry, field=field, ref=ref, planes=planes):
            for y in range(CY):
                at = pl.ds(PX_AT[field] + (x * CY + y) * 8, 8)
                low_x[at, :] = row_of(ref, x, y)
                high_x[at, :] = row_of(ref, x + CX - planes, y)
            return carry

        lax.fori_loop(0, planes, plane, 0)
        for x in range(CX):
            for y in range(D):
                at = pl.ds(field * HALO_Y + (x * D + y) * 8, 8)
                low_y[at, :] = row_of(ref, x, y)
                high_y[at, :] = row_of(ref, x, y + CY - D)

    def flux(y, carry):
        for out, near, far in ((low_x, D - 2, D - 1), (high_x, CX - D + 1, CX - D)):
            face = 0.5 * (line_of(perturb, near, y) + line_of(perturb, far, y))
            at = pl.ds(pl.multiple_of(PX_FLUX + y * 8, 8), 8)
            out[at, :] = face * (line_of(back, far, y) - line_of(back, near, y))
        return carry

    lax.fori_loop(0, CY, flux, 0)


def own_kernel(
    permit_hbm,
    back_hbm,
    perturb_hbm,
    meta,
    q,
    bg,
    qp,
    cz,
    bz,
    dz,
    hot,
    permit,
    back,
    perturb,
    sems,
):
    pairs = ((permit_hbm, permit), (back_hbm, back), (perturb_hbm, perturb))
    copies = [pltpu.make_async_copy(a, b, sems.at[i]) for i, (a, b) in enumerate(pairs)]
    for copy in copies:
        copy.start()

    def entries(i, carry):
        k, lanes = i // 2, pl.ds(pl.multiple_of((i % 2) * 512, 512), 512)
        node = meta[pl.ds(k, 1), lanes].astype(jnp.int32)
        at = pl.ds(pl.multiple_of(i * 512, 512), 512)
        put_one_hot(node & (CZ - 1), CZ, hot, 0, at)
        return carry

    lax.fori_loop(0, 8, entries, 0)
    for copy in copies:
        copy.wait()

    def plane(x, carry):
        for y in range(CY):
            q[x + D, y + D] = row_of(permit, x, y) * (0.5 / HALF)
            bg[x + D, y + D] = row_of(back, x, y)
            qp[x + D, y + D] = row_of(perturb, x, y) * 0.5
        for y in range(0, CY, 4):
            at = pl.ds(y + D, 4)
            cz[x + D, at] = z_face(q[x + D, at])
            field = bg[x + D, at]
            step = jnp.where(z_end(4), 0.0, z_up(field) - field)
            dz[x, pl.ds(y, 4)] = step
            fz = step * z_face(qp[x + D, at])
            bz[x, pl.ds(y, 4)] = fz - z_down(fz)
        return carry

    lax.fori_loop(0, CX, plane, 0)


def corner_kernel(py_low, py_high, after, low, high):
    del after
    for side, ref in enumerate((py_low, py_high)):
        for field in range(3):
            for i, (dx, dy) in enumerate(CELLS):
                y = D - dy if side == 0 else dy - 1
                at = side * PART + field * HALO_C + i * 8
                for out, x in ((low, dx - 1), (high, CX - dx)):
                    first = field * HALO_Y + (x * D + y) * 8
                    out[at : at + 8, :] = ref[first : first + 8, :]
        at = side * PART + 3 * HALO_C
        low[at : at + META, :] = ref[3 * HALO_Y :, :]
        high[at : at + META, :] = ref[3 * HALO_Y :, :]


def vmem(count):
    return [pl.BlockSpec(memory_space=pltpu.VMEM)] * count


def shift(x, axis, by):
    count = lax.axis_size(axis)
    return lax.ppermute(x, axis, [(i, (i + by) % count) for i in range(count)])


def body(
    background_field,
    perturbation,
    permittivity,
    probe_nodes,
    probe_weights,
    probe_owner,
    probe_sensor,
    sensor_weight,
):
    devices = lax.axis_size("px") * lax.axis_size("py")
    fields = [by_tiles(f) for f in (permittivity, background_field, perturbation)]
    weights = jnp.pad(sensor_weight, (0, 128 - sensor_weight.shape[0]))[None, :]

    def rows(*counts):
        return [jax.ShapeDtypeStruct((n, 128), F32) for n in counts]

    def call(kernel, outs, *args, hbm=0, away=0, passed=0, at=1, scratch=(), limit, bytes_accessed=0):
        held = [pltpu.with_memory_space_constraint(a, pltpu.HBM) for a in args[:hbm]]
        args = held + list(args[hbm:])
        return pl.pallas_call(
            kernel,
            out_shape=tuple(outs),
            in_specs=[pl.BlockSpec(memory_space=pltpu.HBM)] * hbm + vmem(len(args) - hbm),
            out_specs=tuple(
                [pl.BlockSpec(memory_space=pl.ANY)] * away + vmem(len(outs) - away)
            ),
            scratch_shapes=scratch,
            input_output_aliases={len(args) - passed + i: at + i for i in range(passed)},
            compiler_params=pltpu.CompilerParams(vmem_limit_bytes=limit * 2**20),
            cost_estimate=pl.CostEstimate(
                flops=0, bytes_accessed=bytes_accessed, transcendentals=0
            ),
        )(*args)

    size_x, size_y, size_c = PX_ROWS, 3 * HALO_Y + META, 2 * PART
    raw = [pltpu.VMEM((ROWS, 128), F32)] * 3
    table = jax.ShapeDtypeStruct((16, 1024), F32)
    low_x, high_x, low_y, high_y, meta = call(
        pack_kernel,
        rows(size_x, size_x, size_y, size_y) + [table],
        *fields,
        probe_nodes,
        probe_weights,
        probe_owner.reshape(1, -1),
        probe_sensor.reshape(1, -1),
        hbm=7,
        scratch=raw
        + [
            pltpu.VMEM((4, 1024), jnp.int32),
            pltpu.VMEM((4, 1024), F32),
            pltpu.VMEM((1, 1024), jnp.int32),
            pltpu.VMEM((1, 1024), jnp.int32),
            pltpu.SemaphoreType.DMA((7,)),
        ],
        limit=6,
    )
    px_low, px_high = shift(high_x, "px", 1), shift(low_x, "px", -1)
    py_low, py_high = shift(high_y, "py", 1), shift(low_y, "py", -1)
    compact = jax.ShapeDtypeStruct((CX, CY, 8, 128), F32)
    full = jax.ShapeDtypeStruct((EX, EY, 8, 128), F32)
    q, bg, qp, cz, bz, dz, hot = call(
        own_kernel,
        [full] * 4 + [compact] * 2 + [jax.ShapeDtypeStruct((CZ, 4096), BF16)],
        *fields,
        meta,
        hbm=3,
        scratch=raw + [pltpu.SemaphoreType.DMA((3,))],
        limit=10,
        bytes_accessed=8 * 2**20,
    )
    low_c, high_c = call(corner_kernel, rows(size_c, size_c), py_low, py_high, bz, limit=4)
    c_low, c_high = shift(high_c, "px", 1), shift(low_c, "px", -1)
    q, bg, qp, cz, b, y1, y2 = call(
        middle_kernel,
        [full] * 7,
        py_low,
        py_high,
        low_c,
        bz,
        q,
        bg,
        qp,
        cz,
        passed=4,
        at=0,
        limit=6,
        bytes_accessed=8 * 2**20,
    )
    block = pltpu.VMEM((EX, EY, 8, 128), F32)
    readings, q, bg, qp, cz, b, y1, y2 = call(
        tangent_kernel,
        rows(devices * 9) + [full] * 7,
        px_low,
        px_high,
        c_low,
        c_high,
        bz,
        meta,
        hot,
        weights,
        q,
        bg,
        qp,
        cz,
        b,
        y1,
        y2,
        passed=7,
        scratch=[block, pltpu.VMEM((2 * CX * CY, CZ), BF16), pltpu.VMEM((8, 1024), F32)],
        limit=20,
    )
    got = lax.all_to_all(
        readings.reshape(devices, 1, 9 * 128),
        ("px", "py"),
        split_axis=0,
        concat_axis=0,
        tiled=True,
    ).reshape(devices * 9, 128)
    half = D * PLANE // 2
    weighted, lhs, own_source, low_s, high_s = call(
        source_kernel,
        rows(8) + [jax.ShapeDtypeStruct((2 * CX * CY, 4096), BF16)] + rows(ROWS, half, half),
        got,
        meta,
        hot,
        scratch=[pltpu.VMEM((8, 1024), F32)],
        limit=12,
    )
    low_0, high_0 = shift(high_s, "px", 1), shift(low_s, "px", -1)
    own_source, low_s, high_s = call(
        other_half_kernel,
        rows(ROWS, half, half),
        lhs,
        hot,
        own_source,
        passed=1,
        at=0,
        limit=12,
        bytes_accessed=8 * 2**20,
    )
    low_1, high_1 = shift(high_s, "px", 1), shift(low_s, "px", -1)
    src, y1, y2, y3 = call(
        strips_kernel,
        [full] * 4,
        weighted,
        py_low,
        py_high,
        c_low,
        c_high,
        own_source,
        q,
        cz,
        scratch=[
            pltpu.VMEM((2 * 4 * CX * D, 4096), BF16),
            pltpu.VMEM((256, 4096), BF16),
            pltpu.VMEM((16, 1024), F32),
            pltpu.VMEM((8, 1024), F32),
        ],
        limit=16,
        bytes_accessed=24 * 2**20,
    )
    result = call(
        adjoint_kernel,
        rows(ROWS) + [full] * 4,
        low_0,
        high_0,
        low_1,
        high_1,
        q,
        bg,
        cz,
        dz,
        src,
        y1,
        y2,
        y3,
        passed=4,
        away=1,
        scratch=[pltpu.VMEM((ROWS, 128), F32), pltpu.SemaphoreType.DMA((CX,))],
        limit=8,
    )[0]
    return from_tiles(result)


def solution(mesh):
    placed = (
        P("px", "py", None),
        P("px", "py", None),
        P("px", "py", None),
        P(None, ("px", "py")),
        P(None, ("px", "py")),
        P(("px", "py"), None),
        P(("px", "py")),
        P(("px", "py")),
    )
    return jax.shard_map(
        body, mesh=mesh, in_specs=placed, out_specs=P("px", "py", None), check_vma=False
    )
```

```python
import jax
import jax.numpy as jnp
import numpy as np
from jax import lax
from jax.experimental import pallas as pl
from jax.experimental.pallas import tpu as pltpu
from jax.sharding import PartitionSpec as P

SWEEPS = 4
MASS = 1.0
LOW = 1.0
HIGH = 25.0
CENTRE = 0.5 * (HIGH + LOW)
HALF = 0.5 * (HIGH - LOW)

CX, CY, CZ = 8, 32, 1024
D = 4
EX, EY = CX + 2 * D, CY + 2 * D
ROWS = CX * CY * 8
PLANE = CY * 8
PX_AT = (0, D * PLANE, (2 * D - 1) * PLANE)
PX_FLUX = (3 * D - 2) * PLANE
PX_ROWS = (3 * D - 1) * PLANE
HALO_Y = CX * D * 8
CELLS = tuple((dx, dy) for dx in range(1, D) for dy in range(1, D) if dx + dy <= D)
HALO_C = len(CELLS) * 8
META = 80
PART = 3 * HALO_C + META
F32 = jnp.float32
BF16 = jnp.bfloat16


def horner_terms():
    spread = CENTRE / HALF
    size = SWEEPS
    iterate = np.zeros(size)
    remain = np.eye(size)[0]
    search = remain / CENTRE
    ratio = 1.0 / spread
    for sweep in range(SWEEPS):
        iterate = iterate + search
        if sweep < SWEEPS - 1:
            shifted = np.concatenate([[0.0], search[:-1]])
            remain = remain - (CENTRE * search + HALF * shifted)
            following = 1.0 / (2.0 * spread - ratio)
            search = following * ratio * search + 2.0 * following / HALF * remain
            ratio = following
    return [float(v) for v in iterate]


A0, A1, A2, A3 = horner_terms()


def lane_of(n):
    return lax.broadcasted_iota(jnp.int32, (n, 8, 128), 2)


def z_up(f):
    r = pltpu.roll(f, 127, 2)
    return jnp.where(lane_of(f.shape[0]) == 127, pltpu.roll(r, 7, 1), r)


def z_down(f):
    r = pltpu.roll(f, 1, 2)
    return jnp.where(lane_of(f.shape[0]) == 0, pltpu.roll(r, 1, 1), r)


def z_end(n):
    return (lax.broadcasted_iota(jnp.int32, (n, 8, 128), 1) == 7) & (lane_of(n) == 127)


def z_face(q):
    return jnp.where(z_end(q.shape[0]), 0.0, q + z_up(q))


def side_fluxes(src, q, x, y, n):
    fe, qe = src[x, pl.ds(y - 1, n + 2)], q[x, pl.ds(y - 1, n + 2)]
    f, qc = fe[1:-1], qe[1:-1]
    fy = (fe[1:] - fe[:-1]) * (qe[1:] + qe[:-1])
    acc = fy[1:] - fy[:-1]
    acc += (src[x + 1, pl.ds(y, n)] - f) * (q[x + 1, pl.ds(y, n)] + qc)
    acc += (src[x - 1, pl.ds(y, n)] - f) * (q[x - 1, pl.ds(y, n)] + qc)
    return f, acc


def z_fluxes(f, faces):
    fz = (z_up(f) - f) * faces
    return fz - z_down(fz)


def fluxes(src, q, cz, x, y, n):
    f, acc = side_fluxes(src, q, x, y, n)
    return f, acc + z_fluxes(f, cz[x, pl.ds(y, n)])


def cover(low, high, n):
    starts = list(range(low, high - n + 1, n))
    if starts[-1] + n < high:
        starts.append(high - n)
    return starts


def early(margin, plane):
    def step(x, carry):
        plane(x)
        return carry

    lax.fori_loop(margin + D, EX - D - margin, step, 0)


def late(margin, plane):
    def step(i, carry):
        plane(jnp.where(i < D, margin + i, EX - 2 * D - margin + i))
        return carry

    lax.fori_loop(0, 2 * D, step, 0)


def lines(margin, n, step):
    def plane(x):
        for y in cover(margin, EY - margin, n):
            step(x, y, n)

    return plane


def put_py(field, py_low, py_high, out, scale):
    for ref, at in ((py_low, 0), (py_high, D + CY)):
        v = ref[field * HALO_Y : (field + 1) * HALO_Y, :]
        out[D : D + CX, at : at + D] = v.reshape(CX, D, 8, 128) * scale


def put_px(field, sides, out, scale):
    px_low, px_high, c_low, c_high = sides
    middle_y = slice(D, D + CY)
    planes = D if field == 0 else D - 1
    for ref, at in ((px_low, D - planes), (px_high, D + CX)):
        v = ref[PX_AT[field] : PX_AT[field] + planes * PLANE, :]
        out[at : at + planes, middle_y] = v.reshape(planes, CY, 8, 128) * scale
    blank = jnp.zeros((D, D, 8, 128), F32)
    for x, ref in ((0, c_low), (D + CX, c_high)):
        for side, y in enumerate((0, D + CY)):
            out[x : x + D, y : y + D] = blank
            for i, (dx, dy) in enumerate(CELLS):
                at = side * PART + field * HALO_C + i * 8
                cell_x = x + D - dx if x == 0 else x + dx - 1
                cell_y = y + D - dy if y == 0 else y + dy - 1
                out[cell_x, cell_y] = ref[at : at + 8, :] * scale


def far_planes(sides, bg, qp):
    middle_y = slice(D, D + CY)
    for ref, at, beside in ((sides[0], 0, 1), (sides[1], EX - 1, EX - 2)):
        flux = ref[PX_FLUX : PX_FLUX + PLANE, :].reshape(CY, 8, 128)
        bg[at, middle_y] = bg[beside, middle_y] + flux
        qp[at, middle_y] = 1.0 - qp[beside, middle_y]


def close_py(out, sign, planes):
    py, last_y = lax.axis_index("py"), lax.axis_size("py") - 1

    @pl.when(py == 0)
    def _():
        out[planes, D - 1] = out[planes, D] * sign

    @pl.when(py == last_y)
    def _():
        out[planes, D + CY] = out[planes, D + CY - 1] * sign


def first_solve(q, bg, qp, cz, bz, b, y1, y2):
    def whole(x, y, n):
        f, acc = side_fluxes(bg, qp, x, y, n)
        b[x, pl.ds(y, n)] = acc + z_fluxes(f, z_face(qp[x, pl.ds(y, n)]))
        cz[x, pl.ds(y, n)] = z_face(q[x, pl.ds(y, n)])

    def right_own(x):
        whole(x, 1, D - 1)
        whole(x, D + CY, D - 1)
        for y in cover(D, D + CY, 4):
            _, acc = side_fluxes(bg, qp, x, y, 4)
            b[x, pl.ds(y, 4)] = acc + bz[x - D, pl.ds(y - D, 4)]

    def second(x, y, n):
        f, acc = fluxes(b, q, cz, x, y, n)
        y1[x, pl.ds(y, n)] = (A2 - A3) * f - A3 * acc

    def third(x, y, n):
        f, acc = fluxes(y1, q, cz, x, y, n)
        y2[x, pl.ds(y, n)] = A1 * b[x, pl.ds(y, n)] - f - acc

    return lines(1, 2, whole), right_own, lines(2, 4, second), lines(3, 2, third)


def middle_kernel(
    py_low, py_high, after, bz, q_in, bg_in, qp_in, cz_in, q, bg, qp, cz, b, y1, y2
):
    del after, q_in, bg_in, qp_in, cz_in
    own = slice(D, D + CX)
    for field, out, scale, sign in ((0, q, 0.5 / HALF, -1.0), (1, bg, 1.0, 1.0), (2, qp, 0.5, -1.0)):
        put_py(field, py_low, py_high, out, scale)
        close_py(out, sign, own)
    _, right_own, second, third = first_solve(q, bg, qp, cz, bz, b, y1, y2)
    early(1, right_own)
    early(2, second)
    early(3, third)


def close_edges(out, sign):
    px, last_x = lax.axis_index("px"), lax.axis_size("px") - 1

    @pl.when(px == 0)
    def _():
        out[D - 1] = out[D] * sign

    @pl.when(px == last_x)
    def _():
        out[D + CX] = out[D + CX - 1] * sign

    close_py(out, sign, slice(0, EX))


def take_meta(ref, base, out):
    for c in range(8):
        lanes = slice(c * 128, (c + 1) * 128)
        out[0:8, lanes] = ref[base + c * 8 : base + c * 8 + 8, :]
        for i in range(2):
            at = base + 64 + i * 8 + c
            out[8 + i : 9 + i, lanes] = ref[at : at + 1, :]


def two_parts(v):
    high = v.astype(BF16)
    return high, (v - high.astype(F32)).astype(BF16)


def three_parts(v):
    high = v.astype(BF16)
    rest = v - high.astype(F32)
    mid = rest.astype(BF16)
    return high, mid, (rest - mid.astype(F32)).astype(BF16)


def one_hot(index, count):
    at = lax.broadcasted_iota(jnp.int32, (count, index.shape[1]), 0)
    return jnp.where(at == index, 1.0, 0.0).astype(BF16)


def rows16(index):
    shape = (16, index.shape[1])
    numbers = lax.broadcasted_iota(jnp.int32, shape, 0).astype(jnp.int16)
    return jnp.broadcast_to(index, shape).astype(jnp.int16), numbers


def put_one_hot(index, count, out, first, lanes):
    wanted, numbers = rows16(index)
    one, zero = jnp.ones(wanted.shape, BF16), jnp.zeros(wanted.shape, BF16)
    for r in range(count // 16):
        hit = numbers + jnp.int16(r * 16) == wanted
        out[first + r * 16 : first + (r + 1) * 16, lanes] = jnp.where(hit, one, zero)


def dot(a, b, over):
    return lax.dot_general(a, b, (over, ((), ())), preferred_element_type=F32)


def tangent_kernel(
    px_low,
    px_high,
    c_low,
    c_high,
    bz,
    meta,
    hot,
    weights,
    q_in,
    bg_in,
    qp_in,
    cz_in,
    b_in,
    y1_in,
    y2_in,
    out,
    q,
    bg,
    qp,
    cz,
    b,
    y1,
    y2,
    y3,
    table,
    vals,
):
    del q_in, bg_in, qp_in, cz_in, b_in, y1_in, y2_in
    sides = (px_low, px_high, c_low, c_high)
    put_px(0, sides, q, 0.5 / HALF)
    put_px(1, sides, bg, 1.0)
    put_px(2, sides, qp, 0.5)
    far_planes(sides, bg, qp)
    close_edges(q, -1.0)
    close_edges(qp, -1.0)
    close_edges(bg, 1.0)
    right, right_own, second, third = first_solve(q, bg, qp, cz, bz, b, y1, y2)

    def outer_planes(i, carry):
        right(jnp.where(i < D - 1, 1 + i, CX + 1 + i))
        return carry

    def edge_planes(i, carry):
        right_own(D + i * (CX - 1))
        return carry

    lax.fori_loop(0, 2 * (D - 1), outer_planes, 0)
    lax.fori_loop(0, 2, edge_planes, 0)
    late(2, second)
    late(3, third)

    def fourth(x, y, n):
        f, acc = fluxes(y2, q, cz, x, y, n)
        y3[x, pl.ds(y, n)] = A0 * b[x, pl.ds(y, n)] - f - acc

    late(4, lines(4, 4, fourth))

    flat = y3.reshape(EX * EY * 8, 128)
    for x in range(CX):
        for c in range(8):
            v = flat[pl.ds(((x + D) * EY + D) * 8 + c, CY, stride=8), :]
            high, low = two_parts(v)
            table[x * CY : (x + 1) * CY, c * 128 : (c + 1) * 128] = high
            table[CX * CY + x * CY : CX * CY + (x + 1) * CY, c * 128 : (c + 1) * 128] = low

    vals[...] = jnp.zeros_like(vals)

    def gather(k, carry):
        node = meta[pl.ds(k, 1), :].astype(jnp.int32)
        lanes = pl.ds(pl.multiple_of(k * 1024, 1024), 1024)
        found = dot(table[...], hot[:, lanes], ((1,), (0,)))
        found = found[: CX * CY] + found[CX * CY :]
        at = lax.broadcasted_iota(jnp.int32, found.shape, 0)
        found = jnp.sum(jnp.where(at == node >> 10, found, 0.0), axis=0, keepdims=True)
        vals[0:1, :] += meta[pl.ds(k + 4, 1), :] * found
        return carry

    lax.fori_loop(0, 4, gather, 0)

    owner, sensor = meta[8:9, :].astype(jnp.int32), meta[9:10, :].astype(jnp.int32)
    at = lax.broadcasted_iota(jnp.int32, (8, 1024), 0)
    owned = jnp.where(at == sensor, vals[0:1, :], 0.0)
    parts = jnp.concatenate(three_parts(owned), axis=0)
    sums = dot(parts, one_hot(owner, 128), ((1,), (1,)))
    readings = sums[0:8] + sums[8:16] + sums[16:24]
    block = jnp.concatenate([readings, weights[...]] * 8, axis=0)
    for i in range(out.shape[0] // 72):
        out[i * 72 : (i + 1) * 72, :] = block


def scatter(meta, values, rows, per, tiles, width, lhs, keep, hot):
    for k in range(4):
        wanted, numbers = rows16(rows(meta[k : k + 1, :].astype(jnp.int32)))
        value = jnp.broadcast_to(values[k : k + 1, :], wanted.shape)
        high, low = two_parts(value)
        zero = jnp.zeros(wanted.shape, BF16)
        lanes = slice(k * 1024, (k + 1) * 1024)
        for r in range(per // 16):
            hit = numbers + jnp.int16(r * 16) == wanted
            lhs[r * 16 : (r + 1) * 16, lanes] = jnp.where(hit, high, zero)
            lhs[per + r * 16 : per + (r + 1) * 16, lanes] = jnp.where(hit, low, zero)

    def tile(t, carry):
        total = None
        for k in range(4):
            lanes = slice(k * 1024, (k + 1) * 1024)
            hits = hot[pl.ds(pl.multiple_of(t * width, width), width), lanes]
            part = dot(lhs[0 : 2 * per, lanes], hits, ((1,), (1,)))
            total = part if total is None else total + part
        keep(t, total[0:per] + total[per : 2 * per])
        return carry

    if tiles == 1:
        tile(0, 0)
    else:
        lax.fori_loop(0, tiles, tile, 0)


def returned(weighted, table, values):
    owner, sensor = table[8:9, :].astype(jnp.int32), table[9:10, :].astype(jnp.int32)
    parts = jnp.concatenate(three_parts(weighted), axis=0)
    found = dot(parts, one_hot(owner, 128), ((1,), (0,)))
    found = found[0:8] + found[8:16] + found[16:24]
    at = lax.broadcasted_iota(jnp.int32, found.shape, 0)
    found = jnp.sum(jnp.where(at == sensor, found, 0.0), axis=0, keepdims=True)
    values[0:4, :] = table[4:8, :] * found


def source_kernel(got, meta, hot, weighted, own, low, high, lhs, values):
    count = got.shape[0] // 9
    sums = [jnp.sum(got[pl.ds(i, count, stride=9), :], axis=0, keepdims=True) for i in range(8)]
    readings = jnp.concatenate(sums, axis=0)
    weights = jnp.transpose(got[pl.ds(8, count, stride=9), :])[0:8]
    weighted[...] = readings * weights

    def keep(t, sums):
        for x in range(CX):
            for i in range(4):
                block = sums[x * CY : (x + 1) * CY, i * 128 : (i + 1) * 128]
                own[pl.ds(x * PLANE + t * 4 + i, CY, stride=8), :] = block
                side, at = (low, x) if x < D else (high, x - (CX - D))
                side[pl.ds(at * PLANE + t * 4 + i, CY, stride=8), :] = block

    returned(weighted[...], meta, values)
    scatter(meta, values, lambda n: n >> 10, CX * CY, 2, 512, lhs, keep, hot)


def second_solve(src, q, cz, y1, y2, y3):
    def first(x, y, n):
        f, acc = fluxes(src, q, cz, x, y, n)
        y1[x, pl.ds(y, n)] = (A2 - A3) * f - A3 * acc

    def second(x, y, n):
        f, acc = fluxes(y1, q, cz, x, y, n)
        y2[x, pl.ds(y, n)] = A1 * src[x, pl.ds(y, n)] - f - acc

    def third(x, y, n):
        f, acc = fluxes(y2, q, cz, x, y, n)
        y3[x, pl.ds(y, n)] = A0 * src[x, pl.ds(y, n)] - f - acc

    return lines(1, 2, first), lines(2, 4, second), lines(3, 2, third)


def strips_kernel(
    weighted,
    py_low,
    py_high,
    c_low,
    c_high,
    own,
    q,
    cz,
    src,
    y1,
    y2,
    y3,
    lhs,
    near_hot,
    near,
    values,
):
    src[D : D + CX, D : D + CY] = own[...].reshape(CX, CY, 8, 128)
    flat = src.reshape(EX * EY * 8, 128)

    def columns(count):
        for k in range(4):
            node = near[k : k + 1, :].astype(jnp.int32)
            put_one_hot(node & (count - 1), count, near_hot, 0, slice(k * 1024, (k + 1) * 1024))

    for ref, y0, first_y in ((py_low, 0, CY - D), (py_high, D + CY, 0)):
        take_meta(ref, 3 * HALO_Y, near)
        returned(weighted[...], near, values)
        columns(256)

        def rows(node, first_y=first_y):
            x, y = node >> 15, ((node >> 10) & (CY - 1)) - first_y
            good = (y >= 0) & (y < D)
            return jnp.where(good, (((node >> 8) & 3) * CX + x) * D + y, -1)

        def keep(t, sums, y0=y0):
            for zq in range(4):
                for x in range(CX):
                    first = (zq * CX + x) * D
                    for half in range(2):
                        flat[
                            pl.ds(((x + D) * EY + y0) * 8 + zq * 2 + half, D, stride=8), :
                        ] = sums[first : first + D, half * 128 : (half + 1) * 128]

        scatter(near, values, rows, 4 * CX * D, 1, 256, lhs, keep, near_hot)

    for ref, x_low in ((c_low, True), (c_high, False)):
        for side, y_low in enumerate((True, False)):
            take_meta(ref, side * PART + 3 * HALO_C, near)
            returned(weighted[...], near, values)
            columns(128)

            def rows(node, x_low=x_low, y_low=y_low):
                x, y = node >> 15, (node >> 10) & (CY - 1)
                dx = CX - x if x_low else x + 1
                dy = CY - y if y_low else y + 1
                cell = jnp.where(dx == 1, dy - 1, jnp.where(dx == 2, dy + 2, 5))
                return jnp.where(dx + dy <= D, ((node >> 7) & 7) * len(CELLS) + cell, -1)

            def keep(t, sums, x_low=x_low, y_low=y_low):
                x0, y0 = 0 if x_low else D + CX, 0 if y_low else D + CY
                src[x0 : x0 + D, y0 : y0 + D] = jnp.zeros((D, D, 8, 128), F32)
                for i, (dx, dy) in enumerate(CELLS):
                    x = D - dx if x_low else D + CX + dx - 1
                    y = D - dy if y_low else D + CY + dy - 1
                    for c in range(8):
                        row = c * len(CELLS) + i
                        flat[(x * EY + y) * 8 + c : (x * EY + y) * 8 + c + 1, :] = sums[
                            row : row + 1, :
                        ]

            scatter(near, values, rows, 8 * len(CELLS), 1, 128, lhs, keep, near_hot)

    first, second, third = second_solve(src, q, cz, y1, y2, y3)
    early(1, first)
    early(2, second)
    early(3, third)


def adjoint_kernel(
    px_low, px_high, q, bg, cz, dz, src_in, y1_in, y2_in, y3_in, out_hbm, src, y1, y2, y3, out, sems
):
    del src_in, y1_in, y2_in, y3_in
    for x, ref in ((0, px_low), (D + CX, px_high)):
        src[x : x + D, D : D + CY] = ref[...].reshape(D, CY, 8, 128)
    first, second, third = second_solve(src, q, cz, y1, y2, y3)
    late(1, first)
    late(2, second)
    late(3, third)

    def last(x, y, n):
        ae, be = y3[x, pl.ds(y - 1, n + 2)], bg[x, pl.ds(y - 1, n + 2)]
        a, k = ae[1:-1], be[1:-1]
        sy = (ae[1:] - ae[:-1]) * (be[1:] - be[:-1])
        total = sy[1:] + sy[:-1]
        total += (y3[x + 1, pl.ds(y, n)] - a) * (bg[x + 1, pl.ds(y, n)] - k)
        total += (y3[x - 1, pl.ds(y, n)] - a) * (bg[x - 1, pl.ds(y, n)] - k)
        sz = (z_up(a) - a) * dz[x - D, pl.ds(y - D, n)]
        total = -0.5 * (total + (sz + z_down(sz)))
        yy = y - D
        for i in range(n):
            row = (x - D) * (CY // 8) + (yy + i) // 8
            out[pl.ds(row * 64 + (yy + i) % 8, 8, stride=8), :] = total[i]

    def leave(x):
        i = x - D
        at = pl.ds(pl.multiple_of(i * PLANE, PLANE), PLANE)
        return pltpu.make_async_copy(out.at[at], out_hbm.at[at], sems.at[i])

    compute = lines(4, 4, last)

    def plane(x):
        compute(x)
        leave(x).start()

    late(4, plane)
    for x in range(D, D + CX):
        leave(x).wait()


def by_tiles(block):
    lead = block.shape[:-2]
    rows, cols = block.shape[-2:]
    split = block.reshape(*lead, rows // 8, 8, cols // 128, 128)
    return jnp.swapaxes(split, -3, -2).reshape(-1, 128)


def from_tiles(rows):
    split = rows.reshape(CX, CY // 8, CZ // 128, 8, 128)
    return jnp.swapaxes(split, -3, -2).reshape(CX, CY, CZ)


def row_of(ref, x, y):
    return ref[pl.ds((x * (CY // 8) + y // 8) * 64 + y % 8, 8, stride=8), :]


def line_of(ref, x, y):
    return ref[pl.ds((x * (CY // 8) + y // 8) * 64 + y % 8, 8, stride=8), :]


def pack_kernel(
    permit_hbm,
    back_hbm,
    perturb_hbm,
    nodes_hbm,
    weights_hbm,
    owner_hbm,
    sensor_hbm,
    low_x,
    high_x,
    low_y,
    high_y,
    meta,
    permit,
    back,
    perturb,
    nodes,
    weights,
    owner,
    sensor,
    sems,
):
    pairs = (
        (nodes_hbm, nodes),
        (weights_hbm, weights),
        (owner_hbm, owner),
        (sensor_hbm, sensor),
        (permit_hbm, permit),
        (back_hbm, back),
        (perturb_hbm, perturb),
    )
    copies = [pltpu.make_async_copy(a, b, sems.at[i]) for i, (a, b) in enumerate(pairs)]
    for copy in copies:
        copy.start()
    for copy in copies[:4]:
        copy.wait()
    meta[0:4, :] = nodes[...].astype(F32)
    meta[4:8, :] = weights[...]
    meta[8:9, :] = owner[...].astype(F32)
    meta[9:10, :] = sensor[...].astype(F32)
    meta[10:16, :] = jnp.zeros((6, 1024), F32)
    for out, at in ((low_y, 3 * HALO_Y), (high_y, 3 * HALO_Y)):
        for c in range(8):
            lanes = slice(c * 128, (c + 1) * 128)
            out[at + c * 8 : at + c * 8 + 8, :] = meta[0:8, lanes]
            for i in range(2):
                out[at + 64 + i * 8 + c : at + 65 + i * 8 + c, :] = meta[8 + i : 9 + i, lanes]

    for field, ref in enumerate((permit, back, perturb)):
        copies[4 + field].wait()
        planes = D if field == 0 else D - 1

        def plane(x, carry, field=field, ref=ref, planes=planes):
            for y in range(CY):
                at = pl.ds(PX_AT[field] + (x * CY + y) * 8, 8)
                low_x[at, :] = row_of(ref, x, y)
                high_x[at, :] = row_of(ref, x + CX - planes, y)
            return carry

        lax.fori_loop(0, planes, plane, 0)
        for x in range(CX):
            for y in range(D):
                at = pl.ds(field * HALO_Y + (x * D + y) * 8, 8)
                low_y[at, :] = row_of(ref, x, y)
                high_y[at, :] = row_of(ref, x, y + CY - D)

    def flux(y, carry):
        for out, near, far in ((low_x, D - 2, D - 1), (high_x, CX - D + 1, CX - D)):
            face = 0.5 * (line_of(perturb, near, y) + line_of(perturb, far, y))
            at = pl.ds(pl.multiple_of(PX_FLUX + y * 8, 8), 8)
            out[at, :] = face * (line_of(back, far, y) - line_of(back, near, y))
        return carry

    lax.fori_loop(0, CY, flux, 0)


def own_kernel(
    permit_hbm,
    back_hbm,
    perturb_hbm,
    meta,
    q,
    bg,
    qp,
    cz,
    bz,
    dz,
    hot,
    permit,
    back,
    perturb,
    sems,
):
    pairs = ((permit_hbm, permit), (back_hbm, back), (perturb_hbm, perturb))
    copies = [pltpu.make_async_copy(a, b, sems.at[i]) for i, (a, b) in enumerate(pairs)]
    for copy in copies:
        copy.start()

    def entries(i, carry):
        k, lanes = i // 2, pl.ds(pl.multiple_of((i % 2) * 512, 512), 512)
        node = meta[pl.ds(k, 1), lanes].astype(jnp.int32)
        at = pl.ds(pl.multiple_of(i * 512, 512), 512)
        put_one_hot(node & (CZ - 1), CZ, hot, 0, at)
        return carry

    lax.fori_loop(0, 8, entries, 0)
    for copy in copies:
        copy.wait()

    def plane(x, carry):
        for y in range(CY):
            q[x + D, y + D] = row_of(permit, x, y) * (0.5 / HALF)
            bg[x + D, y + D] = row_of(back, x, y)
            qp[x + D, y + D] = row_of(perturb, x, y) * 0.5
        for y in range(0, CY, 4):
            at = pl.ds(y + D, 4)
            cz[x + D, at] = z_face(q[x + D, at])
            field = bg[x + D, at]
            step = jnp.where(z_end(4), 0.0, z_up(field) - field)
            dz[x, pl.ds(y, 4)] = step
            fz = step * z_face(qp[x + D, at])
            bz[x, pl.ds(y, 4)] = fz - z_down(fz)
        return carry

    lax.fori_loop(0, CX, plane, 0)


def corner_kernel(py_low, py_high, after, low, high):
    del after
    for side, ref in enumerate((py_low, py_high)):
        for field in range(3):
            for i, (dx, dy) in enumerate(CELLS):
                y = D - dy if side == 0 else dy - 1
                at = side * PART + field * HALO_C + i * 8
                for out, x in ((low, dx - 1), (high, CX - dx)):
                    first = field * HALO_Y + (x * D + y) * 8
                    out[at : at + 8, :] = ref[first : first + 8, :]
        at = side * PART + 3 * HALO_C
        low[at : at + META, :] = ref[3 * HALO_Y :, :]
        high[at : at + META, :] = ref[3 * HALO_Y :, :]


def vmem(count):
    return [pl.BlockSpec(memory_space=pltpu.VMEM)] * count


def shift(x, axis, by):
    count = lax.axis_size(axis)
    return lax.ppermute(x, axis, [(i, (i + by) % count) for i in range(count)])


def body(
    background_field,
    perturbation,
    permittivity,
    probe_nodes,
    probe_weights,
    probe_owner,
    probe_sensor,
    sensor_weight,
):
    devices = lax.axis_size("px") * lax.axis_size("py")
    fields = [by_tiles(f) for f in (permittivity, background_field, perturbation)]
    weights = jnp.pad(sensor_weight, (0, 128 - sensor_weight.shape[0]))[None, :]

    def rows(*counts):
        return [jax.ShapeDtypeStruct((n, 128), F32) for n in counts]

    def call(kernel, outs, *args, hbm=0, away=0, passed=0, at=1, scratch=(), limit, bytes_accessed=0):
        held = [pltpu.with_memory_space_constraint(a, pltpu.HBM) for a in args[:hbm]]
        args = held + list(args[hbm:])
        return pl.pallas_call(
            kernel,
            out_shape=tuple(outs),
            in_specs=[pl.BlockSpec(memory_space=pltpu.HBM)] * hbm + vmem(len(args) - hbm),
            out_specs=tuple(
                [pl.BlockSpec(memory_space=pl.ANY)] * away + vmem(len(outs) - away)
            ),
            scratch_shapes=scratch,
            input_output_aliases={len(args) - passed + i: at + i for i in range(passed)},
            compiler_params=pltpu.CompilerParams(vmem_limit_bytes=limit * 2**20),
            cost_estimate=pl.CostEstimate(
                flops=0, bytes_accessed=bytes_accessed, transcendentals=0
            ),
        )(*args)

    size_x, size_y, size_c = PX_ROWS, 3 * HALO_Y + META, 2 * PART
    raw = [pltpu.VMEM((ROWS, 128), F32)] * 3
    table = jax.ShapeDtypeStruct((16, 1024), F32)
    low_x, high_x, low_y, high_y, meta = call(
        pack_kernel,
        rows(size_x, size_x, size_y, size_y) + [table],
        *fields,
        probe_nodes,
        probe_weights,
        probe_owner.reshape(1, -1),
        probe_sensor.reshape(1, -1),
        hbm=7,
        scratch=raw
        + [
            pltpu.VMEM((4, 1024), jnp.int32),
            pltpu.VMEM((4, 1024), F32),
            pltpu.VMEM((1, 1024), jnp.int32),
            pltpu.VMEM((1, 1024), jnp.int32),
            pltpu.SemaphoreType.DMA((7,)),
        ],
        limit=6,
    )
    px_low, px_high = shift(high_x, "px", 1), shift(low_x, "px", -1)
    py_low, py_high = shift(high_y, "py", 1), shift(low_y, "py", -1)
    compact = jax.ShapeDtypeStruct((CX, CY, 8, 128), F32)
    full = jax.ShapeDtypeStruct((EX, EY, 8, 128), F32)
    q, bg, qp, cz, bz, dz, hot = call(
        own_kernel,
        [full] * 4 + [compact] * 2 + [jax.ShapeDtypeStruct((CZ, 4096), BF16)],
        *fields,
        meta,
        hbm=3,
        scratch=raw + [pltpu.SemaphoreType.DMA((3,))],
        limit=10,
        bytes_accessed=8 * 2**20,
    )
    low_c, high_c = call(corner_kernel, rows(size_c, size_c), py_low, py_high, bz, limit=4)
    c_low, c_high = shift(high_c, "px", 1), shift(low_c, "px", -1)
    q, bg, qp, cz, b, y1, y2 = call(
        middle_kernel,
        [full] * 7,
        py_low,
        py_high,
        low_c,
        bz,
        q,
        bg,
        qp,
        cz,
        passed=4,
        at=0,
        limit=6,
        bytes_accessed=8 * 2**20,
    )
    block = pltpu.VMEM((EX, EY, 8, 128), F32)
    readings, q, bg, qp, cz, b, y1, y2 = call(
        tangent_kernel,
        rows(devices * 9) + [full] * 7,
        px_low,
        px_high,
        c_low,
        c_high,
        bz,
        meta,
        hot,
        weights,
        q,
        bg,
        qp,
        cz,
        b,
        y1,
        y2,
        passed=7,
        scratch=[block, pltpu.VMEM((2 * CX * CY, CZ), BF16), pltpu.VMEM((8, 1024), F32)],
        limit=20,
    )
    got = lax.all_to_all(
        readings.reshape(devices, 1, 9 * 128),
        ("px", "py"),
        split_axis=0,
        concat_axis=0,
        tiled=True,
    ).reshape(devices * 9, 128)
    weighted, own_source, low_s, high_s = call(
        source_kernel,
        rows(8, ROWS, D * PLANE, D * PLANE),
        got,
        meta,
        hot,
        scratch=[pltpu.VMEM((2 * CX * CY, 4096), BF16), pltpu.VMEM((8, 1024), F32)],
        limit=18,
    )
    source_low, source_high = shift(high_s, "px", 1), shift(low_s, "px", -1)
    src, y1, y2, y3 = call(
        strips_kernel,
        [full] * 4,
        weighted,
        py_low,
        py_high,
        c_low,
        c_high,
        own_source,
        q,
        cz,
        scratch=[
            pltpu.VMEM((2 * 4 * CX * D, 4096), BF16),
            pltpu.VMEM((256, 4096), BF16),
            pltpu.VMEM((16, 1024), F32),
            pltpu.VMEM((8, 1024), F32),
        ],
        limit=16,
        bytes_accessed=24 * 2**20,
    )
    result = call(
        adjoint_kernel,
        rows(ROWS) + [full] * 4,
        source_low,
        source_high,
        q,
        bg,
        cz,
        dz,
        src,
        y1,
        y2,
        y3,
        passed=4,
        away=1,
        scratch=[pltpu.VMEM((ROWS, 128), F32), pltpu.SemaphoreType.DMA((CX,))],
        limit=8,
    )[0]
    return from_tiles(result)


def solution(mesh):
    placed = (
        P("px", "py", None),
        P("px", "py", None),
        P("px", "py", None),
        P(None, ("px", "py")),
        P(None, ("px", "py")),
        P(("px", "py"), None),
        P(("px", "py")),
        P(("px", "py")),
    )
    return jax.shard_map(
        body, mesh=mesh, in_specs=placed, out_specs=P("px", "py", None), check_vma=False
    )
```
